512 devices in a mesh: wide: 32 (over x, y), narrow: 16 (over z, core).
Axes of the slice: x: 4, y: 8, z: 8, core: 2. Of those that a mesh axis runs over, the one named last changes fastest.
Arguments:
- student_feats: bfloat16 [1024, 512], P(('wide', 'narrow')), may hold values from -8 to 8
- teacher_feats: bfloat16 [1024, 512], P(('wide', 'narrow')), may hold values from -8 to 8
- prototypes: bfloat16 [262144, 512], P(('wide', 'narrow')), may hold values from -8 to 8
Outputs:
- student_grad: float32 [1024, 512], P(('wide', 'narrow'))
- proto_grad: float32 [262144, 512], P(('wide', 'narrow'))
The draws below stay inside these ranges and needn't reach their ends.
All inputs are finite; a program needn't handle non-finite values.
Results may differ from the reference program's by a relative error of at most 0.0006.
The reference program's roundings to bfloat16 on the way (of `student_hat`, `teacher_hat`, `proto_hat` and `grad_logits`) count: a program that leaves them out, or rounds other values in their place, can miss the bound.
Values may be sent and summed in bfloat16 or wider, within the bound.
A program may use at most 64 MiB of HBM per device.

```python
import math
import jax
import jax.numpy as jnp
from jax import lax

D = 512
PROTOS = 262144
ROWS = 1024
SINK_ITERS = 3


cluster_count = 16


def cluster_centers(key):
    return jax.random.normal(jax.random.fold_in(key, 7), (cluster_count, D), jnp.float32) / jnp.sqrt(jnp.float32(D))


def proto_rows(key, ident):
    centers = cluster_centers(key)
    proto_key = jax.random.fold_in(key, 3)

    def single(index):
        own_key = jax.random.fold_in(proto_key, index)
        first = jax.random.randint(jax.random.fold_in(own_key, 1), (), 0, cluster_count)
        second = jax.random.randint(jax.random.fold_in(own_key, 2), (), 0, cluster_count)
        member = jnp.minimum(first, second)
        weight = jax.random.uniform(jax.random.fold_in(own_key, 4), (), jnp.float32, 0.3, 1.0)
        noise = jax.random.normal(jax.random.fold_in(own_key, 5), (D,), jnp.float32) / jnp.sqrt(jnp.float32(D))
        return weight * centers[member] + 0.8 * noise
    return jax.vmap(single)(ident)


def features(key, salt_value):
    centers = cluster_centers(key)
    chosen_ids = jax.random.randint(jax.random.fold_in(key, 11), (ROWS,), 0, PROTOS)
    first = jax.random.randint(jax.random.fold_in(key, 12), (ROWS,), 0, cluster_count)
    second = jax.random.randint(jax.random.fold_in(key, 13), (ROWS,), 0, cluster_count)
    row_cluster = jnp.maximum(first, second)
    chosen = proto_rows(key, chosen_ids)
    center_part = centers[row_cluster]
    along = jax.random.uniform(jax.random.fold_in(key, salt_value), (ROWS, 1), jnp.float32, 0.3, 1.5)
    toward = jax.random.uniform(jax.random.fold_in(key, salt_value + 3), (ROWS, 1), jnp.float32, 0.0, 1.0)
    spread = jnp.exp(jax.random.uniform(jax.random.fold_in(key, salt_value + 4), (ROWS, 1), jnp.float32, math.log(0.1), 0.0))
    jitter = jax.random.normal(jax.random.fold_in(key, salt_value + 1), (ROWS, D), jnp.float32) / jnp.sqrt(jnp.float32(D))
    mixed = along * center_part + toward * chosen + spread * jitter
    return jnp.clip(mixed, -8.0, 8.0).astype(jnp.bfloat16)


def draw_student_feats(key, part):
    return features(key, 21)


def draw_teacher_feats(key, part):
    return features(key, 31)


def draw_prototypes(key, part):
    protos = proto_rows(key, jnp.arange(PROTOS, dtype=jnp.int32))
    return jnp.clip(protos, -8.0, 8.0).astype(jnp.bfloat16)


def setup_inputs(seed: int = 0) -> dict:
    splits = jax.random.split(jax.random.key(seed), 4)
    student_feats = draw_student_feats(jax.random.fold_in(splits[3], 71), 0)
    teacher_feats = draw_teacher_feats(jax.random.fold_in(splits[3], 71), 0)
    prototypes = draw_prototypes(jax.random.fold_in(splits[3], 71), 0)
    return dict(student_feats=student_feats, teacher_feats=teacher_feats, prototypes=prototypes)


epsilon = 1e-06
teacher_temp = 0.07
student_temp = 0.1
loss_scale = 1.0

def unit_rows(values):
    widened = values.astype(jnp.float32)
    inverse = lax.rsqrt(lax.optimization_barrier(jnp.sum(widened * widened, axis=1, keepdims=True)) + epsilon)
    return (widened * inverse, inverse)

def reference(student_feats, teacher_feats, prototypes):
    student_unit, student_inv = unit_rows(student_feats)
    teacher_unit = unit_rows(teacher_feats)[0]
    proto_unit, proto_inv = unit_rows(prototypes)
    student_hat = student_unit.astype(jnp.bfloat16)
    teacher_hat = teacher_unit.astype(jnp.bfloat16)
    proto_hat = proto_unit.astype(jnp.bfloat16)
    logits = jnp.dot(student_hat, proto_hat.T, preferred_element_type=jnp.float32)
    teacher_logits = jnp.dot(teacher_hat, proto_hat.T, preferred_element_type=jnp.float32)
    exp_teacher = jnp.exp(teacher_logits / teacher_temp)
    row_scale = jnp.ones((ROWS,), jnp.float32)
    col_scale = jnp.ones((PROTOS,), jnp.float32)
    for sweep in range(SINK_ITERS):
        col_scale = 1.0 / lax.optimization_barrier(jnp.sum(exp_teacher * row_scale[:, None], axis=0))
        row_scale = 1.0 / lax.optimization_barrier(jnp.sum(exp_teacher * col_scale[None, :], axis=1))
    target = row_scale[:, None] * exp_teacher * col_scale[None, :]
    exp_student = jnp.exp(logits / student_temp)
    student_prob = exp_student / lax.optimization_barrier(jnp.sum(exp_student, axis=1, keepdims=True))
    grad_logits = (loss_scale * (student_prob - target) / student_temp).astype(jnp.bfloat16)
    proto_step = jnp.dot(grad_logits.T, student_hat, preferred_element_type=jnp.float32)
    proto_grad = (proto_step - proto_unit * lax.optimization_barrier(jnp.sum(proto_unit * proto_step, axis=1, keepdims=True))) * proto_inv
    row_step = jnp.dot(grad_logits, proto_hat, preferred_element_type=jnp.float32)
    student_grad = (row_step - student_unit * lax.optimization_barrier(jnp.sum(student_unit * row_step, axis=1, keepdims=True))) * student_inv
    return (student_grad, proto_grad)
```

```python
import functools

import jax
import jax.numpy as jnp
from jax import lax
from jax.experimental import pallas as pl
from jax.experimental.pallas import tpu as pltpu
from jax.sharding import Mesh
from jax.sharding import PartitionSpec as P

MESH = pl.DeviceIdType.MESH
AXES = ("wide_0", "wide_1", "narrow_0", "narrow_1")
SINK_ITERS = 3
NX, NU, CORES = 4, 8, 2
D = 512
OWN = 2
ROWS = NX * NU * NU * CORES * OWN
HALF = ROWS // CORES
SLAB = HALF // NX
TILE = NU * OWN
PROTOS = 512
BLOCK = 64
LANES = 128
TALL = ROWS // LANES
CUT = D // 2

epsilon = 1e-06
teacher_temp = 0.07
student_temp = 0.1

f32 = jnp.float32
bf16 = jnp.bfloat16


def inverse_norm(wide):
    return lax.rsqrt(jnp.sum(wide * wide, axis=1, keepdims=True) + epsilon)


def kernel(
    student_ref,
    teacher_ref,
    proto_ref,
    sgrad_ref,
    pgrad_ref,
    first,
    stage,
    gat_t,
    gat_s,
    proto_hat,
    proto_inv,
    e_t,
    e_s,
    cols,
    grad,
    near_src,
    near,
    far_src,
    far,
    part,
    other,
    cross,
    xbuf,
    ubuf,
    xslots,
    uslots,
    xsum,
    xuslots,
    xvsrc,
    xvslots,
    uvsrc,
    uvslots,
    first_send,
    first_recv,
    gat_send,
    gat_recv,
    swap_send,
    swap_recv,
    near_send,
    near_recv,
    far_send,
    far_recv,
    cross_send,
    cross_recv,
    big_send,
    big_recv,
    end_send,
    end_recv,
):
    x, y, z, c = (lax.axis_index(a) for a in AXES)
    u = z + c * (y - z)
    v = y + c * (z - y)
    oc = 1 - c

    def device(px, pu, pv):
        return (px, pv + c * (pu - pv), pu + c * (pv - pu), c)

    mate = (x, y, z, oc)

    def wait(ref, sem):
        pltpu.make_async_copy(ref, ref, sem).wait()

    def push(src, dst, send, recv, target):
        pltpu.make_async_remote_copy(
            src_ref=src, dst_ref=dst, send_sem=send, recv_sem=recv, device_id=target, device_id_type=MESH
        ).start()

    barrier = pltpu.get_barrier_semaphore()

    def greet_near(k, _):
        q = lax.rem(z * CORES + c + k, NU * CORES)
        pl.semaphore_signal(barrier, inc=1, device_id=(x, y, q // CORES, lax.rem(q, CORES)), device_id_type=MESH)
        return 0

    def greet_far(k, _):
        q = lax.rem(x * NU + y + k, NX * NU)
        pl.semaphore_signal(barrier, inc=1, device_id=(q // NU, lax.rem(q, NU), z, c), device_id_type=MESH)
        return 0

    def greet_side(k, _):
        px = lax.rem(x + 1 + k // (NU - 1), NX)
        pz = lax.rem(z + 1 + lax.rem(k, NU - 1), NU)
        pl.semaphore_signal(barrier, inc=1, device_id=(px, y, pz, c), device_id_type=MESH)
        return 0

    lax.fori_loop(1, NX * NU, greet_far, 0)
    lax.fori_loop(0, (NX - 1) * (NU - 1), greet_side, 0)
    lax.fori_loop(1, NU * CORES, greet_near, 0)

    wide_s = student_ref[...].astype(f32)
    wide_t = teacher_ref[...].astype(f32)
    s_inv = inverse_norm(wide_s)
    s_unit = wide_s * s_inv
    t_unit = wide_t * inverse_norm(wide_t)
    first[v, 0:OWN, :] = s_unit
    first[v, OWN : 2 * OWN, :] = t_unit

    def norm_block(i, _):
        at = pl.ds(pl.multiple_of(i * BLOCK, BLOCK), BLOCK)
        wide = proto_ref[at, :].astype(f32)
        inv = inverse_norm(wide)
        proto_inv[at, :] = jnp.broadcast_to(inv, (BLOCK, LANES))
        proto_hat[at, :] = (wide * inv).astype(bf16)
        return 0

    lax.fori_loop(0, PROTOS // BLOCK, norm_block, 0)

    pl.semaphore_wait(barrier, NU * CORES - 1 + NX * NU - 1 + (NX - 1) * (NU - 1))

    def send_first(k, _):
        push(first.at[v], first.at[v], first_send, first_recv, device(x, u, lax.rem(v + k, NU)))
        return 0

    lax.fori_loop(1, NU, send_first, 0)
    wait(first.at[pl.ds(0, NU - 1)], first_recv)
    for i in range(NU):
        stage[0, OWN * i : OWN * (i + 1), :] = first[i, 0:OWN, :]
        stage[1, OWN * i : OWN * (i + 1), :] = first[i, OWN : 2 * OWN, :]
    mine = pl.ds(pl.multiple_of(c * HALF + x * SLAB + u * TILE, TILE), TILE)
    gat_s[mine, :] = stage[0].astype(bf16)
    gat_t[mine, :] = stage[1].astype(bf16)

    def spread(buf, n):
        def send(k, _):
            q = lax.rem(x * NU + u + k, NX * NU)
            push(buf.at[mine], buf.at[mine], gat_send.at[n], gat_recv.at[n, x], device(q // NU, lax.rem(q, NU), v))
            return 0

        lax.fori_loop(1, NX * NU, send, 0)

    def slab(core, px):
        return pl.ds(pl.multiple_of(core * HALF + px * SLAB, SLAB), SLAB)

    def relay(buf, n):
        for k in range(NX):
            px = lax.rem(x + k, NX)
            wait(buf.at[pl.ds(0, SLAB - TILE if k == 0 else SLAB)], gat_recv.at[n, px])
            here = slab(c, px)
            push(buf.at[here], buf.at[here], swap_send.at[n], swap_recv.at[n], mate)

    def settle(buf, n):
        wait(buf.at[pl.ds(0, HALF)], swap_recv.at[n])
        wait(buf.at[pl.ds(0, HALF - TILE)], gat_send.at[n])
        wait(buf.at[pl.ds(0, HALF)], swap_send.at[n])

    spread(gat_t, 1)
    spread(gat_s, 0)
    wait(first.at[pl.ds(0, NU - 1)], first_send)
    relay(gat_t, 1)
    settle(gat_t, 1)

    def exponentials(buf, out, temp):
        for k in range(ROWS // 256):
            at = slice(k * 256, (k + 1) * 256)
            product = lax.dot_general(
                proto_hat[...], buf[at, :], (((1,), (1,)), ((), ())), preferred_element_type=f32
            )
            out[:, at] = jnp.exp(product * (1.0 / temp))

    def folded(value):
        return jnp.sum(value.reshape(BLOCK // 8, 8, ROWS), axis=0)

    def flat(ref):
        return jnp.concatenate([ref[k : k + 1, :] for k in range(TALL)], axis=1)

    def put(dst, at, acc):
        for k in range(TALL):
            dst[at + k : at + k + 1, :] = jnp.sum(acc[:, k * LANES : (k + 1) * LANES], axis=0, keepdims=True)

    def sweep(scale):
        def body(i, acc):
            at = pl.ds(pl.multiple_of(i * BLOCK, BLOCK), BLOCK)
            e = e_t[at, :]
            weighed = e if scale is None else e * scale
            col = 1.0 / jnp.sum(weighed, axis=1, keepdims=True)
            cols[at, :] = jnp.broadcast_to(col, (BLOCK, LANES))
            return acc + folded(e * col)

        return lax.fori_loop(0, PROTOS // BLOCK, body, jnp.zeros((8, ROWS), f32))

    def near_start(n, tall):
        me = z * CORES + c

        def send(k, _):
            q = lax.rem(me + k, NU * CORES)
            src = near_src.at[n, pl.ds(0, tall)]
            push(src, near.at[n, me, pl.ds(0, tall)], near_send.at[n], near_recv.at[n], (x, y, q // CORES, lax.rem(q, CORES)))
            return 0

        lax.fori_loop(1, NU * CORES, send, 0)
        near[n, me, 0:tall, :] = near_src[n, 0:tall, :]

    def near_end(n, tall):
        for sem in (near_recv, near_send):
            wait(near.at[n, pl.ds(0, NU * CORES - 1), pl.ds(0, tall)], sem.at[n])
        far_src[n, 0:tall, :] = jnp.sum(near[n, :, 0:tall, :], axis=0)

    def far_start(n, tall):
        me = x * NU + y

        def send(k, _):
            q = lax.rem(me + k, NX * NU)
            src = far_src.at[n, pl.ds(0, tall)]
            push(src, far.at[n, me, pl.ds(0, tall)], far_send.at[n], far_recv.at[n], (q // NU, lax.rem(q, NU), z, c))
            return 0

        lax.fori_loop(1, NX * NU, send, 0)
        far[n, me, 0:tall, :] = far_src[n, 0:tall, :]

    def far_end(n, tall):
        for sem in (far_recv, far_send):
            wait(far.at[n, pl.ds(0, NX * NU - 1), pl.ds(0, tall)], sem.at[n])
        return 1.0 / jnp.sum(far[n, :, 0:tall, :], axis=0)

    def row_of(inverse):
        part[...] = inverse
        return flat(part)

    exponentials(gat_t, e_t, teacher_temp)
    put(near_src.at[0], 0, sweep(None))
    near_start(0, TALL)
    relay(gat_s, 0)
    near_end(0, TALL)
    far_start(0, TALL)
    settle(gat_s, 0)
    exponentials(gat_s, e_s, student_temp)

    def student_sum(i, acc):
        at = pl.ds(pl.multiple_of(i * BLOCK, BLOCK), BLOCK)
        return acc + folded(e_s[at, :])

    put(near_src.at[1], TALL, lax.fori_loop(0, PROTOS // BLOCK, student_sum, jnp.zeros((8, ROWS), f32)))
    row_scale = row_of(far_end(0, TALL))
    put(near_src.at[1], 0, sweep(row_scale))
    near_start(1, 2 * TALL)
    near_end(1, 2 * TALL)
    far_start(1, 2 * TALL)
    both = far_end(1, 2 * TALL)
    row_scale = row_of(both[0:TALL])
    put(near_src.at[2], 0, sweep(row_scale))
    near_start(2, TALL)

    student_scale = row_of(both[TALL:] * (1.0 / student_temp))

    def scale_block(i, _):
        at = pl.ds(pl.multiple_of(i * BLOCK, BLOCK), BLOCK)
        e_s[at, :] = e_s[at, :] * student_scale
        e_t[at, :] = e_t[at, :] * cols[at, 0:1]
        return 0

    lax.fori_loop(0, PROTOS // BLOCK, scale_block, 0)
    near_end(2, TALL)
    far_start(2, TALL)
    row_scale = row_of(far_end(2, TALL) * (1.0 / student_temp))

    def grad_block(i, _):
        at = pl.ds(pl.multiple_of(i * BLOCK, BLOCK), BLOCK)
        grad[at, :] = (e_s[at, :] - e_t[at, :] * row_scale).astype(bf16)
        return 0

    lax.fori_loop(0, PROTOS // BLOCK, grad_block, 0)

    def row_product(core, k):
        at = pl.ds(pl.multiple_of(core * HALF + k * 256, 256), 256)
        return lax.dot_general(grad[:, at], proto_hat[...], (((0,), (0,)), ((), ())), preferred_element_type=f32)

    for k in range(HALF // 256):
        at = pl.ds(k * 256, 256)
        other[at, :] = row_product(oc, k)
        push(other.at[at], cross.at[at], cross_send, cross_recv.at[k], mate)
    per = 256 // SLAB
    for k in range(HALF // 256):
        at = pl.ds(k * 256, 256)
        mine_part = row_product(c, k)
        wait(cross.at[at], cross_recv.at[k])
        total = mine_part + cross[at, :]
        xbuf[pl.ds(k * per, per)] = total[:, :CUT].reshape(per, SLAB, CUT)
        ubuf[pl.ds(k * per, per)] = total[:, CUT:].reshape(per, NU, TILE, CUT)

    def send_x(k, _):
        px = lax.rem(x + k, NX)
        push(xbuf.at[px], xslots.at[x], big_send.at[0], big_recv.at[0], device(px, u, v))
        return 0

    def send_u(k, _):
        pu = lax.rem(u + k, NU)
        push(ubuf.at[:, pu], uslots.at[u], big_send.at[1], big_recv.at[1], device(x, pu, v))
        return 0

    lax.fori_loop(1, NX, send_x, 0)
    lax.fori_loop(1, NU, send_u, 0)
    xslots[x] = xbuf[x]
    uslots[u] = ubuf[:, u]

    def proto_block(i):
        at = slice(i * 256, (i + 1) * 256)
        step = jnp.dot(grad[at, :], gat_s[...], preferred_element_type=f32)
        inv = proto_inv[at, 0:1]
        unit = proto_ref[at, :].astype(f32) * inv
        pgrad_ref[at, :] = (step - unit * jnp.sum(unit * step, axis=1, keepdims=True)) * inv

    for i in range(PROTOS // 256):
        proto_block(i)

    for sem in (big_recv, big_send):
        wait(xslots.at[pl.ds(0, NX - 1)], sem.at[0])
    xsum[...] = jnp.sum(xslots[...], axis=0)

    def send_xu(k, _):
        pu = lax.rem(u + k, NU)
        src = xsum.at[pl.ds(pl.multiple_of(pu * TILE, TILE), TILE)]
        push(src, xuslots.at[u], end_send.at[0], end_recv.at[0], device(x, pu, v))
        return 0

    lax.fori_loop(1, NU, send_xu, 0)
    xuslots[u] = xsum[pl.ds(pl.multiple_of(u * TILE, TILE), TILE), :]

    for sem in (big_recv, big_send):
        wait(uslots.at[pl.ds(0, NU - 1)], sem.at[1])
    usum = jnp.sum(uslots[...], axis=0)
    for px in range(NX):
        for pv in range(NU):
            uvsrc[px * NU + pv] = usum[px, pv * OWN : (pv + 1) * OWN, :]

    def send_uv(k, _):
        q = lax.rem(x * NU + v + k, NX * NU)
        push(uvsrc.at[q], uvslots.at[x * NU + v], end_send.at[1], end_recv.at[1], device(q // NU, u, lax.rem(q, NU)))
        return 0

    lax.fori_loop(1, NX * NU, send_uv, 0)
    uvslots[x * NU + v] = uvsrc[x * NU + v]

    for sem in (end_recv, end_send):
        wait(xuslots.at[pl.ds(0, NU - 1)], sem.at[0])
    xusum = jnp.sum(xuslots[...], axis=0)
    for pv in range(NU):
        xvsrc[pv] = xusum[pv * OWN : (pv + 1) * OWN, :]

    def send_xv(k, _):
        pv = lax.rem(v + k, NU)
        push(xvsrc.at[pv], xvslots.at[v], end_send.at[2], end_recv.at[2], device(x, u, pv))
        return 0

    lax.fori_loop(1, NU, send_xv, 0)
    xvslots[v] = xvsrc[v]

    for sem in (end_recv, end_send):
        wait(uvslots.at[pl.ds(0, NX * NU - 1)], sem.at[1])
    right = jnp.sum(uvslots[...], axis=0)
    for sem in (end_recv, end_send):
        wait(xvslots.at[pl.ds(0, NU - 1)], sem.at[2])
    left = jnp.sum(xvslots[...], axis=0)
    wait(other, cross_send)

    step = jnp.concatenate([left, right], axis=1)
    sgrad_ref[...] = (step - s_unit * jnp.sum(s_unit * step, axis=1, keepdims=True)) * s_inv


def on_device(student, teacher, protos):
    vmem = pl.BlockSpec(memory_space=pltpu.VMEM)
    dma = pltpu.SemaphoreType.DMA
    return pl.pallas_call(
        kernel,
        out_shape=(
            jax.ShapeDtypeStruct((OWN, D), f32),
            jax.ShapeDtypeStruct((PROTOS, D), f32),
        ),
        in_specs=[vmem] * 3,
        out_specs=(vmem, vmem),
        scratch_shapes=[
            pltpu.VMEM((NU, 2 * OWN, D), f32),
            pltpu.VMEM((2, TILE, D), f32),
            pltpu.VMEM((ROWS, D), bf16),
            pltpu.VMEM((ROWS, D), bf16),
            pltpu.VMEM((PROTOS, D), bf16),
            pltpu.VMEM((PROTOS, LANES), f32),
            pltpu.VMEM((PROTOS, ROWS), f32),
            pltpu.VMEM((PROTOS, ROWS), f32),
            pltpu.VMEM((PROTOS, LANES), f32),
            pltpu.VMEM((PROTOS, ROWS), bf16),
            pltpu.VMEM((SINK_ITERS, 2 * TALL, LANES), f32),
            pltpu.VMEM((SINK_ITERS, NU * CORES, 2 * TALL, LANES), f32),
            pltpu.VMEM((SINK_ITERS, 2 * TALL, LANES), f32),
            pltpu.VMEM((SINK_ITERS, NX * NU, 2 * TALL, LANES), f32),
            pltpu.VMEM((TALL, LANES), f32),
            pltpu.VMEM((HALF, D), f32),
            pltpu.VMEM((HALF, D), f32),
            pltpu.VMEM((NX, SLAB, CUT), f32),
            pltpu.VMEM((NX, NU, TILE, D - CUT), f32),
            pltpu.VMEM((NX, SLAB, CUT), f32),
            pltpu.VMEM((NU, NX, TILE, D - CUT), f32),
            pltpu.VMEM((SLAB, CUT), f32),
            pltpu.VMEM((NU, TILE, CUT), f32),
            pltpu.VMEM((NU, OWN, CUT), f32),
            pltpu.VMEM((NU, OWN, CUT), f32),
            pltpu.VMEM((NX * NU, OWN, D - CUT), f32),
            pltpu.VMEM((NX * NU, OWN, D - CUT), f32),
            dma,
            dma,
            dma((2,)),
            dma((2, NX)),
            dma((2,)),
            dma((2,)),
            dma((SINK_ITERS,)),
            dma((SINK_ITERS,)),
            dma((SINK_ITERS,)),
            dma((SINK_ITERS,)),
            dma,
            dma((2,)),
            dma((2,)),
            dma((2,)),
            dma((3,)),
            dma((3,)),
        ],
        compiler_params=pltpu.CompilerParams(
            collective_id=0, has_side_effects=True, vmem_limit_bytes=48 << 20
        ),
        name="prototype_head",
    )(student, teacher, protos)


def solution(mesh):
    torus = Mesh(mesh.devices.reshape(NX, NU, NU, CORES), AXES)
    return jax.shard_map(
        on_device,
        mesh=torus,
        in_specs=(P(AXES, None),) * 3,
        out_specs=(P(AXES, None), P(AXES, None)),
        check_vma=False,
    )
```

```python
import functools

import jax
import jax.numpy as jnp
from jax import lax
from jax.experimental import pallas as pl
from jax.experimental.pallas import tpu as pltpu
from jax.sharding import Mesh
from jax.sharding import PartitionSpec as P

MESH = pl.DeviceIdType.MESH
AXES = ("wide_0", "wide_1", "narrow_0", "narrow_1")
SUMS = 4
NX, NU, CORES = 4, 8, 2
D = 512
OWN = 2
ROWS = NX * NU * NU * CORES * OWN
HALF = ROWS // CORES
SLAB = HALF // NX
TILE = NU * OWN
PROTOS = 512
BLOCK = 64
LANES = 128
TALL = ROWS // LANES
CUT = D // 2

epsilon = 1e-06
teacher_temp = 0.07
student_temp = 0.1

f32 = jnp.float32
bf16 = jnp.bfloat16


def inverse_norm(wide):
    return lax.rsqrt(jnp.sum(wide * wide, axis=1, keepdims=True) + epsilon)


def kernel(
    student_hbm,
    teacher_hbm,
    proto_hbm,
    sgrad_ref,
    pgrad_ref,
    student_ref,
    teacher_ref,
    proto_ref,
    first,
    stage,
    gat_t,
    gat_s,
    proto_hat,
    proto_inv,
    e_t,
    e_s,
    cols,
    grad,
    near_src,
    near,
    far_src,
    far,
    part,
    other,
    cross,
    xbuf,
    ubuf,
    xslots,
    uslots,
    xsum,
    xuslots,
    xvsrc,
    xvslots,
    uvsrc,
    uvslots,
    load,
    first_send,
    first_recv,
    gat_send,
    gat_recv,
    swap_send,
    swap_recv,
    near_send,
    near_recv,
    far_send,
    far_recv,
    cross_send,
    cross_recv,
    big_send,
    big_recv,
    end_send,
    end_recv,
):
    x, y, z, c = (lax.axis_index(a) for a in AXES)
    u = z + c * (y - z)
    v = y + c * (z - y)
    oc = 1 - c

    def device(px, pu, pv):
        return (px, pv + c * (pu - pv), pu + c * (pv - pu), c)

    mate = (x, y, z, oc)

    def turned(at, k, n):
        return lax.rem(at + n // 2 + (1 - 2 * lax.rem(k, 2)) * ((k + 1) // 2), n)

    def near_peer(k):
        return (x, y, turned(z, k // CORES, NU), lax.rem(c + 1 + lax.rem(k, CORES), CORES))

    def far_peer(k):
        return (turned(x, lax.rem(k, NX), NX), turned(y, k // NX, NU), z, c)

    def plane(k, at):
        return turned(x, lax.rem(k, NX), NX), turned(at, k // NX, NU)

    def wait(ref, sem):
        pltpu.make_async_copy(ref, ref, sem).wait()

    def push(src, dst, send, recv, target):
        pltpu.make_async_remote_copy(
            src_ref=src, dst_ref=dst, send_sem=send, recv_sem=recv, device_id=target, device_id_type=MESH
        ).start()

    barrier = pltpu.get_barrier_semaphore()

    def greet(target):
        pl.semaphore_signal(barrier, inc=1, device_id=target, device_id_type=MESH)
        return 0

    def greet_side(k, _):
        return greet((turned(x, lax.rem(k, NX - 1), NX), y, turned(z, k // (NX - 1), NU), c))

    lax.fori_loop(0, NX * NU - 1, lambda k, _: greet(far_peer(k)), 0)
    lax.fori_loop(0, (NX - 1) * (NU - 1), greet_side, 0)
    lax.fori_loop(0, NU * CORES - 1, lambda k, _: greet(near_peer(k)), 0)

    inputs = [
        pltpu.make_async_copy(src, dst, load.at[i])
        for i, (src, dst) in enumerate(
            ((student_hbm, student_ref), (teacher_hbm, teacher_ref), (proto_hbm, proto_ref))
        )
    ]
    for copy in inputs:
        copy.start()
    for copy in inputs[:2]:
        copy.wait()

    wide_s = student_ref[...].astype(f32)
    wide_t = teacher_ref[...].astype(f32)
    s_inv = inverse_norm(wide_s)
    s_unit = wide_s * s_inv
    t_unit = wide_t * inverse_norm(wide_t)
    first[v, 0:OWN, :] = s_unit
    first[v, OWN : 2 * OWN, :] = t_unit

    def norm_block(i, _):
        at = pl.ds(pl.multiple_of(i * BLOCK, BLOCK), BLOCK)
        wide = proto_ref[at, :].astype(f32)
        inv = inverse_norm(wide)
        proto_inv[at, :] = jnp.broadcast_to(inv, (BLOCK, LANES))
        proto_hat[at, :] = (wide * inv).astype(bf16)
        return 0

    inputs[2].wait()
    lax.fori_loop(0, PROTOS // BLOCK, norm_block, 0)

    pl.semaphore_wait(barrier, NU * CORES - 1 + NX * NU - 1 + (NX - 1) * (NU - 1))

    def send_first(k, _):
        push(first.at[v], first.at[v], first_send, first_recv, device(x, u, turned(v, k, NU)))
        return 0

    lax.fori_loop(0, NU - 1, send_first, 0)
    wait(first.at[pl.ds(0, NU - 1)], first_recv)
    for i in range(NU):
        stage[0, OWN * i : OWN * (i + 1), :] = first[i, 0:OWN, :]
        stage[1, OWN * i : OWN * (i + 1), :] = first[i, OWN : 2 * OWN, :]
    mine = pl.ds(pl.multiple_of(c * HALF + x * SLAB + u * TILE, TILE), TILE)
    gat_s[mine, :] = stage[0].astype(bf16)
    gat_t[mine, :] = stage[1].astype(bf16)

    def spread(buf, n):
        def send(k, _):
            px, pu = plane(k, u)
            push(buf.at[mine], buf.at[mine], gat_send.at[n], gat_recv.at[n, x], device(px, pu, v))
            return 0

        lax.fori_loop(0, NX * NU - 1, send, 0)

    def slab(core, px):
        return pl.ds(pl.multiple_of(core * HALF + px * SLAB, SLAB), SLAB)

    def relay(buf, n):
        for k in range(NX):
            px = lax.rem(x + k, NX)
            wait(buf.at[pl.ds(0, SLAB - TILE if k == 0 else SLAB)], gat_recv.at[n, px])
            here = slab(c, px)
            push(buf.at[here], buf.at[here], swap_send.at[n], swap_recv.at[n], mate)

    def settle(buf, n):
        wait(buf.at[pl.ds(0, HALF)], swap_recv.at[n])
        wait(buf.at[pl.ds(0, HALF - TILE)], gat_send.at[n])
        wait(buf.at[pl.ds(0, HALF)], swap_send.at[n])

    spread(gat_t, 1)
    wait(first.at[pl.ds(0, NU - 1)], first_send)
    relay(gat_t, 1)
    settle(gat_t, 1)

    def exponentials(buf, out, temp):
        for k in range(ROWS // 256):
            at = slice(k * 256, (k + 1) * 256)
            product = lax.dot_general(
                proto_hat[...], buf[at, :], (((1,), (1,)), ((), ())), preferred_element_type=f32
            )
            out[:, at] = jnp.exp(product * (1.0 / temp))

    def folded(value):
        return jnp.sum(value.reshape(BLOCK // 8, 8, ROWS), axis=0)

    def flat(ref):
        return jnp.concatenate([ref[k : k + 1, :] for k in range(TALL)], axis=1)

    def put(dst, acc):
        for k in range(TALL):
            dst[k : k + 1, :] = jnp.sum(acc[:, k * LANES : (k + 1) * LANES], axis=0, keepdims=True)

    def sweep(scale):
        def body(i, acc):
            at = pl.ds(pl.multiple_of(i * BLOCK, BLOCK), BLOCK)
            e = e_t[at, :]
            weighed = e if scale is None else e * scale
            col = 1.0 / jnp.sum(weighed, axis=1, keepdims=True)
            cols[at, :] = jnp.broadcast_to(col, (BLOCK, LANES))
            return acc + folded(e * col)

        return lax.fori_loop(0, PROTOS // BLOCK, body, jnp.zeros((8, ROWS), f32))

    def near_start(n):
        me = z * CORES + c

        def send(k, _):
            push(near_src.at[n], near.at[n, me], near_send.at[n], near_recv.at[n], near_peer(k))
            return 0

        lax.fori_loop(0, NU * CORES - 1, send, 0)
        near[n, me] = near_src[n]

    def near_end(n):
        for sem in (near_recv, near_send):
            wait(near.at[n, pl.ds(0, NU * CORES - 1)], sem.at[n])
        far_src[n] = jnp.sum(near[n], axis=0)

    def far_start(n):
        me = x * NU + y

        def send(k, _):
            push(far_src.at[n], far.at[n, me], far_send.at[n], far_recv.at[n], far_peer(k))
            return 0

        lax.fori_loop(0, NX * NU - 1, send, 0)
        far[n, me] = far_src[n]

    def far_end(n):
        for sem in (far_recv, far_send):
            wait(far.at[n, pl.ds(0, NX * NU - 1)], sem.at[n])
        return 1.0 / jnp.sum(far[n], axis=0)

    def row_of(inverse):
        part[...] = inverse
        return flat(part)

    def student_sum(i, acc):
        at = pl.ds(pl.multiple_of(i * BLOCK, BLOCK), BLOCK)
        return acc + folded(e_s[at, :])

    exponentials(gat_t, e_t, teacher_temp)
    put(near_src.at[0], sweep(None))
    near_start(0)
    spread(gat_s, 0)
    near_end(0)
    far_start(0)
    relay(gat_s, 0)
    row_scale = row_of(far_end(0))

    put(near_src.at[1], sweep(row_scale))
    near_start(1)
    settle(gat_s, 0)
    exponentials(gat_s, e_s, student_temp)
    put(near_src.at[3], lax.fori_loop(0, PROTOS // BLOCK, student_sum, jnp.zeros((8, ROWS), f32)))
    near_start(3)
    near_end(1)
    far_start(1)
    near_end(3)
    far_start(3)
    row_scale = row_of(far_end(1))

    put(near_src.at[2], sweep(row_scale))
    near_start(2)
    student_scale = row_of(far_end(3) * (1.0 / student_temp))

    def scale_block(i, _):
        at = pl.ds(pl.multiple_of(i * BLOCK, BLOCK), BLOCK)
        e_s[at, :] = e_s[at, :] * student_scale
        e_t[at, :] = e_t[at, :] * cols[at, 0:1]
        return 0

    lax.fori_loop(0, PROTOS // BLOCK, scale_block, 0)
    near_end(2)
    far_start(2)
    row_scale = row_of(far_end(2) * (1.0 / student_temp))

    def grad_block(i, _):
        at = pl.ds(pl.multiple_of(i * BLOCK, BLOCK), BLOCK)
        grad[at, :] = (e_s[at, :] - e_t[at, :] * row_scale).astype(bf16)
        return 0

    lax.fori_loop(0, PROTOS // BLOCK, grad_block, 0)

    def row_product(at):
        return lax.dot_general(grad[:, at], proto_hat[...], (((0,), (0,)), ((), ())), preferred_element_type=f32)

    for k in range(NX):
        px = turned(x, k, NX)
        other[px] = row_product(slab(oc, px))
        push(other.at[px], cross.at[px], cross_send, cross_recv.at[px], mate)
    for k in range(NX):
        px = turned(x, k, NX)
        mine_part = row_product(slab(c, px))
        wait(cross.at[px], cross_recv.at[px])
        total = mine_part + cross[px]
        xbuf[px] = total[:, :CUT]
        ubuf[px] = total[:, CUT:].reshape(NU, TILE, D - CUT)
        if k < NX - 1:
            push(xbuf.at[px], xslots.at[x], big_send.at[0], big_recv.at[0], device(px, u, v))

    def send_u(k, _):
        pu = turned(u, k, NU)
        push(ubuf.at[:, pu], uslots.at[u], big_send.at[1], big_recv.at[1], device(x, pu, v))
        return 0

    lax.fori_loop(0, NU - 1, send_u, 0)
    xslots[x] = xbuf[x]
    uslots[u] = ubuf[:, u]

    def proto_block(i):
        at = slice(i * 256, (i + 1) * 256)
        step = jnp.dot(grad[at, :], gat_s[...], preferred_element_type=f32)
        inv = proto_inv[at, 0:1]
        unit = proto_ref[at, :].astype(f32) * inv
        pgrad_ref[at, :] = (step - unit * jnp.sum(unit * step, axis=1, keepdims=True)) * inv

    for i in range(PROTOS // 256):
        proto_block(i)

    for sem in (big_recv, big_send):
        wait(xslots.at[pl.ds(0, NX - 1)], sem.at[0])
    xsum[...] = jnp.sum(xslots[...], axis=0)

    def send_xu(k, _):
        pu = turned(u, k, NU)
        src = xsum.at[pl.ds(pl.multiple_of(pu * TILE, TILE), TILE)]
        push(src, xuslots.at[u], end_send.at[0], end_recv.at[0], device(x, pu, v))
        return 0

    lax.fori_loop(0, NU - 1, send_xu, 0)
    xuslots[u] = xsum[pl.ds(pl.multiple_of(u * TILE, TILE), TILE), :]

    for sem in (big_recv, big_send):
        wait(uslots.at[pl.ds(0, NU - 1)], sem.at[1])
    usum = jnp.sum(uslots[...], axis=0)
    for px in range(NX):
        for pv in range(NU):
            uvsrc[px * NU + pv] = usum[px, pv * OWN : (pv + 1) * OWN, :]

    def send_uv(k, _):
        px, pv = plane(k, v)
        push(uvsrc.at[px * NU + pv], uvslots.at[x * NU + v], end_send.at[1], end_recv.at[1], device(px, u, pv))
        return 0

    lax.fori_loop(0, NX * NU - 1, send_uv, 0)
    uvslots[x * NU + v] = uvsrc[x * NU + v]

    for sem in (end_recv, end_send):
        wait(xuslots.at[pl.ds(0, NU - 1)], sem.at[0])
    xusum = jnp.sum(xuslots[...], axis=0)
    for pv in range(NU):
        xvsrc[pv] = xusum[pv * OWN : (pv + 1) * OWN, :]

    def send_xv(k, _):
        pv = turned(v, k, NU)
        push(xvsrc.at[pv], xvslots.at[v], end_send.at[2], end_recv.at[2], device(x, u, pv))
        return 0

    lax.fori_loop(0, NU - 1, send_xv, 0)
    xvslots[v] = xvsrc[v]

    for sem in (end_recv, end_send):
        wait(uvslots.at[pl.ds(0, NX * NU - 1)], sem.at[1])
    right = jnp.sum(uvslots[...], axis=0)
    for sem in (end_recv, end_send):
        wait(xvslots.at[pl.ds(0, NU - 1)], sem.at[2])
    left = jnp.sum(xvslots[...], axis=0)
    wait(other, cross_send)

    step = jnp.concatenate([left, right], axis=1)
    sgrad_ref[...] = (step - s_unit * jnp.sum(s_unit * step, axis=1, keepdims=True)) * s_inv


def on_device(student, teacher, protos):
    vmem = pl.BlockSpec(memory_space=pltpu.VMEM)
    dma = pltpu.SemaphoreType.DMA
    return pl.pallas_call(
        kernel,
        out_shape=(
            jax.ShapeDtypeStruct((OWN, D), f32),
            jax.ShapeDtypeStruct((PROTOS, D), f32),
        ),
        in_specs=[pl.BlockSpec(memory_space=pltpu.HBM)] * 3,
        out_specs=(vmem, vmem),
        scratch_shapes=[
            pltpu.VMEM((OWN, D), bf16),
            pltpu.VMEM((OWN, D), bf16),
            pltpu.VMEM((PROTOS, D), bf16),
            pltpu.VMEM((NU, 2 * OWN, D), f32),
            pltpu.VMEM((2, TILE, D), f32),
            pltpu.VMEM((ROWS, D), bf16),
            pltpu.VMEM((ROWS, D), bf16),
            pltpu.VMEM((PROTOS, D), bf16),
            pltpu.VMEM((PROTOS, LANES), f32),
            pltpu.VMEM((PROTOS, ROWS), f32),
            pltpu.VMEM((PROTOS, ROWS), f32),
            pltpu.VMEM((PROTOS, LANES), f32),
            pltpu.VMEM((PROTOS, ROWS), bf16),
            pltpu.VMEM((SUMS, TALL, LANES), f32),
            pltpu.VMEM((SUMS, NU * CORES, TALL, LANES), f32),
            pltpu.VMEM((SUMS, TALL, LANES), f32),
            pltpu.VMEM((SUMS, NX * NU, TALL, LANES), f32),
            pltpu.VMEM((TALL, LANES), f32),
            pltpu.VMEM((NX, SLAB, D), f32),
            pltpu.VMEM((NX, SLAB, D), f32),
            pltpu.VMEM((NX, SLAB, CUT), f32),
            pltpu.VMEM((NX, NU, TILE, D - CUT), f32),
            pltpu.VMEM((NX, SLAB, CUT), f32),
            pltpu.VMEM((NU, NX, TILE, D - CUT), f32),
            pltpu.VMEM((SLAB, CUT), f32),
            pltpu.VMEM((NU, TILE, CUT), f32),
            pltpu.VMEM((NU, OWN, CUT), f32),
            pltpu.VMEM((NU, OWN, CUT), f32),
            pltpu.VMEM((NX * NU, OWN, D - CUT), f32),
            pltpu.VMEM((NX * NU, OWN, D - CUT), f32),
            dma((3,)),
            dma,
            dma,
            dma((2,)),
            dma((2, NX)),
            dma((2,)),
            dma((2,)),
            dma((SUMS,)),
            dma((SUMS,)),
            dma((SUMS,)),
            dma((SUMS,)),
            dma,
            dma((NX,)),
            dma((2,)),
            dma((2,)),
            dma((3,)),
            dma((3,)),
        ],
        compiler_params=pltpu.CompilerParams(
            collective_id=0, has_side_effects=True, vmem_limit_bytes=48 << 20
        ),
        name="prototype_head",
    )(*(pltpu.with_memory_space_constraint(a, pltpu.HBM) for a in (student, teacher, protos)))


def solution(mesh):
    torus = Mesh(mesh.devices.reshape(NX, NU, NU, CORES), AXES)
    return jax.shard_map(
        on_device,
        mesh=torus,
        in_specs=(P(AXES, None),) * 3,
        out_specs=(P(AXES, None), P(AXES, None)),
        check_vma=False,
    )
```

```python
import functools

import jax
import jax.numpy as jnp
from jax import lax
from jax.experimental import pallas as pl
from jax.experimental.pallas import tpu as pltpu
from jax.sharding import Mesh
from jax.sharding import PartitionSpec as P

MESH = pl.DeviceIdType.MESH
AXES = ("wide_0", "wide_1", "narrow_0", "narrow_1")
SUMS = 4
NX, NU, CORES = 4, 8, 2
D = 512
OWN = 2
ROWS = NX * NU * NU * CORES * OWN
HALF = ROWS // CORES
SLAB = HALF // NX
TILE = NU * OWN
PROTOS = 512
BLOCK = 64
LANES = 128
TALL = ROWS // LANES
CUT = D // 2

epsilon = 1e-06
teacher_temp = 0.07
student_temp = 0.1

f32 = jnp.float32
bf16 = jnp.bfloat16


def inverse_norm(wide):
    return lax.rsqrt(jnp.sum(wide * wide, axis=1, keepdims=True) + epsilon)


def kernel(
    student_hbm,
    teacher_hbm,
    proto_hbm,
    sgrad_ref,
    pgrad_ref,
    student_ref,
    teacher_ref,
    proto_ref,
    first,
    stage,
    gat_t,
    gat_s,
    proto_hat,
    proto_inv,
    e_t,
    e_s,
    cols,
    grad,
    near_src,
    near,
    far_src,
    far,
    part,
    own,
    proto_mate,
    grad_mate,
    xbuf,
    ubuf,
    xslots,
    uslots,
    xsum,
    xuslots,
    xvsrc,
    xvslots,
    uvsrc,
    uvslots,
    load,
    first_send,
    first_recv,
    gat_send,
    gat_recv,
    swap_send,
    swap_recv,
    near_send,
    near_recv,
    far_send,
    far_recv,
    mate_send,
    mate_recv,
    big_send,
    big_recv,
    end_send,
    end_recv,
):
    x, y, z, c = (lax.axis_index(a) for a in AXES)
    u = z + c * (y - z)
    v = y + c * (z - y)
    oc = 1 - c

    def device(px, pu, pv):
        return (px, pv + c * (pu - pv), pu + c * (pv - pu), c)

    mate = (x, y, z, oc)

    def turned(at, k, n):
        return lax.rem(at + n // 2 + (1 - 2 * lax.rem(k, 2)) * ((k + 1) // 2), n)

    def near_peer(k):
        return (x, y, turned(z, k // CORES, NU), lax.rem(c + 1 + lax.rem(k, CORES), CORES))

    def far_peer(k):
        return (turned(x, lax.rem(k, NX), NX), turned(y, k // NX, NU), z, c)

    def plane(k, at):
        return turned(x, lax.rem(k, NX), NX), turned(at, k // NX, NU)

    def wait(ref, sem):
        pltpu.make_async_copy(ref, ref, sem).wait()

    def push(src, dst, send, recv, target):
        pltpu.make_async_remote_copy(
            src_ref=src, dst_ref=dst, send_sem=send, recv_sem=recv, device_id=target, device_id_type=MESH
        ).start()

    barrier = pltpu.get_barrier_semaphore()

    def greet(target):
        pl.semaphore_signal(barrier, inc=1, device_id=target, device_id_type=MESH)
        return 0

    def greet_side(k, _):
        return greet((turned(x, lax.rem(k, NX - 1), NX), y, turned(z, k // (NX - 1), NU), c))

    lax.fori_loop(0, NX * NU - 1, lambda k, _: greet(far_peer(k)), 0)
    lax.fori_loop(0, (NX - 1) * (NU - 1), greet_side, 0)
    lax.fori_loop(0, NU * CORES - 1, lambda k, _: greet(near_peer(k)), 0)

    inputs = [
        pltpu.make_async_copy(src, dst, load.at[i])
        for i, (src, dst) in enumerate(
            ((student_hbm, student_ref), (teacher_hbm, teacher_ref), (proto_hbm, proto_ref))
        )
    ]
    for copy in inputs:
        copy.start()
    for copy in inputs[:2]:
        copy.wait()

    wide_s = student_ref[...].astype(f32)
    wide_t = teacher_ref[...].astype(f32)
    s_inv = inverse_norm(wide_s)
    s_unit = wide_s * s_inv
    t_unit = wide_t * inverse_norm(wide_t)
    first[v, 0:OWN, :] = s_unit
    first[v, OWN : 2 * OWN, :] = t_unit

    def norm_block(i, _):
        at = pl.ds(pl.multiple_of(i * BLOCK, BLOCK), BLOCK)
        wide = proto_ref[at, :].astype(f32)
        inv = inverse_norm(wide)
        proto_inv[at, :] = jnp.broadcast_to(inv, (BLOCK, LANES))
        proto_hat[at, :] = (wide * inv).astype(bf16)
        return 0

    inputs[2].wait()
    lax.fori_loop(0, PROTOS // BLOCK, norm_block, 0)

    pl.semaphore_wait(barrier, NU * CORES - 1 + NX * NU - 1 + (NX - 1) * (NU - 1))

    def send_first(k, _):
        push(first.at[v], first.at[v], first_send, first_recv, device(x, u, turned(v, k, NU)))
        return 0

    lax.fori_loop(0, NU - 1, send_first, 0)
    wait(first.at[pl.ds(0, NU - 1)], first_recv)
    for i in range(NU):
        stage[0, OWN * i : OWN * (i + 1), :] = first[i, 0:OWN, :]
        stage[1, OWN * i : OWN * (i + 1), :] = first[i, OWN : 2 * OWN, :]
    mine = pl.ds(pl.multiple_of(c * HALF + x * SLAB + u * TILE, TILE), TILE)
    gat_s[mine, :] = stage[0].astype(bf16)
    gat_t[mine, :] = stage[1].astype(bf16)

    def spread(buf, n, start=0, stop=NX * NU - 1):
        def send(k, _):
            px, pu = turned(x, k // NU, NX), turned(u, lax.rem(k, NU), NU)
            push(buf.at[mine], buf.at[mine], gat_send.at[n], gat_recv.at[n, x], device(px, pu, v))
            return 0

        lax.fori_loop(start, stop, send, 0)

    def slab(core, px):
        return pl.ds(pl.multiple_of(core * HALF + px * SLAB, SLAB), SLAB)

    def relay(buf, n):
        for k in range(NX):
            px = turned(x, k, NX)
            wait(buf.at[pl.ds(0, SLAB - TILE if k == NX - 1 else SLAB)], gat_recv.at[n, px])
            here = slab(c, px)
            push(buf.at[here], buf.at[here], swap_send.at[n], swap_recv.at[n], mate)

    def settle(buf, n):
        wait(buf.at[pl.ds(0, HALF)], swap_recv.at[n])
        wait(buf.at[pl.ds(0, HALF - TILE)], gat_send.at[n])
        wait(buf.at[pl.ds(0, HALF)], swap_send.at[n])

    spread(gat_t, 1)
    push(proto_hat, proto_mate, mate_send.at[0], mate_recv.at[0], mate)
    wait(first.at[pl.ds(0, NU - 1)], first_send)
    relay(gat_t, 1)
    settle(gat_t, 1)

    def exponentials(buf, out, temp):
        for k in range(ROWS // 256):
            at = slice(k * 256, (k + 1) * 256)
            product = lax.dot_general(
                proto_hat[...], buf[at, :], (((1,), (1,)), ((), ())), preferred_element_type=f32
            )
            out[:, at] = jnp.exp(product * (1.0 / temp))

    def folded(value):
        return jnp.sum(value.reshape(BLOCK // 8, 8, ROWS), axis=0)

    def flat(ref):
        return jnp.concatenate([ref[k : k + 1, :] for k in range(TALL)], axis=1)

    def put(dst, acc):
        for k in range(TALL):
            dst[k : k + 1, :] = jnp.sum(acc[:, k * LANES : (k + 1) * LANES], axis=0, keepdims=True)

    def sweep(scale):
        def body(i, acc):
            at = pl.ds(pl.multiple_of(i * BLOCK, BLOCK), BLOCK)
            e = e_t[at, :]
            weighed = e if scale is None else e * scale
            col = 1.0 / jnp.sum(weighed, axis=1, keepdims=True)
            cols[at, :] = jnp.broadcast_to(col, (BLOCK, LANES))
            return acc + folded(e * col)

        return lax.fori_loop(0, PROTOS // BLOCK, body, jnp.zeros((8, ROWS), f32))

    def near_start(n):
        me = z * CORES + c

        def send(k, _):
            push(near_src.at[n], near.at[n, me], near_send.at[n], near_recv.at[n], near_peer(k))
            return 0

        lax.fori_loop(0, NU * CORES - 1, send, 0)
        near[n, me] = near_src[n]

    def near_end(n):
        for sem in (near_recv, near_send):
            wait(near.at[n, pl.ds(0, NU * CORES - 1)], sem.at[n])
        far_src[n] = jnp.sum(near[n], axis=0)

    def far_start(n):
        me = x * NU + y

        def send(k, _):
            push(far_src.at[n], far.at[n, me], far_send.at[n], far_recv.at[n], far_peer(k))
            return 0

        lax.fori_loop(0, NX * NU - 1, send, 0)
        far[n, me] = far_src[n]

    def far_end(n):
        for sem in (far_recv, far_send):
            wait(far.at[n, pl.ds(0, NX * NU - 1)], sem.at[n])
        return 1.0 / jnp.sum(far[n], axis=0)

    def row_of(inverse):
        part[...] = inverse
        return flat(part)

    def student_sum(i, acc):
        at = pl.ds(pl.multiple_of(i * BLOCK, BLOCK), BLOCK)
        return acc + folded(e_s[at, :])

    exponentials(gat_t, e_t, teacher_temp)
    put(near_src.at[0], sweep(None))
    near_start(0)
    spread(gat_s, 0, 0, NX * NU // 2)
    near_end(0)
    far_start(0)
    spread(gat_s, 0, NX * NU // 2)
    row_scale = row_of(far_end(0))

    put(near_src.at[1], sweep(row_scale))
    near_start(1)
    relay(gat_s, 0)
    near_end(1)
    far_start(1)
    settle(gat_s, 0)
    exponentials(gat_s, e_s, student_temp)
    put(near_src.at[3], lax.fori_loop(0, PROTOS // BLOCK, student_sum, jnp.zeros((8, ROWS), f32)))
    near_start(3)
    row_scale = row_of(far_end(1))

    put(near_src.at[2], sweep(row_scale))
    near_start(2)
    near_end(3)
    far_start(3)
    near_end(2)
    far_start(2)
    student_scale = row_of(far_end(3) * (1.0 / student_temp))

    def scale_block(i, _):
        at = pl.ds(pl.multiple_of(i * BLOCK, BLOCK), BLOCK)
        e_s[at, :] = e_s[at, :] * student_scale
        e_t[at, :] = e_t[at, :] * cols[at, 0:1]
        return 0

    lax.fori_loop(0, PROTOS // BLOCK, scale_block, 0)
    part[...] = far_end(2) * (1.0 / student_temp)

    def gradients(core):
        rows = [part[pl.ds(core * (TALL // CORES) + k, 1), :] for k in range(TALL // CORES)]
        scale = jnp.concatenate(rows, axis=1)
        lanes = pl.ds(pl.multiple_of(core * HALF, HALF), HALF)

        def body(i, _):
            at = pl.ds(pl.multiple_of(i * BLOCK, BLOCK), BLOCK)
            grad[core, at, :] = (e_s[at, lanes] - e_t[at, lanes] * scale).astype(bf16)
            return 0

        lax.fori_loop(0, PROTOS // BLOCK, body, 0)

    gradients(oc)
    push(grad.at[oc], grad_mate, mate_send.at[1], mate_recv.at[1], mate)
    gradients(c)

    def row_product(left, px, right):
        at = pl.ds(pl.multiple_of(px * SLAB, SLAB), SLAB)
        return lax.dot_general(left[:, at], right[...], (((0,), (0,)), ((), ())), preferred_element_type=f32)

    for px in range(NX):
        own[px] = row_product(grad.at[c], px, proto_hat)
    wait(proto_mate, mate_recv.at[0])
    wait(grad_mate, mate_recv.at[1])
    for k in range(NX):
        px = turned(x, k, NX)
        total = own[px] + row_product(grad_mate, px, proto_mate)
        xbuf[px] = total[:, :CUT]
        ubuf[px] = total[:, CUT:].reshape(NU, TILE, D - CUT)
        if k < NX - 1:
            push(xbuf.at[px], xslots.at[x], big_send.at[0], big_recv.at[0], device(px, u, v))

    def send_u(k, _):
        pu = turned(u, k, NU)
        push(ubuf.at[:, pu], uslots.at[u], big_send.at[1], big_recv.at[1], device(x, pu, v))
        return 0

    lax.fori_loop(0, NU - 1, send_u, 0)
    xslots[x] = xbuf[x]
    uslots[u] = ubuf[:, u]

    def proto_block(i):
        at = slice(i * 256, (i + 1) * 256)
        step = jnp.dot(grad[0, at, :], gat_s[:HALF, :], preferred_element_type=f32)
        step += jnp.dot(grad[1, at, :], gat_s[HALF:, :], preferred_element_type=f32)
        inv = proto_inv[at, 0:1]
        unit = proto_ref[at, :].astype(f32) * inv
        pgrad_ref[at, :] = (step - unit * jnp.sum(unit * step, axis=1, keepdims=True)) * inv

    for i in range(PROTOS // 256):
        proto_block(i)

    for sem in (big_recv, big_send):
        wait(xslots.at[pl.ds(0, NX - 1)], sem.at[0])
    xsum[...] = jnp.sum(xslots[...], axis=0)

    def send_xu(k, _):
        pu = turned(u, k, NU)
        src = xsum.at[pl.ds(pl.multiple_of(pu * TILE, TILE), TILE)]
        push(src, xuslots.at[u], end_send.at[0], end_recv.at[0], device(x, pu, v))
        return 0

    lax.fori_loop(0, NU - 1, send_xu, 0)
    xuslots[u] = xsum[pl.ds(pl.multiple_of(u * TILE, TILE), TILE), :]

    for sem in (big_recv, big_send):
        wait(uslots.at[pl.ds(0, NU - 1)], sem.at[1])
    usum = jnp.sum(uslots[...], axis=0)
    for px in range(NX):
        for pv in range(NU):
            uvsrc[px * NU + pv] = usum[px, pv * OWN : (pv + 1) * OWN, :]

    def send_uv(k, _):
        px, pv = plane(k, v)
        push(uvsrc.at[px * NU + pv], uvslots.at[x * NU + v], end_send.at[1], end_recv.at[1], device(px, u, pv))
        return 0

    lax.fori_loop(0, NX * NU - 1, send_uv, 0)
    uvslots[x * NU + v] = uvsrc[x * NU + v]

    for sem in (end_recv, end_send):
        wait(xuslots.at[pl.ds(0, NU - 1)], sem.at[0])
    xusum = jnp.sum(xuslots[...], axis=0)
    for pv in range(NU):
        xvsrc[pv] = xusum[pv * OWN : (pv + 1) * OWN, :]

    def send_xv(k, _):
        pv = turned(v, k, NU)
        push(xvsrc.at[pv], xvslots.at[v], end_send.at[2], end_recv.at[2], device(x, u, pv))
        return 0

    lax.fori_loop(0, NU - 1, send_xv, 0)
    xvslots[v] = xvsrc[v]

    for sem in (end_recv, end_send):
        wait(uvslots.at[pl.ds(0, NX * NU - 1)], sem.at[1])
    right = jnp.sum(uvslots[...], axis=0)
    for sem in (end_recv, end_send):
        wait(xvslots.at[pl.ds(0, NU - 1)], sem.at[2])
    left = jnp.sum(xvslots[...], axis=0)
    wait(proto_mate, mate_send.at[0])
    wait(grad_mate, mate_send.at[1])

    step = jnp.concatenate([left, right], axis=1)
    sgrad_ref[...] = (step - s_unit * jnp.sum(s_unit * step, axis=1, keepdims=True)) * s_inv


def on_device(student, teacher, protos):
    vmem = pl.BlockSpec(memory_space=pltpu.VMEM)
    dma = pltpu.SemaphoreType.DMA
    return pl.pallas_call(
        kernel,
        out_shape=(
            jax.ShapeDtypeStruct((OWN, D), f32),
            jax.ShapeDtypeStruct((PROTOS, D), f32),
        ),
        in_specs=[pl.BlockSpec(memory_space=pltpu.HBM)] * 3,
        out_specs=(vmem, vmem),
        scratch_shapes=[
            pltpu.VMEM((OWN, D), bf16),
            pltpu.VMEM((OWN, D), bf16),
            pltpu.VMEM((PROTOS, D), bf16),
            pltpu.VMEM((NU, 2 * OWN, D), f32),
            pltpu.VMEM((2, TILE, D), f32),
            pltpu.VMEM((ROWS, D), bf16),
            pltpu.VMEM((ROWS, D), bf16),
            pltpu.VMEM((PROTOS, D), bf16),
            pltpu.VMEM((PROTOS, LANES), f32),
            pltpu.VMEM((PROTOS, ROWS), f32),
            pltpu.VMEM((PROTOS, ROWS), f32),
            pltpu.VMEM((PROTOS, LANES), f32),
            pltpu.VMEM((CORES, PROTOS, HALF), bf16),
            pltpu.VMEM((SUMS, TALL, LANES), f32),
            pltpu.VMEM((SUMS, NU * CORES, TALL, LANES), f32),
            pltpu.VMEM((SUMS, TALL, LANES), f32),
            pltpu.VMEM((SUMS, NX * NU, TALL, LANES), f32),
            pltpu.VMEM((TALL, LANES), f32),
            pltpu.VMEM((NX, SLAB, D), f32),
            pltpu.VMEM((PROTOS, D), bf16),
            pltpu.VMEM((PROTOS, HALF), bf16),
            pltpu.VMEM((NX, SLAB, CUT), f32),
            pltpu.VMEM((NX, NU, TILE, D - CUT), f32),
            pltpu.VMEM((NX, SLAB, CUT), f32),
            pltpu.VMEM((NU, NX, TILE, D - CUT), f32),
            pltpu.VMEM((SLAB, CUT), f32),
            pltpu.VMEM((NU, TILE, CUT), f32),
            pltpu.VMEM((NU, OWN, CUT), f32),
            pltpu.VMEM((NU, OWN, CUT), f32),
            pltpu.VMEM((NX * NU, OWN, D - CUT), f32),
            pltpu.VMEM((NX * NU, OWN, D - CUT), f32),
            dma((3,)),
            dma,
            dma,
            dma((2,)),
            dma((2, NX)),
            dma((2,)),
            dma((2,)),
            dma((SUMS,)),
            dma((SUMS,)),
            dma((SUMS,)),
            dma((SUMS,)),
            dma((2,)),
            dma((2,)),
            dma((2,)),
            dma((2,)),
            dma((3,)),
            dma((3,)),
        ],
        compiler_params=pltpu.CompilerParams(
            collective_id=0, has_side_effects=True, vmem_limit_bytes=48 << 20
        ),
        name="prototype_head",
    )(*(pltpu.with_memory_space_constraint(a, pltpu.HBM) for a in (student, teacher, protos)))


def solution(mesh):
    torus = Mesh(mesh.devices.reshape(NX, NU, NU, CORES), AXES)
    return jax.shard_map(
        on_device,
        mesh=torus,
        in_specs=(P(AXES, None),) * 3,
        out_specs=(P(AXES, None), P(AXES, None)),
        check_vma=False,
    )
```

```python
import functools

import jax
import jax.numpy as jnp
from jax import lax
from jax.experimental import pallas as pl
from jax.experimental.pallas import tpu as pltpu
from jax.sharding import Mesh
from jax.sharding import PartitionSpec as P

MESH = pl.DeviceIdType.MESH
AXES = ("wide_0", "wide_1", "narrow_0", "narrow_1")
SUMS = 4
NX, NU, CORES = 4, 8, 2
D = 512
OWN = 2
ROWS = NX * NU * NU * CORES * OWN
HALF = ROWS // CORES
SLAB = HALF // NX
TILE = NU * OWN
PROTOS = 512
BLOCK = 64
LANES = 128
TALL = ROWS // LANES
CUT = D // 2

epsilon = 1e-06
teacher_temp = 0.07
student_temp = 0.1

f32 = jnp.float32
bf16 = jnp.bfloat16


def inverse_norm(wide):
    return lax.rsqrt(jnp.sum(wide * wide, axis=1, keepdims=True) + epsilon)


def kernel(
    student_hbm,
    teacher_hbm,
    proto_hbm,
    sgrad_ref,
    pgrad_ref,
    student_ref,
    teacher_ref,
    proto_ref,
    first,
    stage,
    gat_t,
    gat_s,
    proto_hat,
    proto_inv,
    e_t,
    e_s,
    cols,
    grad,
    near_src,
    near,
    far_src,
    far,
    part,
    own,
    proto_mate,
    grad_mate,
    xbuf,
    ubuf,
    xslots,
    uslots,
    xsum,
    xuslots,
    xvsrc,
    xvslots,
    uvsrc,
    uvslots,
    load,
    first_send,
    first_recv,
    gat_send,
    gat_recv,
    swap_send,
    swap_recv,
    near_send,
    near_recv,
    far_send,
    far_recv,
    mate_send,
    mate_recv,
    big_send,
    big_recv,
    end_send,
    end_recv,
):
    x, y, z, c = (lax.axis_index(a) for a in AXES)
    u = z + c * (y - z)
    v = y + c * (z - y)
    oc = 1 - c

    def device(px, pu, pv):
        return (px, pv + c * (pu - pv), pu + c * (pv - pu), c)

    mate = (x, y, z, oc)

    def turned(at, k, n):
        return lax.rem(at + n // 2 + (1 - 2 * lax.rem(k, 2)) * ((k + 1) // 2), n)

    def near_peer(k):
        return (x, y, turned(z, k // CORES, NU), lax.rem(c + 1 + lax.rem(k, CORES), CORES))

    def far_peer(k):
        return (turned(x, lax.rem(k, NX), NX), turned(y, k // NX, NU), z, c)

    def plane(k, at):
        return turned(x, lax.rem(k, NX), NX), turned(at, k // NX, NU)

    def wait(ref, sem):
        pltpu.make_async_copy(ref, ref, sem).wait()

    def push(src, dst, send, recv, target):
        pltpu.make_async_remote_copy(
            src_ref=src, dst_ref=dst, send_sem=send, recv_sem=recv, device_id=target, device_id_type=MESH
        ).start()

    inputs = [
        pltpu.make_async_copy(src, dst, load.at[i])
        for i, (src, dst) in enumerate(
            ((student_hbm, student_ref), (teacher_hbm, teacher_ref), (proto_hbm, proto_ref))
        )
    ]
    for copy in inputs:
        copy.start()

    barrier = pltpu.get_barrier_semaphore()

    def greet(target):
        pl.semaphore_signal(barrier, inc=1, device_id=target, device_id_type=MESH)
        return 0

    def greet_side(k, _):
        return greet((turned(x, lax.rem(k, NX - 1), NX), y, turned(z, k // (NX - 1), NU), c))

    lax.fori_loop(0, NX * NU - 1, lambda k, _: greet(far_peer(k)), 0)
    lax.fori_loop(0, (NX - 1) * (NU - 1), greet_side, 0)
    lax.fori_loop(0, NU * CORES - 1, lambda k, _: greet(near_peer(k)), 0)

    for copy in inputs[:2]:
        copy.wait()
    wide_s = student_ref[...].astype(f32)
    wide_t = teacher_ref[...].astype(f32)
    s_inv = inverse_norm(wide_s)
    s_unit = wide_s * s_inv
    t_unit = wide_t * inverse_norm(wide_t)
    first[v, 0:OWN, :] = s_unit
    first[v, OWN : 2 * OWN, :] = t_unit

    def norm_block(i, _):
        at = pl.ds(pl.multiple_of(i * BLOCK, BLOCK), BLOCK)
        wide = proto_ref[at, :].astype(f32)
        inv = inverse_norm(wide)
        proto_inv[at, :] = jnp.broadcast_to(inv, (BLOCK, LANES))
        proto_hat[at, :] = (wide * inv).astype(bf16)
        return 0

    pl.semaphore_wait(barrier, NU * CORES - 1 + NX * NU - 1 + (NX - 1) * (NU - 1))

    def send_first(k, _):
        push(first.at[v], first.at[v], first_send, first_recv, device(x, u, turned(v, k, NU)))
        return 0

    lax.fori_loop(0, NU - 1, send_first, 0)
    inputs[2].wait()
    lax.fori_loop(0, PROTOS // BLOCK, norm_block, 0)
    wait(first.at[pl.ds(0, NU - 1)], first_recv)
    for i in range(NU):
        stage[0, OWN * i : OWN * (i + 1), :] = first[i, 0:OWN, :]
        stage[1, OWN * i : OWN * (i + 1), :] = first[i, OWN : 2 * OWN, :]
    for h in range(2):
        at = slice(h * CUT, (h + 1) * CUT)
        gat_s[h, c, x, u] = stage[0, :, at].astype(bf16)
        gat_t[h, c, x, u] = stage[1, :, at].astype(bf16)

    def open_step(buf, n):
        def send_hi(k, _):
            block = buf.at[1, c, x, u]
            push(block, block, gat_send.at[n, 1], gat_recv.at[n, 1], device(turned(x, k, NX), u, v))
            return 0

        def send_lo(k, _):
            block = buf.at[0, c, x, u]
            push(block, block, gat_send.at[n, 0], gat_recv.at[n, 0], device(x, turned(u, k, NU), v))
            return 0

        lax.fori_loop(0, NU - 1, send_lo, 0)
        lax.fori_loop(0, NX - 1, send_hi, 0)

    def spread_step(buf, n):
        def send_hi(k, _):
            block = buf.at[1, c, :, u]
            push(block, block, gat_send.at[n, 2], gat_recv.at[n, 2], device(x, turned(u, k, NU), v))
            return 0

        def send_lo(k, _):
            block = buf.at[0, c, x]
            push(block, block, gat_send.at[n, 3], gat_recv.at[n, 3 + x], device(turned(x, k, NX), u, v))
            return 0

        wait(buf.at[0, 0, 0, pl.ds(0, NX - 1)], gat_recv.at[n, 1])
        lax.fori_loop(0, NU - 1, send_hi, 0)
        wait(buf.at[0, 0, 0, pl.ds(0, NU - 1)], gat_recv.at[n, 0])
        lax.fori_loop(0, NX - 1, send_lo, 0)

    def relay(buf, n):
        for k in range(NX):
            px = turned(x, NX - 1 if k == 0 else k - 1, NX)
            if k > 0:
                wait(buf.at[0, 0, 0], gat_recv.at[n, 3 + px])
            push(buf.at[0, c, px], buf.at[0, c, px], swap_send.at[n], swap_recv.at[n], mate)
        wait(buf.at[0, 0, :, pl.ds(0, NU - 1)], gat_recv.at[n, 2])
        push(buf.at[1, c], buf.at[1, c], swap_send.at[n], swap_recv.at[n], mate)

    def settle(buf, n):
        wait(buf.at[:, 0], swap_recv.at[n])
        wait(buf.at[0, 0, 0, pl.ds(0, NU - 1)], gat_send.at[n, 0])
        wait(buf.at[0, 0, 0, pl.ds(0, NX - 1)], gat_send.at[n, 1])
        wait(buf.at[0, 0, :, pl.ds(0, NU - 1)], gat_send.at[n, 2])
        wait(buf.at[0, 0, pl.ds(0, NX - 1)], gat_send.at[n, 3])
        wait(buf.at[:, 0], swap_send.at[n])

    open_step(gat_t, 1)
    push(proto_hat, proto_mate, mate_send.at[0], mate_recv.at[0], mate)
    wait(first.at[pl.ds(0, NU - 1)], first_send)
    spread_step(gat_t, 1)
    relay(gat_t, 1)
    settle(gat_t, 1)

    def exponentials(buf, out, temp):
        for k in range(ROWS // 256):
            at = slice(k * 256, (k + 1) * 256)
            px = k % 2 * 2
            product = sum(
                lax.dot_general(
                    proto_hat[:, h * CUT : (h + 1) * CUT],
                    buf[h, k // 2, px : px + 2].reshape(256, CUT),
                    (((1,), (1,)), ((), ())),
                    preferred_element_type=f32,
                )
                for h in range(2)
            )
            out[:, at] = jnp.exp(product * (1.0 / temp))

    def folded(value):
        return jnp.sum(value.reshape(BLOCK // 8, 8, ROWS), axis=0)

    def flat(ref):
        return jnp.concatenate([ref[k : k + 1, :] for k in range(TALL)], axis=1)

    def put(dst, acc):
        for k in range(TALL):
            dst[k : k + 1, :] = jnp.sum(acc[:, k * LANES : (k + 1) * LANES], axis=0, keepdims=True)

    def sweep(scale):
        def body(i, acc):
            at = pl.ds(pl.multiple_of(i * BLOCK, BLOCK), BLOCK)
            e = e_t[at, :]
            weighed = e if scale is None else e * scale
            col = 1.0 / jnp.sum(weighed, axis=1, keepdims=True)
            cols[at, :] = jnp.broadcast_to(col, (BLOCK, LANES))
            return acc + folded(e * col)

        return lax.fori_loop(0, PROTOS // BLOCK, body, jnp.zeros((8, ROWS), f32))

    def near_start(n):
        me = z * CORES + c

        def send(k, _):
            push(near_src.at[n], near.at[n, me], near_send.at[n], near_recv.at[n], near_peer(k))
            return 0

        lax.fori_loop(0, NU * CORES - 1, send, 0)
        near[n, me] = near_src[n]

    def near_end(n):
        for sem in (near_recv, near_send):
            wait(near.at[n, pl.ds(0, NU * CORES - 1)], sem.at[n])
        far_src[n] = jnp.sum(near[n], axis=0)

    def far_start(n):
        me = x * NU + y

        def send(k, _):
            push(far_src.at[n], far.at[n, me], far_send.at[n], far_recv.at[n], far_peer(k))
            return 0

        lax.fori_loop(0, NX * NU - 1, send, 0)
        far[n, me] = far_src[n]

    def far_end(n):
        for sem in (far_recv, far_send):
            wait(far.at[n, pl.ds(0, NX * NU - 1)], sem.at[n])
        return 1.0 / jnp.sum(far[n], axis=0)

    def row_of(inverse):
        part[...] = inverse
        return flat(part)

    def student_sum(i, acc):
        at = pl.ds(pl.multiple_of(i * BLOCK, BLOCK), BLOCK)
        return acc + folded(e_s[at, :])

    exponentials(gat_t, e_t, teacher_temp)
    put(near_src.at[0], sweep(None))
    near_start(0)
    open_step(gat_s, 0)
    near_end(0)
    far_start(0)
    spread_step(gat_s, 0)
    row_scale = row_of(far_end(0))
    relay(gat_s, 0)

    put(near_src.at[1], sweep(row_scale))
    near_start(1)
    settle(gat_s, 0)
    exponentials(gat_s, e_s, student_temp)
    put(near_src.at[3], lax.fori_loop(0, PROTOS // BLOCK, student_sum, jnp.zeros((8, ROWS), f32)))
    near_start(3)
    near_end(1)
    far_start(1)
    near_end(3)
    far_start(3)
    row_scale = row_of(far_end(1))

    put(near_src.at[2], sweep(row_scale))
    near_start(2)
    student_scale = row_of(far_end(3) * (1.0 / student_temp))

    def scale_block(i, _):
        at = pl.ds(pl.multiple_of(i * BLOCK, BLOCK), BLOCK)
        e_s[at, :] = e_s[at, :] * student_scale
        e_t[at, :] = e_t[at, :] * cols[at, 0:1]
        return 0

    lax.fori_loop(0, PROTOS // BLOCK, scale_block, 0)
    near_end(2)
    far_start(2)
    part[...] = far_end(2) * (1.0 / student_temp)

    def gradients(core):
        rows = [part[pl.ds(core * (TALL // CORES) + k, 1), :] for k in range(TALL // CORES)]
        scale = jnp.concatenate(rows, axis=1)
        lanes = pl.ds(pl.multiple_of(core * HALF, HALF), HALF)

        def body(i, _):
            at = pl.ds(pl.multiple_of(i * BLOCK, BLOCK), BLOCK)
            grad[core, at, :] = (e_s[at, lanes] - e_t[at, lanes] * scale).astype(bf16)
            return 0

        lax.fori_loop(0, PROTOS // BLOCK, body, 0)

    gradients(oc)
    push(grad.at[oc], grad_mate, mate_send.at[1], mate_recv.at[1], mate)
    gradients(c)

    def row_product(left, px, right):
        at = pl.ds(pl.multiple_of(px * SLAB, SLAB), SLAB)
        return lax.dot_general(left[:, at], right[...], (((0,), (0,)), ((), ())), preferred_element_type=f32)

    for px in range(NX):
        own[px] = row_product(grad.at[c], px, proto_hat)
    wait(proto_mate, mate_recv.at[0])
    wait(grad_mate, mate_recv.at[1])
    for k in range(NX):
        px = turned(x, k, NX)
        total = own[px] + row_product(grad_mate, px, proto_mate)
        xbuf[px] = total[:, :CUT]
        ubuf[px] = total[:, CUT:].reshape(NU, TILE, D - CUT)
        if k < NX - 1:
            push(xbuf.at[px], xslots.at[x], big_send.at[0], big_recv.at[0], device(px, u, v))

    def send_u(k, _):
        pu = turned(u, k, NU)
        push(ubuf.at[:, pu], uslots.at[u], big_send.at[1], big_recv.at[1], device(x, pu, v))
        return 0

    lax.fori_loop(0, NU - 1, send_u, 0)
    xslots[x] = xbuf[x]
    uslots[u] = ubuf[:, u]

    def proto_block(i):
        at = slice(i * 256, (i + 1) * 256)
        halves = [
            sum(
                jnp.dot(grad[core, at, :], gat_s[h, core].reshape(HALF, CUT), preferred_element_type=f32)
                for core in range(CORES)
            )
            for h in range(2)
        ]
        step = jnp.concatenate(halves, axis=1)
        inv = proto_inv[at, 0:1]
        unit = proto_ref[at, :].astype(f32) * inv
        pgrad_ref[at, :] = (step - unit * jnp.sum(unit * step, axis=1, keepdims=True)) * inv

    for i in range(PROTOS // 256):
        proto_block(i)

    for sem in (big_recv, big_send):
        wait(xslots.at[pl.ds(0, NX - 1)], sem.at[0])
    xsum[...] = jnp.sum(xslots[...], axis=0)

    def send_xu(k, _):
        pu = turned(u, k, NU)
        src = xsum.at[pl.ds(pl.multiple_of(pu * TILE, TILE), TILE)]
        push(src, xuslots.at[u], end_send.at[0], end_recv.at[0], device(x, pu, v))
        return 0

    lax.fori_loop(0, NU - 1, send_xu, 0)
    xuslots[u] = xsum[pl.ds(pl.multiple_of(u * TILE, TILE), TILE), :]

    for sem in (big_recv, big_send):
        wait(uslots.at[pl.ds(0, NU - 1)], sem.at[1])
    usum = jnp.sum(uslots[...], axis=0)
    for px in range(NX):
        for pv in range(NU):
            uvsrc[px * NU + pv] = usum[px, pv * OWN : (pv + 1) * OWN, :]

    def send_uv(k, _):
        px, pv = plane(k, v)
        push(uvsrc.at[px * NU + pv], uvslots.at[x * NU + v], end_send.at[1], end_recv.at[1], device(px, u, pv))
        return 0

    lax.fori_loop(0, NX * NU - 1, send_uv, 0)
    uvslots[x * NU + v] = uvsrc[x * NU + v]

    for sem in (end_recv, end_send):
        wait(xuslots.at[pl.ds(0, NU - 1)], sem.at[0])
    xusum = jnp.sum(xuslots[...], axis=0)
    for pv in range(NU):
        xvsrc[pv] = xusum[pv * OWN : (pv + 1) * OWN, :]

    def send_xv(k, _):
        pv = turned(v, k, NU)
        push(xvsrc.at[pv], xvslots.at[v], end_send.at[2], end_recv.at[2], device(x, u, pv))
        return 0

    lax.fori_loop(0, NU - 1, send_xv, 0)
    xvslots[v] = xvsrc[v]

    for sem in (end_recv, end_send):
        wait(uvslots.at[pl.ds(0, NX * NU - 1)], sem.at[1])
    right = jnp.sum(uvslots[...], axis=0)
    for sem in (end_recv, end_send):
        wait(xvslots.at[pl.ds(0, NU - 1)], sem.at[2])
    left = jnp.sum(xvslots[...], axis=0)
    wait(proto_mate, mate_send.at[0])
    wait(grad_mate, mate_send.at[1])

    step = jnp.concatenate([left, right], axis=1)
    sgrad_ref[...] = (step - s_unit * jnp.sum(s_unit * step, axis=1, keepdims=True)) * s_inv


def on_device(student, teacher, protos):
    vmem = pl.BlockSpec(memory_space=pltpu.VMEM)
    dma = pltpu.SemaphoreType.DMA
    return pl.pallas_call(
        kernel,
        out_shape=(
            jax.ShapeDtypeStruct((OWN, D), f32),
            jax.ShapeDtypeStruct((PROTOS, D), f32),
        ),
        in_specs=[pl.BlockSpec(memory_space=pltpu.HBM)] * 3,
        out_specs=(vmem, vmem),
        scratch_shapes=[
            pltpu.VMEM((OWN, D), bf16),
            pltpu.VMEM((OWN, D), bf16),
            pltpu.VMEM((PROTOS, D), bf16),
            pltpu.VMEM((NU, 2 * OWN, D), f32),
            pltpu.VMEM((2, TILE, D), f32),
            pltpu.VMEM((2, CORES, NX, NU, TILE, CUT), bf16),
            pltpu.VMEM((2, CORES, NX, NU, TILE, CUT), bf16),
            pltpu.VMEM((PROTOS, D), bf16),
            pltpu.VMEM((PROTOS, LANES), f32),
            pltpu.VMEM((PROTOS, ROWS), f32),
            pltpu.VMEM((PROTOS, ROWS), f32),
            pltpu.VMEM((PROTOS, LANES), f32),
            pltpu.VMEM((CORES, PROTOS, HALF), bf16),
            pltpu.VMEM((SUMS, TALL, LANES), f32),
            pltpu.VMEM((SUMS, NU * CORES, TALL, LANES), f32),
            pltpu.VMEM((SUMS, TALL, LANES), f32),
            pltpu.VMEM((SUMS, NX * NU, TALL, LANES), f32),
            pltpu.VMEM((TALL, LANES), f32),
            pltpu.VMEM((NX, SLAB, D), f32),
            pltpu.VMEM((PROTOS, D), bf16),
            pltpu.VMEM((PROTOS, HALF), bf16),
            pltpu.VMEM((NX, SLAB, CUT), f32),
            pltpu.VMEM((NX, NU, TILE, D - CUT), f32),
            pltpu.VMEM((NX, SLAB, CUT), f32),
            pltpu.VMEM((NU, NX, TILE, D - CUT), f32),
            pltpu.VMEM((SLAB, CUT), f32),
            pltpu.VMEM((NU, TILE, CUT), f32),
            pltpu.VMEM((NU, OWN, CUT), f32),
            pltpu.VMEM((NU, OWN, CUT), f32),
            pltpu.VMEM((NX * NU, OWN, D - CUT), f32),
            pltpu.VMEM((NX * NU, OWN, D - CUT), f32),
            dma((3,)),
            dma,
            dma,
            dma((2, 4)),
            dma((2, 3 + NX)),
            dma((2,)),
            dma((2,)),
            dma((SUMS,)),
            dma((SUMS,)),
            dma((SUMS,)),
            dma((SUMS,)),
            dma((2,)),
            dma((2,)),
            dma((2,)),
            dma((2,)),
            dma((3,)),
            dma((3,)),
        ],
        compiler_params=pltpu.CompilerParams(
            collective_id=0, has_side_effects=True, vmem_limit_bytes=48 << 20
        ),
        name="prototype_head",
    )(*(pltpu.with_memory_space_constraint(a, pltpu.HBM) for a in (student, teacher, protos)))


def solution(mesh):
    torus = Mesh(mesh.devices.reshape(NX, NU, NU, CORES), AXES)
    return jax.shard_map(
        on_device,
        mesh=torus,
        in_specs=(P(AXES, None),) * 3,
        out_specs=(P(AXES, None), P(AXES, None)),
        check_vma=False,
    )
```

```python
import jax
import jax.numpy as jnp
from jax import lax
from jax.experimental import pallas as pl
from jax.experimental.pallas import tpu as pltpu
from jax.sharding import Mesh
from jax.sharding import PartitionSpec as P

MESH = pl.DeviceIdType.MESH
AXES = ("wide_0", "wide_1", "narrow_0", "narrow_1")
SUMS = 4
NX, NU, CORES = 4, 8, 2
D = 512
OWN = 2
ROWS = NX * NU * NU * CORES * OWN
HALF = ROWS // CORES
SLAB = HALF // NX
TILE = NU * OWN
PROTOS = 512
BLOCK = 64
LANES = 128
TALL = ROWS // LANES
CUT = D // 2

epsilon = 1e-06
teacher_temp = 0.07
student_temp = 0.1

f32 = jnp.float32
bf16 = jnp.bfloat16


def inverse_norm(wide):
    return lax.rsqrt(jnp.sum(wide * wide, axis=1, keepdims=True) + epsilon)


def kernel(
    student_hbm,
    teacher_hbm,
    proto_hbm,
    sgrad_ref,
    pgrad_ref,
    student_ref,
    teacher_ref,
    proto_ref,
    first,
    stage,
    gat_t,
    gat_s,
    proto_hat,
    proto_inv,
    e_t,
    e_s,
    cols,
    grad,
    near_src,
    near,
    far_src,
    far,
    part,
    proto_mate,
    grad_mate,
    xbuf,
    ubuf,
    xslots,
    uslots,
    xsum,
    xuslots,
    xvsrc,
    xvslots,
    uvsrc,
    uvslots,
    load,
    first_send,
    first_recv,
    gat_send,
    gat_recv,
    swap_send,
    swap_recv,
    near_send,
    near_recv,
    far_send,
    far_recv,
    mate_send,
    mate_recv,
    grad_recv,
    big_send,
    big_recv,
    end_send,
    end_recv,
):
    x, y, z, c = (lax.axis_index(a) for a in AXES)
    u = z + c * (y - z)
    v = y + c * (z - y)
    oc = 1 - c

    def device(px, pu, pv):
        return (px, pv + c * (pu - pv), pu + c * (pv - pu), c)

    mate = (x, y, z, oc)

    def turned(at, k, n):
        return lax.rem(at + n // 2 + (1 - 2 * lax.rem(k, 2)) * ((k + 1) // 2), n)

    def near_peer(k):
        return (x, y, turned(z, k // CORES, NU), lax.rem(c + 1 + lax.rem(k, CORES), CORES))

    def far_peer(k):
        return (turned(x, lax.rem(k, NX), NX), turned(y, k // NX, NU), z, c)

    def plane(k, at):
        return turned(x, lax.rem(k, NX), NX), turned(at, k // NX, NU)

    def wait(ref, sem):
        pltpu.make_async_copy(ref, ref, sem).wait()

    def push(src, dst, send, recv, target):
        pltpu.make_async_remote_copy(
            src_ref=src, dst_ref=dst, send_sem=send, recv_sem=recv, device_id=target, device_id_type=MESH
        ).start()

    inputs = [
        pltpu.make_async_copy(src, dst, load.at[i])
        for i, (src, dst) in enumerate(
            ((student_hbm, student_ref), (teacher_hbm, teacher_ref), (proto_hbm, proto_ref))
        )
    ]
    for copy in inputs:
        copy.start()

    barrier = pltpu.get_barrier_semaphore()

    def greet(target):
        pl.semaphore_signal(barrier, inc=1, device_id=target, device_id_type=MESH)
        return 0

    def greet_side(k, _):
        return greet((turned(x, lax.rem(k, NX - 1), NX), y, turned(z, k // (NX - 1), NU), c))

    lax.fori_loop(0, NX * NU - 1, lambda k, _: greet(far_peer(k)), 0)
    lax.fori_loop(0, (NX - 1) * (NU - 1), greet_side, 0)
    lax.fori_loop(0, NU * CORES - 1, lambda k, _: greet(near_peer(k)), 0)

    for copy in inputs[:2]:
        copy.wait()
    wide_s = student_ref[...].astype(f32)
    wide_t = teacher_ref[...].astype(f32)
    s_inv = inverse_norm(wide_s)
    s_unit = wide_s * s_inv
    t_unit = wide_t * inverse_norm(wide_t)
    first[v, 0:OWN, :] = s_unit
    first[v, OWN : 2 * OWN, :] = t_unit

    def norm_block(i, _):
        at = pl.ds(pl.multiple_of(i * BLOCK, BLOCK), BLOCK)
        wide = proto_ref[at, :].astype(f32)
        inv = inverse_norm(wide)
        proto_inv[at, :] = jnp.broadcast_to(inv, (BLOCK, LANES))
        proto_hat[at, :] = (wide * inv).astype(bf16)
        return 0

    pl.semaphore_wait(barrier, NU * CORES - 1 + NX * NU - 1 + (NX - 1) * (NU - 1))

    def send_first(k, _):
        push(first.at[v], first.at[v], first_send, first_recv, device(x, u, turned(v, k, NU)))
        return 0

    lax.fori_loop(0, NU - 1, send_first, 0)
    inputs[2].wait()
    lax.fori_loop(0, PROTOS // BLOCK, norm_block, 0)
    wait(first.at[pl.ds(0, NU - 1)], first_recv)
    for i in range(NU):
        stage[0, OWN * i : OWN * (i + 1), :] = first[i, 0:OWN, :]
        stage[1, OWN * i : OWN * (i + 1), :] = first[i, OWN : 2 * OWN, :]
    for h in range(2):
        at = slice(h * CUT, (h + 1) * CUT)
        gat_s[h, c, x, u] = stage[0, :, at].astype(bf16)
        gat_t[h, c, x, u] = stage[1, :, at].astype(bf16)

    def open_step(buf, n):
        def send_hi(k, _):
            block = buf.at[1, c, x, u]
            push(block, block, gat_send.at[n, 1], gat_recv.at[n, 1], device(turned(x, k, NX), u, v))
            return 0

        def send_lo(k, _):
            block = buf.at[0, c, x, u]
            push(block, block, gat_send.at[n, 0], gat_recv.at[n, 0], device(x, turned(u, k, NU), v))
            return 0

        lax.fori_loop(0, NU - 1, send_lo, 0)
        lax.fori_loop(0, NX - 1, send_hi, 0)

    def spread_step(buf, n):
        def send_hi(k, _):
            block = buf.at[1, c, :, u]
            push(block, block, gat_send.at[n, 2], gat_recv.at[n, 2], device(x, turned(u, k, NU), v))
            return 0

        def send_lo(k, _):
            block = buf.at[0, c, x]
            push(block, block, gat_send.at[n, 3], gat_recv.at[n, 3 + x], device(turned(x, k, NX), u, v))
            return 0

        wait(buf.at[0, 0, 0, pl.ds(0, NX - 1)], gat_recv.at[n, 1])
        lax.fori_loop(0, NU - 1, send_hi, 0)
        wait(buf.at[0, 0, 0, pl.ds(0, NU - 1)], gat_recv.at[n, 0])
        lax.fori_loop(0, NX - 1, send_lo, 0)

    def relay(buf, n):
        for k in range(NX):
            px = turned(x, NX - 1 if k == 0 else k - 1, NX)
            if k > 0:
                wait(buf.at[0, 0, 0], gat_recv.at[n, 3 + px])
            push(buf.at[0, c, px], buf.at[0, c, px], swap_send.at[n], swap_recv.at[n], mate)
        wait(buf.at[0, 0, :, pl.ds(0, NU - 1)], gat_recv.at[n, 2])
        push(buf.at[1, c], buf.at[1, c], swap_send.at[n], swap_recv.at[n], mate)

    def settle(buf, n):
        wait(buf.at[:, 0], swap_recv.at[n])
        wait(buf.at[0, 0, 0, pl.ds(0, NU - 1)], gat_send.at[n, 0])
        wait(buf.at[0, 0, 0, pl.ds(0, NX - 1)], gat_send.at[n, 1])
        wait(buf.at[0, 0, :, pl.ds(0, NU - 1)], gat_send.at[n, 2])
        wait(buf.at[0, 0, pl.ds(0, NX - 1)], gat_send.at[n, 3])
        wait(buf.at[:, 0], swap_send.at[n])

    open_step(gat_t, 1)
    push(proto_hat, proto_mate, mate_send.at[0], mate_recv, mate)
    wait(first.at[pl.ds(0, NU - 1)], first_send)
    spread_step(gat_t, 1)
    relay(gat_t, 1)
    settle(gat_t, 1)

    def exponentials(buf, out, temp):
        for k in range(ROWS // 256):
            at = slice(k * 256, (k + 1) * 256)
            px = k % 2 * 2
            product = sum(
                lax.dot_general(
                    proto_hat[:, h * CUT : (h + 1) * CUT],
                    buf[h, k // 2, px : px + 2].reshape(256, CUT),
                    (((1,), (1,)), ((), ())),
                    preferred_element_type=f32,
                )
                for h in range(2)
            )
            out[:, at] = jnp.exp(product * (1.0 / temp))

    def folded(value):
        return jnp.sum(value.reshape(BLOCK // 8, 8, ROWS), axis=0)

    def flat(ref):
        return jnp.concatenate([ref[k : k + 1, :] for k in range(TALL)], axis=1)

    def put(dst, acc):
        for k in range(TALL):
            dst[k : k + 1, :] = jnp.sum(acc[:, k * LANES : (k + 1) * LANES], axis=0, keepdims=True)

    def sweep(scale):
        def body(i, acc):
            at = pl.ds(pl.multiple_of(i * BLOCK, BLOCK), BLOCK)
            e = e_t[at, :]
            weighed = e if scale is None else e * scale
            col = 1.0 / jnp.sum(weighed, axis=1, keepdims=True)
            cols[at, :] = jnp.broadcast_to(col, (BLOCK, LANES))
            return acc + folded(e * col)

        return lax.fori_loop(0, PROTOS // BLOCK, body, jnp.zeros((8, ROWS), f32))

    def near_start(n):
        me = z * CORES + c

        def send(k, _):
            push(near_src.at[n], near.at[n, me], near_send.at[n], near_recv.at[n], near_peer(k))
            return 0

        lax.fori_loop(0, NU * CORES - 1, send, 0)
        near[n, me] = near_src[n]

    def near_end(n):
        for sem in (near_recv, near_send):
            wait(near.at[n, pl.ds(0, NU * CORES - 1)], sem.at[n])
        far_src[n] = jnp.sum(near[n], axis=0)

    def far_start(n):
        me = x * NU + y

        def send(k, _):
            push(far_src.at[n], far.at[n, me], far_send.at[n], far_recv.at[n], far_peer(k))
            return 0

        lax.fori_loop(0, NX * NU - 1, send, 0)
        far[n, me] = far_src[n]

    def far_end(n):
        for sem in (far_recv, far_send):
            wait(far.at[n, pl.ds(0, NX * NU - 1)], sem.at[n])
        return 1.0 / jnp.sum(far[n], axis=0)

    def row_of(inverse):
        part[...] = inverse
        return flat(part)

    def student_sum(i, acc):
        at = pl.ds(pl.multiple_of(i * BLOCK, BLOCK), BLOCK)
        return acc + folded(e_s[at, :])

    exponentials(gat_t, e_t, teacher_temp)
    put(near_src.at[0], sweep(None))
    near_start(0)
    open_step(gat_s, 0)
    near_end(0)
    far_start(0)
    spread_step(gat_s, 0)
    row_scale = row_of(far_end(0))

    put(near_src.at[1], sweep(row_scale))
    near_start(1)
    relay(gat_s, 0)
    near_end(1)
    far_start(1)
    settle(gat_s, 0)
    exponentials(gat_s, e_s, student_temp)
    put(near_src.at[3], lax.fori_loop(0, PROTOS // BLOCK, student_sum, jnp.zeros((8, ROWS), f32)))
    near_start(3)
    near_end(3)
    far_start(3)
    row_scale = row_of(far_end(1))

    put(near_src.at[2], sweep(row_scale))
    near_start(2)
    near_end(2)
    far_start(2)
    student_scale = row_of(far_end(3) * (1.0 / student_temp))

    def scale_block(i, _):
        at = pl.ds(pl.multiple_of(i * BLOCK, BLOCK), BLOCK)
        e_s[at, :] = e_s[at, :] * student_scale
        e_t[at, :] = e_t[at, :] * cols[at, 0:1]
        return 0

    lax.fori_loop(0, PROTOS // BLOCK, scale_block, 0)
    part[...] = far_end(2) * (1.0 / student_temp)

    def gradients(core, px):
        scale = part[pl.ds(core * NX + px, 1), :]

        def body(i, _):
            at = pl.ds(pl.multiple_of(i * 128, 128), 128)
            lanes = pl.ds(pl.multiple_of(core * HALF + px * SLAB, SLAB), SLAB)
            grad[core, px, at, :] = (e_s[at, lanes] - e_t[at, lanes] * scale).astype(bf16)
            return 0

        lax.fori_loop(0, PROTOS // 128, body, 0)

    def row_product(left, right):
        return lax.dot_general(left[...], right[...], (((0,), (0,)), ((), ())), preferred_element_type=f32)

    for k in range(NX):
        px = turned(x, k, NX)
        gradients(oc, px)
        push(grad.at[oc, px], grad_mate.at[px], mate_send.at[1], grad_recv.at[px], mate)
    wait(proto_mate, mate_recv)
    for k in range(NX):
        px = turned(x, k, NX)
        gradients(c, px)
        own = row_product(grad.at[c, px], proto_hat)
        wait(grad_mate.at[px], grad_recv.at[px])
        total = own + row_product(grad_mate.at[px], proto_mate)
        xbuf[px] = total[:, :CUT]
        ubuf[px] = total[:, CUT:].reshape(NU, TILE, D - CUT)
        if k < NX - 1:
            push(xbuf.at[px], xslots.at[x], big_send.at[0], big_recv.at[0], device(px, u, v))

        def send_u(j, _):
            pu = turned(u, j, NU)
            push(ubuf.at[px, pu], uslots.at[u, px], big_send.at[1], big_recv.at[1], device(x, pu, v))
            return 0

        lax.fori_loop(0, NU - 1, send_u, 0)
    xslots[x] = xbuf[x]
    uslots[u] = ubuf[:, u]

    def proto_block(i):
        at = slice(i * 256, (i + 1) * 256)
        halves = [0.0, 0.0]
        for core in range(CORES):
            for px in range(0, NX, 2):
                left = jnp.concatenate([grad[core, px, at, :], grad[core, px + 1, at, :]], axis=1)
                for h in range(2):
                    right = gat_s[h, core, px : px + 2].reshape(2 * SLAB, CUT)
                    halves[h] += jnp.dot(left, right, preferred_element_type=f32)
        step = jnp.concatenate(halves, axis=1)
        inv = proto_inv[at, 0:1]
        unit = proto_ref[at, :].astype(f32) * inv
        pgrad_ref[at, :] = (step - unit * jnp.sum(unit * step, axis=1, keepdims=True)) * inv

    for i in range(PROTOS // 256):
        proto_block(i)

    for sem in (big_recv, big_send):
        wait(xslots.at[pl.ds(0, NX - 1)], sem.at[0])
    xsum[...] = jnp.sum(xslots[...], axis=0)

    def send_xu(k, _):
        pu = turned(u, k, NU)
        src = xsum.at[pl.ds(pl.multiple_of(pu * TILE, TILE), TILE)]
        push(src, xuslots.at[u], end_send.at[0], end_recv.at[0], device(x, pu, v))
        return 0

    lax.fori_loop(0, NU - 1, send_xu, 0)
    xuslots[u] = xsum[pl.ds(pl.multiple_of(u * TILE, TILE), TILE), :]

    for sem in (big_recv, big_send):
        wait(uslots.at[pl.ds(0, NU - 1)], sem.at[1])
    usum = jnp.sum(uslots[...], axis=0)
    for px in range(NX):
        for pv in range(NU):
            uvsrc[px * NU + pv] = usum[px, pv * OWN : (pv + 1) * OWN, :]

    def send_uv(k, _):
        px, pv = plane(k, v)
        push(uvsrc.at[px * NU + pv], uvslots.at[x * NU + v], end_send.at[1], end_recv.at[1], device(px, u, pv))
        return 0

    lax.fori_loop(0, NX * NU - 1, send_uv, 0)
    uvslots[x * NU + v] = uvsrc[x * NU + v]

    for sem in (end_recv, end_send):
        wait(xuslots.at[pl.ds(0, NU - 1)], sem.at[0])
    xusum = jnp.sum(xuslots[...], axis=0)
    for pv in range(NU):
        xvsrc[pv] = xusum[pv * OWN : (pv + 1) * OWN, :]

    def send_xv(k, _):
        pv = turned(v, k, NU)
        push(xvsrc.at[pv], xvslots.at[v], end_send.at[2], end_recv.at[2], device(x, u, pv))
        return 0

    lax.fori_loop(0, NU - 1, send_xv, 0)
    xvslots[v] = xvsrc[v]

    for sem in (end_recv, end_send):
        wait(uvslots.at[pl.ds(0, NX * NU - 1)], sem.at[1])
    right = jnp.sum(uvslots[...], axis=0)
    for sem in (end_recv, end_send):
        wait(xvslots.at[pl.ds(0, NU - 1)], sem.at[2])
    left = jnp.sum(xvslots[...], axis=0)
    wait(proto_mate, mate_send.at[0])
    wait(grad_mate, mate_send.at[1])

    step = jnp.concatenate([left, right], axis=1)
    sgrad_ref[...] = (step - s_unit * jnp.sum(s_unit * step, axis=1, keepdims=True)) * s_inv


def on_device(student, teacher, protos):
    vmem = pl.BlockSpec(memory_space=pltpu.VMEM)
    dma = pltpu.SemaphoreType.DMA
    return pl.pallas_call(
        kernel,
        out_shape=(
            jax.ShapeDtypeStruct((OWN, D), f32),
            jax.ShapeDtypeStruct((PROTOS, D), f32),
        ),
        in_specs=[pl.BlockSpec(memory_space=pltpu.HBM)] * 3,
        out_specs=(vmem, vmem),
        scratch_shapes=[
            pltpu.VMEM((OWN, D), bf16),
            pltpu.VMEM((OWN, D), bf16),
            pltpu.VMEM((PROTOS, D), bf16),
            pltpu.VMEM((NU, 2 * OWN, D), f32),
            pltpu.VMEM((2, TILE, D), f32),
            pltpu.VMEM((2, CORES, NX, NU, TILE, CUT), bf16),
            pltpu.VMEM((2, CORES, NX, NU, TILE, CUT), bf16),
            pltpu.VMEM((PROTOS, D), bf16),
            pltpu.VMEM((PROTOS, LANES), f32),
            pltpu.VMEM((PROTOS, ROWS), f32),
            pltpu.VMEM((PROTOS, ROWS), f32),
            pltpu.VMEM((PROTOS, LANES), f32),
            pltpu.VMEM((CORES, NX, PROTOS, SLAB), bf16),
            pltpu.VMEM((SUMS, TALL, LANES), f32),
            pltpu.VMEM((SUMS, NU * CORES, TALL, LANES), f32),
            pltpu.VMEM((SUMS, TALL, LANES), f32),
            pltpu.VMEM((SUMS, NX * NU, TALL, LANES), f32),
            pltpu.VMEM((TALL, LANES), f32),
            pltpu.VMEM((PROTOS, D), bf16),
            pltpu.VMEM((NX, PROTOS, SLAB), bf16),
            pltpu.VMEM((NX, SLAB, CUT), f32),
            pltpu.VMEM((NX, NU, TILE, D - CUT), f32),
            pltpu.VMEM((NX, SLAB, CUT), f32),
            pltpu.VMEM((NU, NX, TILE, D - CUT), f32),
            pltpu.VMEM((SLAB, CUT), f32),
            pltpu.VMEM((NU, TILE, CUT), f32),
            pltpu.VMEM((NU, OWN, CUT), f32),
            pltpu.VMEM((NU, OWN, CUT), f32),
            pltpu.VMEM((NX * NU, OWN, D - CUT), f32),
            pltpu.VMEM((NX * NU, OWN, D - CUT), f32),
            dma((3,)),
            dma,
            dma,
            dma((2, 4)),
            dma((2, 3 + NX)),
            dma((2,)),
            dma((2,)),
            dma((SUMS,)),
            dma((SUMS,)),
            dma((SUMS,)),
            dma((SUMS,)),
            dma((2,)),
            dma,
            dma((NX,)),
            dma((2,)),
            dma((2,)),
            dma((3,)),
            dma((3,)),
        ],
        compiler_params=pltpu.CompilerParams(
            collective_id=0, has_side_effects=True, vmem_limit_bytes=48 << 20
        ),
        name="prototype_head",
    )(*(pltpu.with_memory_space_constraint(a, pltpu.HBM) for a in (student, teacher, protos)))


def solution(mesh):
    torus = Mesh(mesh.devices.reshape(NX, NU, NU, CORES), AXES)
    return jax.shard_map(
        on_device,
        mesh=torus,
        in_specs=(P(AXES, None),) * 3,
        out_specs=(P(AXES, None), P(AXES, None)),
        check_vma=False,
    )
```

```python
import jax
import jax.numpy as jnp
from jax import lax
from jax.experimental import pallas as pl
from jax.experimental.pallas import tpu as pltpu
from jax.sharding import Mesh
from jax.sharding import PartitionSpec as P

MESH = pl.DeviceIdType.MESH
AXES = ("wide_0", "wide_1", "narrow_0", "narrow_1")
SUMS = 4
NX, NU, CORES = 4, 8, 2
D = 512
OWN = 2
ROWS = NX * NU * NU * CORES * OWN
HALF = ROWS // CORES
SLAB = HALF // NX
TILE = NU * OWN
PROTOS = 512
BLOCK = 64
LANES = 128
TALL = ROWS // LANES
CUT = D // 2

epsilon = 1e-06
teacher_temp = 0.07
student_temp = 0.1

f32 = jnp.float32
bf16 = jnp.bfloat16


def inverse_norm(wide):
    return lax.rsqrt(jnp.sum(wide * wide, axis=1, keepdims=True) + epsilon)


def kernel(
    student_hbm,
    teacher_hbm,
    proto_hbm,
    sgrad_ref,
    pgrad_ref,
    student_ref,
    teacher_ref,
    proto_ref,
    first,
    stage,
    gat_t,
    gat_s,
    proto_hat,
    proto_inv,
    e_t,
    e_s,
    cols,
    grad,
    near_src,
    near,
    far_src,
    far,
    part,
    own,
    proto_mate,
    grad_mate,
    xbuf,
    ubuf,
    xslots,
    uslots,
    xsum,
    xuslots,
    xvsrc,
    xvslots,
    uvsrc,
    uvslots,
    load,
    first_send,
    first_recv,
    gat_send,
    gat_recv,
    swap_send,
    swap_recv,
    near_send,
    near_recv,
    far_send,
    far_recv,
    mate_send,
    mate_recv,
    big_send,
    big_recv,
    end_send,
    end_recv,
):
    x, y, z, c = (lax.axis_index(a) for a in AXES)
    u = z + c * (y - z)
    v = y + c * (z - y)
    oc = 1 - c

    def device(px, pu, pv):
        return (px, pv + c * (pu - pv), pu + c * (pv - pu), c)

    mate = (x, y, z, oc)

    def turned(at, k, n):
        return lax.rem(at + n // 2 + (1 - 2 * lax.rem(k, 2)) * ((k + 1) // 2), n)

    def near_peer(k):
        return (x, y, turned(z, k // CORES, NU), lax.rem(c + 1 + lax.rem(k, CORES), CORES))

    def far_peer(k):
        return (turned(x, lax.rem(k, NX), NX), turned(y, k // NX, NU), z, c)

    def plane(k, at):
        return turned(x, lax.rem(k, NX), NX), turned(at, k // NX, NU)

    def wait(ref, sem):
        pltpu.make_async_copy(ref, ref, sem).wait()

    def push(src, dst, send, recv, target):
        pltpu.make_async_remote_copy(
            src_ref=src, dst_ref=dst, send_sem=send, recv_sem=recv, device_id=target, device_id_type=MESH
        ).start()

    inputs = [
        pltpu.make_async_copy(src, dst, load.at[i])
        for i, (src, dst) in enumerate(
            ((student_hbm, student_ref), (teacher_hbm, teacher_ref), (proto_hbm, proto_ref))
        )
    ]
    for copy in inputs:
        copy.start()

    barrier = pltpu.get_barrier_semaphore()

    def greet(target):
        pl.semaphore_signal(barrier, inc=1, device_id=target, device_id_type=MESH)
        return 0

    def greet_side(k, _):
        return greet((turned(x, lax.rem(k, NX - 1), NX), y, turned(z, k // (NX - 1), NU), c))

    lax.fori_loop(0, NX * NU - 1, lambda k, _: greet(far_peer(k)), 0)
    lax.fori_loop(0, (NX - 1) * (NU - 1), greet_side, 0)
    lax.fori_loop(0, NU * CORES - 1, lambda k, _: greet(near_peer(k)), 0)

    for copy in inputs[:2]:
        copy.wait()
    wide_s = student_ref[...].astype(f32)
    wide_t = teacher_ref[...].astype(f32)
    s_inv = inverse_norm(wide_s)
    s_unit = wide_s * s_inv
    t_unit = wide_t * inverse_norm(wide_t)
    first[v, 0:OWN, :] = s_unit
    first[v, OWN : 2 * OWN, :] = t_unit

    def norm_block(i, _):
        at = pl.ds(pl.multiple_of(i * BLOCK, BLOCK), BLOCK)
        wide = proto_ref[at, :].astype(f32)
        inv = inverse_norm(wide)
        proto_inv[at, :] = jnp.broadcast_to(inv, (BLOCK, LANES))
        proto_hat[at, :] = (wide * inv).astype(bf16)
        return 0

    pl.semaphore_wait(barrier, NU * CORES - 1 + NX * NU - 1 + (NX - 1) * (NU - 1))

    def send_first(k, _):
        push(first.at[v], first.at[v], first_send, first_recv, device(x, u, turned(v, k, NU)))
        return 0

    lax.fori_loop(0, NU - 1, send_first, 0)
    inputs[2].wait()
    lax.fori_loop(0, PROTOS // BLOCK, norm_block, 0)
    wait(first.at[pl.ds(0, NU - 1)], first_recv)
    for i in range(NU):
        stage[0, OWN * i : OWN * (i + 1), :] = first[i, 0:OWN, :]
        stage[1, OWN * i : OWN * (i + 1), :] = first[i, OWN : 2 * OWN, :]
    for h in range(2):
        at = slice(h * CUT, (h + 1) * CUT)
        gat_s[h, c, x, u] = stage[0, :, at].astype(bf16)
        gat_t[h, c, x, u] = stage[1, :, at].astype(bf16)

    def open_step(buf, n):
        def send_hi(k, _):
            block = buf.at[1, c, x, u]
            push(block, block, gat_send.at[n, 1], gat_recv.at[n, 1], device(turned(x, k, NX), u, v))
            return 0

        def send_lo(k, _):
            block = buf.at[0, c, x, u]
            push(block, block, gat_send.at[n, 0], gat_recv.at[n, 0], device(x, turned(u, k, NU), v))
            return 0

        lax.fori_loop(0, NX - 1, send_hi, 0)
        lax.fori_loop(0, NU - 1, send_lo, 0)

    def spread_hi(buf, n):
        def send(k, _):
            block = buf.at[1, c, :, u]
            push(block, block, gat_send.at[n, 2], gat_recv.at[n, 2], device(x, turned(u, k, NU), v))
            return 0

        lax.fori_loop(0, NU - 1, send, 0)

    def spread_lo(buf, n):
        def send(k, _):
            block = buf.at[0, c, x]
            push(block, block, gat_send.at[n, 3], gat_recv.at[n, 3 + x], device(turned(x, k, NX), u, v))
            return 0

        lax.fori_loop(0, NX - 1, send, 0)

    def opened_hi(buf, n):
        wait(buf.at[0, 0, 0, pl.ds(0, NX - 1)], gat_recv.at[n, 1])

    def opened_lo(buf, n):
        wait(buf.at[0, 0, 0, pl.ds(0, NU - 1)], gat_recv.at[n, 0])

    def relay(buf, n):
        for k in range(NX):
            px = turned(x, NX - 1 if k == 0 else k - 1, NX)
            if k > 0:
                wait(buf.at[0, 0, 0], gat_recv.at[n, 3 + px])
            push(buf.at[0, c, px], buf.at[0, c, px], swap_send.at[n], swap_recv.at[n], mate)
        wait(buf.at[0, 0, :, pl.ds(0, NU - 1)], gat_recv.at[n, 2])
        push(buf.at[1, c], buf.at[1, c], swap_send.at[n], swap_recv.at[n], mate)

    def settle(buf, n):
        wait(buf.at[:, 0], swap_recv.at[n])
        wait(buf.at[0, 0, 0, pl.ds(0, NU - 1)], gat_send.at[n, 0])
        wait(buf.at[0, 0, 0, pl.ds(0, NX - 1)], gat_send.at[n, 1])
        wait(buf.at[0, 0, :, pl.ds(0, NU - 1)], gat_send.at[n, 2])
        wait(buf.at[0, 0, pl.ds(0, NX - 1)], gat_send.at[n, 3])
        wait(buf.at[:, 0], swap_send.at[n])

    open_step(gat_t, 1)
    push(proto_hat, proto_mate, mate_send.at[0], mate_recv.at[0], mate)
    wait(first.at[pl.ds(0, NU - 1)], first_send)
    opened_hi(gat_t, 1)
    spread_hi(gat_t, 1)
    opened_lo(gat_t, 1)
    spread_lo(gat_t, 1)
    open_step(gat_s, 0)
    relay(gat_t, 1)
    settle(gat_t, 1)

    def exponentials(buf, out, temp):
        for k in range(ROWS // 256):
            at = slice(k * 256, (k + 1) * 256)
            px = k % 2 * 2
            product = sum(
                lax.dot_general(
                    proto_hat[:, h * CUT : (h + 1) * CUT],
                    buf[h, k // 2, px : px + 2].reshape(256, CUT),
                    (((1,), (1,)), ((), ())),
                    preferred_element_type=f32,
                )
                for h in range(2)
            )
            out[:, at] = jnp.exp(product * (1.0 / temp))

    def folded(value):
        return jnp.sum(value.reshape(BLOCK // 8, 8, ROWS), axis=0)

    def flat(ref):
        return jnp.concatenate([ref[k : k + 1, :] for k in range(TALL)], axis=1)

    def put(dst, acc):
        for k in range(TALL):
            dst[k : k + 1, :] = jnp.sum(acc[:, k * LANES : (k + 1) * LANES], axis=0, keepdims=True)

    def sweep(scale):
        def body(i, acc):
            at = pl.ds(pl.multiple_of(i * BLOCK, BLOCK), BLOCK)
            e = e_t[at, :]
            weighed = e if scale is None else e * scale
            col = 1.0 / jnp.sum(weighed, axis=1, keepdims=True)
            cols[at, :] = jnp.broadcast_to(col, (BLOCK, LANES))
            return acc + folded(e * col)

        return lax.fori_loop(0, PROTOS // BLOCK, body, jnp.zeros((8, ROWS), f32))

    def near_start(n):
        me = z * CORES + c

        def send(k, _):
            push(near_src.at[n], near.at[n, me], near_send.at[n], near_recv.at[n], near_peer(k))
            return 0

        lax.fori_loop(0, NU * CORES - 1, send, 0)
        near[n, me] = near_src[n]

    def near_end(n):
        for sem in (near_recv, near_send):
            wait(near.at[n, pl.ds(0, NU * CORES - 1)], sem.at[n])
        far_src[n] = jnp.sum(near[n], axis=0)

    def far_start(n):
        me = x * NU + y

        def send(k, _):
            push(far_src.at[n], far.at[n, me], far_send.at[n], far_recv.at[n], far_peer(k))
            return 0

        lax.fori_loop(0, NX * NU - 1, send, 0)
        far[n, me] = far_src[n]

    def far_end(n):
        for sem in (far_recv, far_send):
            wait(far.at[n, pl.ds(0, NX * NU - 1)], sem.at[n])
        return 1.0 / jnp.sum(far[n], axis=0)

    def row_of(inverse):
        part[...] = inverse
        return flat(part)

    def student_sum(i, acc):
        at = pl.ds(pl.multiple_of(i * BLOCK, BLOCK), BLOCK)
        return acc + folded(e_s[at, :])

    exponentials(gat_t, e_t, teacher_temp)
    put(near_src.at[0], sweep(None))
    near_start(0)
    opened_hi(gat_s, 0)
    opened_lo(gat_s, 0)
    spread_lo(gat_s, 0)
    pl.when(c == 1)(lambda: spread_hi(gat_s, 0))
    near_end(0)
    far_start(0)
    pl.when(c == 0)(lambda: spread_hi(gat_s, 0))
    row_scale = row_of(far_end(0))
    relay(gat_s, 0)

    put(near_src.at[1], sweep(row_scale))
    near_start(1)
    settle(gat_s, 0)
    exponentials(gat_s, e_s, student_temp)
    put(near_src.at[3], lax.fori_loop(0, PROTOS // BLOCK, student_sum, jnp.zeros((8, ROWS), f32)))
    near_start(3)
    near_end(1)
    far_start(1)
    near_end(3)
    far_start(3)
    row_scale = row_of(far_end(1))

    put(near_src.at[2], sweep(row_scale))
    near_start(2)
    student_scale = row_of(far_end(3) * (1.0 / student_temp))

    def scale_block(i, _):
        at = pl.ds(pl.multiple_of(i * BLOCK, BLOCK), BLOCK)
        e_s[at, :] = e_s[at, :] * student_scale
        e_t[at, :] = e_t[at, :] * cols[at, 0:1]
        return 0

    lax.fori_loop(0, PROTOS // BLOCK, scale_block, 0)
    near_end(2)
    far_start(2)
    part[...] = far_end(2) * (1.0 / student_temp)

    def gradients(core):
        rows = [part[pl.ds(core * (TALL // CORES) + k, 1), :] for k in range(TALL // CORES)]
        scale = jnp.concatenate(rows, axis=1)
        lanes = pl.ds(pl.multiple_of(core * HALF, HALF), HALF)

        def body(i, _):
            at = pl.ds(pl.multiple_of(i * BLOCK, BLOCK), BLOCK)
            grad[core, at, :] = (e_s[at, lanes] - e_t[at, lanes] * scale).astype(bf16)
            return 0

        lax.fori_loop(0, PROTOS // BLOCK, body, 0)

    gradients(oc)
    push(grad.at[oc], grad_mate, mate_send.at[1], mate_recv.at[1], mate)
    gradients(c)

    def row_product(left, px, right):
        at = pl.ds(pl.multiple_of(px * SLAB, SLAB), SLAB)
        return lax.dot_general(left[:, at], right[...], (((0,), (0,)), ((), ())), preferred_element_type=f32)

    for px in range(NX):
        own[px] = row_product(grad.at[c], px, proto_hat)
    wait(proto_mate, mate_recv.at[0])
    wait(grad_mate, mate_recv.at[1])
    for k in range(NX):
        px = turned(x, k, NX)
        total = own[px] + row_product(grad_mate, px, proto_mate)
        xbuf[px] = total[:, :CUT]
        ubuf[px] = total[:, CUT:].reshape(NU, TILE, D - CUT)
        if k < NX - 1:
            push(xbuf.at[px], xslots.at[x], big_send.at[0], big_recv.at[0], device(px, u, v))

    def send_u(k, _):
        pu = turned(u, k, NU)
        push(ubuf.at[:, pu], uslots.at[u], big_send.at[1], big_recv.at[1], device(x, pu, v))
        return 0

    lax.fori_loop(0, NU - 1, send_u, 0)
    xslots[x] = xbuf[x]
    uslots[u] = ubuf[:, u]

    def proto_block(i):
        at = slice(i * 256, (i + 1) * 256)
        halves = [
            sum(
                jnp.dot(grad[core, at, :], gat_s[h, core].reshape(HALF, CUT), preferred_element_type=f32)
                for core in range(CORES)
            )
            for h in range(2)
        ]
        step = jnp.concatenate(halves, axis=1)
        inv = proto_inv[at, 0:1]
        unit = proto_ref[at, :].astype(f32) * inv
        pgrad_ref[at, :] = (step - unit * jnp.sum(unit * step, axis=1, keepdims=True)) * inv

    for i in range(PROTOS // 256):
        proto_block(i)

    for sem in (big_recv, big_send):
        wait(xslots.at[pl.ds(0, NX - 1)], sem.at[0])
    xsum[...] = jnp.sum(xslots[...], axis=0)

    def send_xu(k, _):
        pu = turned(u, k, NU)
        src = xsum.at[pl.ds(pl.multiple_of(pu * TILE, TILE), TILE)]
        push(src, xuslots.at[u], end_send.at[0], end_recv.at[0], device(x, pu, v))
        return 0

    lax.fori_loop(0, NU - 1, send_xu, 0)
    xuslots[u] = xsum[pl.ds(pl.multiple_of(u * TILE, TILE), TILE), :]

    for sem in (big_recv, big_send):
        wait(uslots.at[pl.ds(0, NU - 1)], sem.at[1])
    usum = jnp.sum(uslots[...], axis=0)
    for px in range(NX):
        for pv in range(NU):
            uvsrc[px * NU + pv] = usum[px, pv * OWN : (pv + 1) * OWN, :]

    def send_uv(k, _):
        px, pv = plane(k, v)
        push(uvsrc.at[px * NU + pv], uvslots.at[x * NU + v], end_send.at[1], end_recv.at[1], device(px, u, pv))
        return 0

    lax.fori_loop(0, NX * NU - 1, send_uv, 0)
    uvslots[x * NU + v] = uvsrc[x * NU + v]

    for sem in (end_recv, end_send):
        wait(xuslots.at[pl.ds(0, NU - 1)], sem.at[0])
    xusum = jnp.sum(xuslots[...], axis=0)
    for pv in range(NU):
        xvsrc[pv] = xusum[pv * OWN : (pv + 1) * OWN, :]

    def send_xv(k, _):
        pv = turned(v, k, NU)
        push(xvsrc.at[pv], xvslots.at[v], end_send.at[2], end_recv.at[2], device(x, u, pv))
        return 0

    lax.fori_loop(0, NU - 1, send_xv, 0)
    xvslots[v] = xvsrc[v]

    for sem in (end_recv, end_send):
        wait(uvslots.at[pl.ds(0, NX * NU - 1)], sem.at[1])
    right = jnp.sum(uvslots[...], axis=0)
    for sem in (end_recv, end_send):
        wait(xvslots.at[pl.ds(0, NU - 1)], sem.at[2])
    left = jnp.sum(xvslots[...], axis=0)
    wait(proto_mate, mate_send.at[0])
    wait(grad_mate, mate_send.at[1])

    step = jnp.concatenate([left, right], axis=1)
    sgrad_ref[...] = (step - s_unit * jnp.sum(s_unit * step, axis=1, keepdims=True)) * s_inv


def on_device(student, teacher, protos):
    vmem = pl.BlockSpec(memory_space=pltpu.VMEM)
    dma = pltpu.SemaphoreType.DMA
    return pl.pallas_call(
        kernel,
        out_shape=(
            jax.ShapeDtypeStruct((OWN, D), f32),
            jax.ShapeDtypeStruct((PROTOS, D), f32),
        ),
        in_specs=[pl.BlockSpec(memory_space=pltpu.HBM)] * 3,
        out_specs=(vmem, vmem),
        scratch_shapes=[
            pltpu.VMEM((OWN, D), bf16),
            pltpu.VMEM((OWN, D), bf16),
            pltpu.VMEM((PROTOS, D), bf16),
            pltpu.VMEM((NU, 2 * OWN, D), f32),
            pltpu.VMEM((2, TILE, D), f32),
            pltpu.VMEM((2, CORES, NX, NU, TILE, CUT), bf16),
            pltpu.VMEM((2, CORES, NX, NU, TILE, CUT), bf16),
            pltpu.VMEM((PROTOS, D), bf16),
            pltpu.VMEM((PROTOS, LANES), f32),
            pltpu.VMEM((PROTOS, ROWS), f32),
            pltpu.VMEM((PROTOS, ROWS), f32),
            pltpu.VMEM((PROTOS, LANES), f32),
            pltpu.VMEM((CORES, PROTOS, HALF), bf16),
            pltpu.VMEM((SUMS, TALL, LANES), f32),
            pltpu.VMEM((SUMS, NU * CORES, TALL, LANES), f32),
            pltpu.VMEM((SUMS, TALL, LANES), f32),
            pltpu.VMEM((SUMS, NX * NU, TALL, LANES), f32),
            pltpu.VMEM((TALL, LANES), f32),
            pltpu.VMEM((NX, SLAB, D), f32),
            pltpu.VMEM((PROTOS, D), bf16),
            pltpu.VMEM((PROTOS, HALF), bf16),
            pltpu.VMEM((NX, SLAB, CUT), f32),
            pltpu.VMEM((NX, NU, TILE, D - CUT), f32),
            pltpu.VMEM((NX, SLAB, CUT), f32),
            pltpu.VMEM((NU, NX, TILE, D - CUT), f32),
            pltpu.VMEM((SLAB, CUT), f32),
            pltpu.VMEM((NU, TILE, CUT), f32),
            pltpu.VMEM((NU, OWN, CUT), f32),
            pltpu.VMEM((NU, OWN, CUT), f32),
            pltpu.VMEM((NX * NU, OWN, D - CUT), f32),
            pltpu.VMEM((NX * NU, OWN, D - CUT), f32),
            dma((3,)),
            dma,
            dma,
            dma((2, 4)),
            dma((2, 3 + NX)),
            dma((2,)),
            dma((2,)),
            dma((SUMS,)),
            dma((SUMS,)),
            dma((SUMS,)),
            dma((SUMS,)),
            dma((2,)),
            dma((2,)),
            dma((2,)),
            dma((2,)),
            dma((3,)),
            dma((3,)),
        ],
        compiler_params=pltpu.CompilerParams(
            collective_id=0, has_side_effects=True, vmem_limit_bytes=48 << 20
        ),
        name="prototype_head",
    )(*(pltpu.with_memory_space_constraint(a, pltpu.HBM) for a in (student, teacher, protos)))


def solution(mesh):
    torus = Mesh(mesh.devices.reshape(NX, NU, NU, CORES), AXES)
    return jax.shard_map(
        on_device,
        mesh=torus,
        in_specs=(P(AXES, None),) * 3,
        out_specs=(P(AXES, None), P(AXES, None)),
        check_vma=False,
    )
```

```python
import jax
import jax.numpy as jnp
from jax import lax
from jax.experimental import pallas as pl
from jax.experimental.pallas import tpu as pltpu
from jax.sharding import Mesh
from jax.sharding import PartitionSpec as P

MESH = pl.DeviceIdType.MESH
AXES = ("wide_0", "wide_1", "narrow_0", "narrow_1")
SUMS = 3
NX, NU, CORES = 4, 8, 2
D = 512
OWN = 2
ROWS = NX * NU * NU * CORES * OWN
HALF = ROWS // CORES
SLAB = HALF // NX
TILE = NU * OWN
PROTOS = 512
BLOCK = 64
LANES = 128
TALL = ROWS // LANES
CUT = D // 2

epsilon = 1e-06
teacher_temp = 0.07
student_temp = 0.1

f32 = jnp.float32
bf16 = jnp.bfloat16


def inverse_norm(wide):
    return lax.rsqrt(jnp.sum(wide * wide, axis=1, keepdims=True) + epsilon)


def kernel(
    student_hbm,
    teacher_hbm,
    proto_hbm,
    sgrad_ref,
    pgrad_ref,
    student_ref,
    teacher_ref,
    proto_ref,
    first,
    stage,
    gat_t,
    gat_s,
    proto_hat,
    proto_inv,
    e_t,
    e_s,
    cols,
    grad,
    near_src,
    near,
    far_src,
    far,
    part,
    own,
    proto_mate,
    grad_mate,
    xbuf,
    ubuf,
    xslots,
    uslots,
    xsum,
    xuslots,
    uxsrc,
    uxslots,
    vsrc,
    vslots,
    st_src,
    st_near,
    st_part,
    st_far,
    st_tot,
    st_all,
    load,
    first_send,
    first_recv,
    gat_send,
    gat_recv,
    swap_send,
    swap_recv,
    near_send,
    near_recv,
    far_send,
    far_recv,
    mate_send,
    mate_recv,
    big_send,
    big_recv,
    end_send,
    end_recv,
    st_send,
    st_recv,
):
    x, y, z, c = (lax.axis_index(a) for a in AXES)
    u = z + c * (y - z)
    v = y + c * (z - y)
    oc = 1 - c

    def device(px, pu, pv):
        return (px, pv + c * (pu - pv), pu + c * (pv - pu), c)

    mate = (x, y, z, oc)

    def turned(at, k, n):
        return lax.rem(at + n // 2 + (1 - 2 * lax.rem(k, 2)) * ((k + 1) // 2), n)

    def near_peer(k):
        return (x, y, turned(z, k // CORES, NU), lax.rem(c + 1 + lax.rem(k, CORES), CORES))

    def far_peer(k):
        return (turned(x, lax.rem(k, NX), NX), turned(y, k // NX, NU), z, c)

    def wait(ref, sem):
        pltpu.make_async_copy(ref, ref, sem).wait()

    def push(src, dst, send, recv, target):
        pltpu.make_async_remote_copy(
            src_ref=src, dst_ref=dst, send_sem=send, recv_sem=recv, device_id=target, device_id_type=MESH
        ).start()

    inputs = [
        pltpu.make_async_copy(src, dst, load.at[i])
        for i, (src, dst) in enumerate(
            ((student_hbm, student_ref), (teacher_hbm, teacher_ref), (proto_hbm, proto_ref))
        )
    ]
    for copy in inputs:
        copy.start()

    barrier = pltpu.get_barrier_semaphore()

    def greet(target):
        pl.semaphore_signal(barrier, inc=1, device_id=target, device_id_type=MESH)
        return 0

    lax.fori_loop(0, NX * NU - 1, lambda k, _: greet(far_peer(k)), 0)
    lax.fori_loop(0, NU * CORES - 1, lambda k, _: greet(near_peer(k)), 0)

    for copy in inputs[:2]:
        copy.wait()
    wide_s = student_ref[...].astype(f32)
    wide_t = teacher_ref[...].astype(f32)
    s_inv = inverse_norm(wide_s)
    s_unit = wide_s * s_inv
    t_unit = wide_t * inverse_norm(wide_t)
    first[v, 0:OWN, :] = s_unit
    first[v, OWN : 2 * OWN, :] = t_unit

    def norm_block(i, _):
        at = pl.ds(pl.multiple_of(i * BLOCK, BLOCK), BLOCK)
        wide = proto_ref[at, :].astype(f32)
        inv = inverse_norm(wide)
        proto_inv[at, :] = jnp.broadcast_to(inv, (BLOCK, LANES))
        proto_hat[at, :] = (wide * inv).astype(bf16)
        return 0

    pl.semaphore_wait(barrier, NU * CORES - 1 + NX * NU - 1)

    def send_first(k, _):
        push(first.at[v], first.at[v], first_send, first_recv, device(x, u, turned(v, k, NU)))
        return 0

    lax.fori_loop(0, NU - 1, send_first, 0)
    inputs[2].wait()
    lax.fori_loop(0, PROTOS // BLOCK, norm_block, 0)
    wait(first.at[pl.ds(0, NU - 1)], first_recv)
    for i in range(NU):
        stage[0, OWN * i : OWN * (i + 1), :] = first[i, 0:OWN, :]
        stage[1, OWN * i : OWN * (i + 1), :] = first[i, OWN : 2 * OWN, :]
    for h in range(2):
        at = slice(h * CUT, (h + 1) * CUT)
        gat_s[h, c, x, u] = stage[0, :, at].astype(bf16)
        gat_t[h, c, x, u] = stage[1, :, at].astype(bf16)

    def open_step(buf, n):
        def send_hi(k, _):
            block = buf.at[1, c, x, u]
            push(block, block, gat_send.at[n, 1], gat_recv.at[n, 1], device(turned(x, k, NX), u, v))
            return 0

        def send_lo(k, _):
            block = buf.at[0, c, x, u]
            push(block, block, gat_send.at[n, 0], gat_recv.at[n, 0], device(x, turned(u, k, NU), v))
            return 0

        lax.fori_loop(0, NX - 1, send_hi, 0)
        lax.fori_loop(0, NU - 1, send_lo, 0)

    def spread_hi(buf, n):
        def send(k, _):
            block = buf.at[1, c, :, u]
            push(block, block, gat_send.at[n, 2], gat_recv.at[n, 2], device(x, turned(u, k, NU), v))
            return 0

        lax.fori_loop(0, NU - 1, send, 0)

    def spread_lo(buf, n):
        def send(k, _):
            block = buf.at[0, c, x]
            push(block, block, gat_send.at[n, 3], gat_recv.at[n, 3 + x], device(turned(x, k, NX), u, v))
            return 0

        lax.fori_loop(0, NX - 1, send, 0)

    def opened_hi(buf, n):
        wait(buf.at[0, 0, 0, pl.ds(0, NX - 1)], gat_recv.at[n, 1])

    def opened_lo(buf, n):
        wait(buf.at[0, 0, 0, pl.ds(0, NU - 1)], gat_recv.at[n, 0])

    def relay(buf, n):
        for k in range(NX):
            px = turned(x, NX - 1 if k == 0 else k - 1, NX)
            if k > 0:
                wait(buf.at[0, 0, 0], gat_recv.at[n, 3 + px])
            push(buf.at[0, c, px], buf.at[0, c, px], swap_send.at[n], swap_recv.at[n], mate)
        wait(buf.at[0, 0, :, pl.ds(0, NU - 1)], gat_recv.at[n, 2])
        push(buf.at[1, c], buf.at[1, c], swap_send.at[n], swap_recv.at[n], mate)

    def settle(buf, n):
        wait(buf.at[:, 0], swap_recv.at[n])
        wait(buf.at[0, 0, 0, pl.ds(0, NU - 1)], gat_send.at[n, 0])
        wait(buf.at[0, 0, 0, pl.ds(0, NX - 1)], gat_send.at[n, 1])
        wait(buf.at[0, 0, :, pl.ds(0, NU - 1)], gat_send.at[n, 2])
        wait(buf.at[0, 0, pl.ds(0, NX - 1)], gat_send.at[n, 3])
        wait(buf.at[:, 0], swap_send.at[n])

    open_step(gat_t, 1)
    push(proto_hat, proto_mate, mate_send.at[0], mate_recv.at[0], mate)
    wait(first.at[pl.ds(0, NU - 1)], first_send)
    opened_hi(gat_t, 1)
    spread_hi(gat_t, 1)
    opened_lo(gat_t, 1)
    spread_lo(gat_t, 1)
    open_step(gat_s, 0)
    relay(gat_t, 1)
    settle(gat_t, 1)

    def exponentials(buf, out, temp):
        for k in range(ROWS // 256):
            at = slice(k * 256, (k + 1) * 256)
            px = k % 2 * 2
            product = sum(
                lax.dot_general(
                    proto_hat[:, h * CUT : (h + 1) * CUT],
                    buf[h, k // 2, px : px + 2].reshape(256, CUT),
                    (((1,), (1,)), ((), ())),
                    preferred_element_type=f32,
                )
                for h in range(2)
            )
            out[:, at] = jnp.exp(product * (1.0 / temp))

    def folded(value):
        return jnp.sum(value.reshape(BLOCK // 8, 8, ROWS), axis=0)

    def flat(ref):
        return jnp.concatenate([ref[k : k + 1, :] for k in range(TALL)], axis=1)

    def put(dst, acc):
        for k in range(TALL):
            dst[k : k + 1, :] = jnp.sum(acc[:, k * LANES : (k + 1) * LANES], axis=0, keepdims=True)

    def sweep(scale):
        def body(i, acc):
            at = pl.ds(pl.multiple_of(i * BLOCK, BLOCK), BLOCK)
            e = e_t[at, :]
            weighed = e if scale is None else e * scale
            col = 1.0 / jnp.sum(weighed, axis=1, keepdims=True)
            cols[at, :] = jnp.broadcast_to(col, (BLOCK, LANES))
            return acc + folded(e * col)

        return lax.fori_loop(0, PROTOS // BLOCK, body, jnp.zeros((8, ROWS), f32))

    def near_start(n):
        me = z * CORES + c

        def send(k, _):
            push(near_src.at[n], near.at[n, me], near_send.at[n], near_recv.at[n], near_peer(k))
            return 0

        lax.fori_loop(0, NU * CORES - 1, send, 0)
        near[n, me] = near_src[n]

    def near_end(n):
        for sem in (near_recv, near_send):
            wait(near.at[n, pl.ds(0, NU * CORES - 1)], sem.at[n])
        far_src[n] = jnp.sum(near[n], axis=0)

    def far_start(n):
        me = x * NU + y

        def send(k, _):
            push(far_src.at[n], far.at[n, me], far_send.at[n], far_recv.at[n], far_peer(k))
            return 0

        lax.fori_loop(0, NX * NU - 1, send, 0)
        far[n, me] = far_src[n]

    def far_end(n):
        for sem in (far_recv, far_send):
            wait(far.at[n, pl.ds(0, NX * NU - 1)], sem.at[n])
        return 1.0 / jnp.sum(far[n], axis=0)

    def row_of(inverse):
        part[...] = inverse
        return flat(part)

    def student_sum(i, acc):
        at = pl.ds(pl.multiple_of(i * BLOCK, BLOCK), BLOCK)
        return acc + folded(e_s[at, :])

    exponentials(gat_t, e_t, teacher_temp)
    put(near_src.at[0], sweep(None))
    near_start(0)
    opened_hi(gat_s, 0)
    opened_lo(gat_s, 0)
    spread_lo(gat_s, 0)
    pl.when(c == 1)(lambda: spread_hi(gat_s, 0))
    near_end(0)
    far_start(0)
    pl.when(c == 0)(lambda: spread_hi(gat_s, 0))
    row_scale = row_of(far_end(0))

    put(near_src.at[1], sweep(row_scale))
    near_start(1)
    relay(gat_s, 0)
    near_end(1)
    far_start(1)
    settle(gat_s, 0)
    exponentials(gat_s, e_s, student_temp)
    student_part = lax.fori_loop(0, PROTOS // BLOCK, student_sum, jnp.zeros((8, ROWS), f32))
    for k in range(TALL):
        st_src[k] = jnp.sum(student_part[:, k * LANES : (k + 1) * LANES], axis=0, keepdims=True)

    def send_piece(k, _):
        pz = turned(z, k, NU)
        push(st_src.at[pz], st_near.at[z], st_send.at[0], st_recv.at[0], (x, y, pz, c))
        return 0

    def send_sum(k, _):
        push(st_part, st_far.at[x * NU + y], st_send.at[1], st_recv.at[1], far_peer(k))
        return 0

    def send_back(k, _):
        push(st_tot, st_all.at[z * CORES + c], st_send.at[2], st_recv.at[2], near_peer(k))
        return 0

    lax.fori_loop(0, NU - 1, send_piece, 0)
    st_near[z] = st_src[z]
    for sem in (st_recv, st_send):
        wait(st_near.at[pl.ds(0, NU - 1)], sem.at[0])
    st_part[...] = jnp.sum(st_near[...], axis=0)
    lax.fori_loop(0, NX * NU - 1, send_sum, 0)
    st_far[x * NU + y] = st_part[...]
    row_scale = row_of(far_end(1))

    put(near_src.at[2], sweep(row_scale))
    near_start(2)
    near_end(2)
    far_start(2)
    for sem in (st_recv, st_send):
        wait(st_far.at[pl.ds(0, NX * NU - 1)], sem.at[1])
    st_tot[...] = jnp.sum(st_far[...], axis=0)
    lax.fori_loop(0, NU * CORES - 1, send_back, 0)
    st_all[z * CORES + c] = st_tot[...]
    for sem in (st_recv, st_send):
        wait(st_all.at[pl.ds(0, NU * CORES - 1)], sem.at[2])
    totals = [st_all[CORES * k] + st_all[CORES * k + 1] for k in range(TALL)]
    student_scale = (1.0 / jnp.concatenate(totals, axis=1)) * (1.0 / student_temp)

    def scale_block(i, _):
        at = pl.ds(pl.multiple_of(i * BLOCK, BLOCK), BLOCK)
        e_s[at, :] = e_s[at, :] * student_scale
        e_t[at, :] = e_t[at, :] * cols[at, 0:1]
        return 0

    lax.fori_loop(0, PROTOS // BLOCK, scale_block, 0)
    part[...] = far_end(2) * (1.0 / student_temp)

    def gradients(core):
        rows = [part[pl.ds(core * (TALL // CORES) + k, 1), :] for k in range(TALL // CORES)]
        scale = jnp.concatenate(rows, axis=1)
        lanes = pl.ds(pl.multiple_of(core * HALF, HALF), HALF)

        def body(i, _):
            at = pl.ds(pl.multiple_of(i * BLOCK, BLOCK), BLOCK)
            grad[core, at, :] = (e_s[at, lanes] - e_t[at, lanes] * scale).astype(bf16)
            return 0

        lax.fori_loop(0, PROTOS // BLOCK, body, 0)

    gradients(oc)
    push(grad.at[oc], grad_mate, mate_send.at[1], mate_recv.at[1], mate)
    gradients(c)

    def row_product(left, px, right):
        at = pl.ds(pl.multiple_of(px * SLAB, SLAB), SLAB)
        return lax.dot_general(left[:, at], right[...], (((0,), (0,)), ((), ())), preferred_element_type=f32)

    for px in range(NX):
        own[px] = row_product(grad.at[c], px, proto_hat)
    wait(proto_mate, mate_recv.at[0])
    wait(grad_mate, mate_recv.at[1])
    for k in range(NX):
        px = turned(x, k, NX)
        total = own[px] + row_product(grad_mate, px, proto_mate)
        xbuf[px] = total[:, :CUT]
        ubuf[px] = total[:, CUT:].reshape(NU, TILE, D - CUT)
        if k < NX - 1:
            push(xbuf.at[px], xslots.at[x], big_send.at[0], big_recv.at[0], device(px, u, v))

    def send_u(k, _):
        pu = turned(u, k, NU)
        push(ubuf.at[:, pu], uslots.at[u], big_send.at[1], big_recv.at[1], device(x, pu, v))
        return 0

    lax.fori_loop(0, NU - 1, send_u, 0)
    xslots[x] = xbuf[x]
    uslots[u] = ubuf[:, u]

    def proto_block(i):
        at = slice(i * 256, (i + 1) * 256)
        halves = [
            sum(
                jnp.dot(grad[core, at, :], gat_s[h, core].reshape(HALF, CUT), preferred_element_type=f32)
                for core in range(CORES)
            )
            for h in range(2)
        ]
        step = jnp.concatenate(halves, axis=1)
        inv = proto_inv[at, 0:1]
        unit = proto_ref[at, :].astype(f32) * inv
        pgrad_ref[at, :] = (step - unit * jnp.sum(unit * step, axis=1, keepdims=True)) * inv

    for i in range(PROTOS // 256):
        proto_block(i)

    for sem in (big_recv, big_send):
        wait(xslots.at[pl.ds(0, NX - 1)], sem.at[0])
    xsum[...] = jnp.sum(xslots[...], axis=0)

    def send_xu(k, _):
        pu = turned(u, k, NU)
        src = xsum.at[pl.ds(pl.multiple_of(pu * TILE, TILE), TILE)]
        push(src, xuslots.at[u], end_send.at[0], end_recv.at[0], device(x, pu, v))
        return 0

    lax.fori_loop(0, NU - 1, send_xu, 0)
    xuslots[u] = xsum[pl.ds(pl.multiple_of(u * TILE, TILE), TILE), :]

    for sem in (big_recv, big_send):
        wait(uslots.at[pl.ds(0, NU - 1)], sem.at[1])
    uxsrc[...] = jnp.sum(uslots[...], axis=0)

    def send_ux(k, _):
        px = turned(x, k, NX)
        push(uxsrc.at[px], uxslots.at[x], end_send.at[1], end_recv.at[1], device(px, u, v))
        return 0

    lax.fori_loop(0, NX - 1, send_ux, 0)
    uxslots[x] = uxsrc[x]

    for sem in (end_recv, end_send):
        wait(xuslots.at[pl.ds(0, NU - 1)], sem.at[0])
    left = jnp.sum(xuslots[...], axis=0)
    for sem in (end_recv, end_send):
        wait(uxslots.at[pl.ds(0, NX - 1)], sem.at[1])
    right = jnp.sum(uxslots[...], axis=0)
    for pv in range(NU):
        at = slice(pv * OWN, (pv + 1) * OWN)
        vsrc[pv, :, :CUT] = left[at, :]
        vsrc[pv, :, CUT:] = right[at, :]

    def send_v(k, _):
        pv = turned(v, k, NU)
        push(vsrc.at[pv], vslots.at[v], end_send.at[2], end_recv.at[2], device(x, u, pv))
        return 0

    lax.fori_loop(0, NU - 1, send_v, 0)
    vslots[v] = vsrc[v]
    for sem in (end_recv, end_send):
        wait(vslots.at[pl.ds(0, NU - 1)], sem.at[2])
    step = jnp.sum(vslots[...], axis=0)
    wait(proto_mate, mate_send.at[0])
    wait(grad_mate, mate_send.at[1])

    sgrad_ref[...] = (step - s_unit * jnp.sum(s_unit * step, axis=1, keepdims=True)) * s_inv


def on_device(student, teacher, protos):
    vmem = pl.BlockSpec(memory_space=pltpu.VMEM)
    dma = pltpu.SemaphoreType.DMA
    return pl.pallas_call(
        kernel,
        out_shape=(
            jax.ShapeDtypeStruct((OWN, D), f32),
            jax.ShapeDtypeStruct((PROTOS, D), f32),
        ),
        in_specs=[pl.BlockSpec(memory_space=pltpu.HBM)] * 3,
        out_specs=(vmem, vmem),
        scratch_shapes=[
            pltpu.VMEM((OWN, D), bf16),
            pltpu.VMEM((OWN, D), bf16),
            pltpu.VMEM((PROTOS, D), bf16),
            pltpu.VMEM((NU, 2 * OWN, D), f32),
            pltpu.VMEM((2, TILE, D), f32),
            pltpu.VMEM((2, CORES, NX, NU, TILE, CUT), bf16),
            pltpu.VMEM((2, CORES, NX, NU, TILE, CUT), bf16),
            pltpu.VMEM((PROTOS, D), bf16),
            pltpu.VMEM((PROTOS, LANES), f32),
            pltpu.VMEM((PROTOS, ROWS), f32),
            pltpu.VMEM((PROTOS, ROWS), f32),
            pltpu.VMEM((PROTOS, LANES), f32),
            pltpu.VMEM((CORES, PROTOS, HALF), bf16),
            pltpu.VMEM((SUMS, TALL, LANES), f32),
            pltpu.VMEM((SUMS, NU * CORES, TALL, LANES), f32),
            pltpu.VMEM((SUMS, TALL, LANES), f32),
            pltpu.VMEM((SUMS, NX * NU, TALL, LANES), f32),
            pltpu.VMEM((TALL, LANES), f32),
            pltpu.VMEM((NX, SLAB, D), f32),
            pltpu.VMEM((PROTOS, D), bf16),
            pltpu.VMEM((PROTOS, HALF), bf16),
            pltpu.VMEM((NX, SLAB, CUT), f32),
            pltpu.VMEM((NX, NU, TILE, D - CUT), f32),
            pltpu.VMEM((NX, SLAB, CUT), f32),
            pltpu.VMEM((NU, NX, TILE, D - CUT), f32),
            pltpu.VMEM((SLAB, CUT), f32),
            pltpu.VMEM((NU, TILE, CUT), f32),
            pltpu.VMEM((NX, TILE, D - CUT), f32),
            pltpu.VMEM((NX, TILE, D - CUT), f32),
            pltpu.VMEM((NU, OWN, D), f32),
            pltpu.VMEM((NU, OWN, D), f32),
            pltpu.VMEM((TALL, 1, LANES), f32),
            pltpu.VMEM((NU, 1, LANES), f32),
            pltpu.VMEM((1, LANES), f32),
            pltpu.VMEM((NX * NU, 1, LANES), f32),
            pltpu.VMEM((1, LANES), f32),
            pltpu.VMEM((NU * CORES, 1, LANES), f32),
            dma((3,)),
            dma,
            dma,
            dma((2, 4)),
            dma((2, 3 + NX)),
            dma((2,)),
            dma((2,)),
            dma((SUMS,)),
            dma((SUMS,)),
            dma((SUMS,)),
            dma((SUMS,)),
            dma((2,)),
            dma((2,)),
            dma((2,)),
            dma((2,)),
            dma((3,)),
            dma((3,)),
            dma((3,)),
            dma((3,)),
        ],
        compiler_params=pltpu.CompilerParams(
            collective_id=0, has_side_effects=True, vmem_limit_bytes=48 << 20
        ),
        name="prototype_head",
    )(*(pltpu.with_memory_space_constraint(a, pltpu.HBM) for a in (student, teacher, protos)))


def solution(mesh):
    torus = Mesh(mesh.devices.reshape(NX, NU, NU, CORES), AXES)
    return jax.shard_map(
        on_device,
        mesh=torus,
        in_specs=(P(AXES, None),) * 3,
        out_specs=(P(AXES, None), P(AXES, None)),
        check_vma=False,
    )
```

```python
import jax
import jax.numpy as jnp
from jax import lax
from jax.experimental import pallas as pl
from jax.experimental.pallas import tpu as pltpu
from jax.sharding import Mesh
from jax.sharding import PartitionSpec as P

MESH = pl.DeviceIdType.MESH
AXES = ("wide_0", "wide_1", "narrow_0", "narrow_1")
SUMS = 3
NX, NU, CORES = 4, 8, 2
D = 512
OWN = 2
ROWS = NX * NU * NU * CORES * OWN
HALF = ROWS // CORES
SLAB = HALF // NX
TILE = NU * OWN
PROTOS = 512
BLOCK = 128
LANES = 128
TALL = ROWS // LANES
CUT = D // 2

epsilon = 1e-06
teacher_temp = 0.07
student_temp = 0.1

f32 = jnp.float32
bf16 = jnp.bfloat16


def rem(k, n):
    return k % n if isinstance(k, int) else lax.rem(k, n)


def inverse_norm(wide):
    return lax.rsqrt(jnp.sum(wide * wide, axis=1, keepdims=True) + epsilon)


def kernel(
    student_hbm,
    teacher_hbm,
    proto_hbm,
    sgrad_ref,
    pgrad_ref,
    student_ref,
    teacher_ref,
    proto_ref,
    first,
    stage,
    gat_t,
    gat_s,
    proto_hat,
    proto_inv,
    e_t,
    e_s,
    cols,
    grad,
    near_src,
    near,
    far_src,
    far,
    part,
    own,
    proto_mate,
    grad_mate,
    xbuf,
    ubuf,
    xslots,
    uslots,
    xsum,
    xuslots,
    uxsrc,
    uxslots,
    vsrc,
    vslots,
    st_src,
    st_near,
    st_part,
    st_far,
    st_tot,
    st_all,
    load,
    first_send,
    first_recv,
    gat_send,
    gat_recv,
    swap_send,
    swap_recv,
    near_send,
    near_recv,
    far_send,
    far_recv,
    mate_send,
    mate_recv,
    big_send,
    big_recv,
    end_send,
    end_recv,
    st_send,
    st_recv,
):
    x, y, z, c = (lax.axis_index(a) for a in AXES)
    u = z + c * (y - z)
    v = y + c * (z - y)
    oc = 1 - c

    def device(px, pu, pv):
        return (px, pv + c * (pu - pv), pu + c * (pv - pu), c)

    mate = (x, y, z, oc)

    def turned(at, k, n):
        return lax.rem(at + (n // 2 + (1 - 2 * rem(k, 2)) * ((k + 1) // 2)), n)

    def near_peer(k):
        return (x, y, turned(z, k // CORES, NU), lax.rem(c + (1 + rem(k, CORES)), CORES))

    def far_peer(k):
        return (turned(x, rem(k, NX), NX), turned(y, k // NX, NU), z, c)

    def wait(ref, sem):
        pltpu.make_async_copy(ref, ref, sem).wait()

    def push(src, dst, send, recv, target):
        pltpu.make_async_remote_copy(
            src_ref=src, dst_ref=dst, send_sem=send, recv_sem=recv, device_id=target, device_id_type=MESH
        ).start()

    inputs = [
        pltpu.make_async_copy(src, dst, load.at[i])
        for i, (src, dst) in enumerate(
            ((student_hbm, student_ref), (teacher_hbm, teacher_ref), (proto_hbm, proto_ref))
        )
    ]
    for copy in inputs:
        copy.start()

    barrier = pltpu.get_barrier_semaphore()

    def greet(target):
        pl.semaphore_signal(barrier, inc=1, device_id=target, device_id_type=MESH)

    for k in range(NX * NU - 1):
        greet(far_peer(k))
    for k in range(NU * CORES - 1):
        greet(near_peer(k))

    for copy in inputs[:2]:
        copy.wait()
    wide_s = student_ref[...].astype(f32)
    wide_t = teacher_ref[...].astype(f32)
    s_inv = inverse_norm(wide_s)
    s_unit = wide_s * s_inv
    t_unit = wide_t * inverse_norm(wide_t)
    first[v, 0:OWN, :] = s_unit
    first[v, OWN : 2 * OWN, :] = t_unit

    def norm_block(i, _):
        at = pl.ds(pl.multiple_of(i * BLOCK, BLOCK), BLOCK)
        wide = proto_ref[at, :].astype(f32)
        inv = inverse_norm(wide)
        proto_inv[at, :] = jnp.broadcast_to(inv, (BLOCK, LANES))
        proto_hat[at, :] = (wide * inv).astype(bf16)
        return 0

    pl.semaphore_wait(barrier, NU * CORES - 1 + NX * NU - 1)

    def send_first(k, _):
        push(first.at[v], first.at[v], first_send, first_recv, device(x, u, turned(v, k, NU)))
        return 0

    lax.fori_loop(0, NU - 1, send_first, 0)
    inputs[2].wait()
    lax.fori_loop(0, PROTOS // BLOCK, norm_block, 0)
    wait(first.at[pl.ds(0, NU - 1)], first_recv)
    for i in range(NU):
        stage[0, OWN * i : OWN * (i + 1), :] = first[i, 0:OWN, :]
        stage[1, OWN * i : OWN * (i + 1), :] = first[i, OWN : 2 * OWN, :]
    for h in range(2):
        at = slice(h * CUT, (h + 1) * CUT)
        gat_s[h, c, x, u] = stage[0, :, at].astype(bf16)
        gat_t[h, c, x, u] = stage[1, :, at].astype(bf16)

    def open_step(buf, n):
        def send_hi(k, _):
            block = buf.at[1, c, x, u]
            push(block, block, gat_send.at[n, 1], gat_recv.at[n, 1], device(turned(x, k, NX), u, v))
            return 0

        def send_lo(k, _):
            block = buf.at[0, c, x, u]
            push(block, block, gat_send.at[n, 0], gat_recv.at[n, 0], device(x, turned(u, k, NU), v))
            return 0

        lax.fori_loop(0, NX - 1, send_hi, 0)
        lax.fori_loop(0, NU - 1, send_lo, 0)

    def spread_hi(buf, n):
        def send(k, _):
            block = buf.at[1, c, :, u]
            push(block, block, gat_send.at[n, 2], gat_recv.at[n, 2], device(x, turned(u, k, NU), v))
            return 0

        lax.fori_loop(0, NU - 1, send, 0)

    def spread_lo(buf, n):
        def send(k, _):
            block = buf.at[0, c, x]
            push(block, block, gat_send.at[n, 3], gat_recv.at[n, 3 + x], device(turned(x, k, NX), u, v))
            return 0

        lax.fori_loop(0, NX - 1, send, 0)

    def opened_hi(buf, n):
        wait(buf.at[0, 0, 0, pl.ds(0, NX - 1)], gat_recv.at[n, 1])

    def opened_lo(buf, n):
        wait(buf.at[0, 0, 0, pl.ds(0, NU - 1)], gat_recv.at[n, 0])

    def relay(buf, n):
        for k in range(NX):
            px = turned(x, NX - 1 if k == 0 else k - 1, NX)
            if k > 0:
                wait(buf.at[0, 0, 0], gat_recv.at[n, 3 + px])
            push(buf.at[0, c, px], buf.at[0, c, px], swap_send.at[n], swap_recv.at[n], mate)
        wait(buf.at[0, 0, :, pl.ds(0, NU - 1)], gat_recv.at[n, 2])
        push(buf.at[1, c], buf.at[1, c], swap_send.at[n], swap_recv.at[n], mate)

    def settle(buf, n):
        wait(buf.at[:, 0], swap_recv.at[n])
        wait(buf.at[0, 0, 0, pl.ds(0, NU - 1)], gat_send.at[n, 0])
        wait(buf.at[0, 0, 0, pl.ds(0, NX - 1)], gat_send.at[n, 1])
        wait(buf.at[0, 0, :, pl.ds(0, NU - 1)], gat_send.at[n, 2])
        wait(buf.at[0, 0, pl.ds(0, NX - 1)], gat_send.at[n, 3])
        wait(buf.at[:, 0], swap_send.at[n])

    open_step(gat_t, 1)
    wait(first.at[pl.ds(0, NU - 1)], first_send)
    opened_hi(gat_t, 1)
    spread_hi(gat_t, 1)
    opened_lo(gat_t, 1)
    spread_lo(gat_t, 1)
    open_step(gat_s, 0)
    relay(gat_t, 1)

    def exponentials(buf, out, temp, core):
        for k in range(HALF // 256):
            at = pl.ds(pl.multiple_of(core * HALF + k * 256, 256), 256)
            px = k * 256 // SLAB
            product = sum(
                lax.dot_general(
                    proto_hat[:, h * CUT : (h + 1) * CUT],
                    buf[h, core, px : px + 256 // SLAB].reshape(256, CUT),
                    (((1,), (1,)), ((), ())),
                    preferred_element_type=f32,
                )
                for h in range(2)
            )
            out[:, at] = jnp.exp(product * (1.0 / temp))

    def folded(value):
        return jnp.sum(value.reshape(BLOCK // 8, 8, ROWS), axis=0)

    def flat(ref):
        return jnp.concatenate([ref[k : k + 1, :] for k in range(TALL)], axis=1)

    def put(dst, acc):
        for k in range(TALL):
            dst[k : k + 1, :] = jnp.sum(acc[:, k * LANES : (k + 1) * LANES], axis=0, keepdims=True)

    def sweep(scale):
        def body(i, acc):
            at = pl.ds(pl.multiple_of(i * BLOCK, BLOCK), BLOCK)
            e = e_t[at, :]
            weighed = e if scale is None else e * scale
            col = 1.0 / jnp.sum(weighed, axis=1, keepdims=True)
            cols[at, :] = jnp.broadcast_to(col, (BLOCK, LANES))
            return acc + folded(e * col)

        return lax.fori_loop(0, PROTOS // BLOCK, body, jnp.zeros((8, ROWS), f32))

    def near_start(n):
        me = z * CORES + c

        def send(k, _):
            push(near_src.at[n], near.at[n, me], near_send.at[n], near_recv.at[n], near_peer(k))
            return 0

        lax.fori_loop(0, NU * CORES - 1, send, 0)
        near[n, me] = near_src[n]

    def near_end(n):
        for sem in (near_recv, near_send):
            wait(near.at[n, pl.ds(0, NU * CORES - 1)], sem.at[n])
        far_src[n] = jnp.sum(near[n], axis=0)

    def far_start(n):
        me = x * NU + y

        def send(k, _):
            push(far_src.at[n], far.at[n, me], far_send.at[n], far_recv.at[n], far_peer(k))
            return 0

        lax.fori_loop(0, NX * NU - 1, send, 0)
        far[n, me] = far_src[n]

    def far_end(n):
        for sem in (far_recv, far_send):
            wait(far.at[n, pl.ds(0, NX * NU - 1)], sem.at[n])
        return 1.0 / jnp.sum(far[n], axis=0)

    def row_of(inverse):
        part[...] = inverse
        return flat(part)

    def student_sum(i, acc):
        at = pl.ds(pl.multiple_of(i * BLOCK, BLOCK), BLOCK)
        return acc + folded(e_s[at, :])

    exponentials(gat_t, e_t, teacher_temp, c)
    settle(gat_t, 1)
    exponentials(gat_t, e_t, teacher_temp, oc)
    put(near_src.at[0], sweep(None))
    near_start(0)
    push(proto_hat, proto_mate, mate_send.at[0], mate_recv.at[0], mate)
    opened_hi(gat_s, 0)
    opened_lo(gat_s, 0)
    spread_lo(gat_s, 0)
    pl.when(c == 1)(lambda: spread_hi(gat_s, 0))
    near_end(0)
    far_start(0)
    pl.when(c == 0)(lambda: spread_hi(gat_s, 0))
    row_scale = row_of(far_end(0))

    put(near_src.at[1], sweep(row_scale))
    near_start(1)
    relay(gat_s, 0)
    near_end(1)
    far_start(1)
    settle(gat_s, 0)
    for core in range(CORES):
        exponentials(gat_s, e_s, student_temp, core)
    student_part = lax.fori_loop(0, PROTOS // BLOCK, student_sum, jnp.zeros((8, ROWS), f32))
    for k in range(TALL):
        st_src[k] = jnp.sum(student_part[:, k * LANES : (k + 1) * LANES], axis=0, keepdims=True)

    def send_piece(k, _):
        pz = turned(z, k, NU)
        push(st_src.at[pz], st_near.at[z], st_send.at[0], st_recv.at[0], (x, y, pz, c))
        return 0

    def send_sum(k, _):
        push(st_part, st_far.at[x * NU + y], st_send.at[1], st_recv.at[1], far_peer(k))
        return 0

    def send_back(k, _):
        push(st_tot, st_all.at[z * CORES + c], st_send.at[2], st_recv.at[2], near_peer(k))
        return 0

    lax.fori_loop(0, NU - 1, send_piece, 0)
    st_near[z] = st_src[z]
    for sem in (st_recv, st_send):
        wait(st_near.at[pl.ds(0, NU - 1)], sem.at[0])
    st_part[...] = jnp.sum(st_near[...], axis=0)
    lax.fori_loop(0, NX * NU - 1, send_sum, 0)
    st_far[x * NU + y] = st_part[...]
    row_scale = row_of(far_end(1))

    put(near_src.at[2], sweep(row_scale))
    near_start(2)
    near_end(2)
    far_start(2)
    for sem in (st_recv, st_send):
        wait(st_far.at[pl.ds(0, NX * NU - 1)], sem.at[1])
    st_tot[...] = jnp.sum(st_far[...], axis=0)
    lax.fori_loop(0, NU * CORES - 1, send_back, 0)
    st_all[z * CORES + c] = st_tot[...]
    for sem in (st_recv, st_send):
        wait(st_all.at[pl.ds(0, NU * CORES - 1)], sem.at[2])
    totals = [st_all[CORES * k] + st_all[CORES * k + 1] for k in range(TALL)]
    student_scale = (1.0 / jnp.concatenate(totals, axis=1)) * (1.0 / student_temp)

    def scale_block(i, _):
        at = pl.ds(pl.multiple_of(i * BLOCK, BLOCK), BLOCK)
        e_s[at, :] = e_s[at, :] * student_scale
        e_t[at, :] = e_t[at, :] * cols[at, 0:1]
        return 0

    lax.fori_loop(0, PROTOS // BLOCK, scale_block, 0)
    part[...] = far_end(2) * (1.0 / student_temp)

    def gradients(core):
        rows = [part[pl.ds(core * (TALL // CORES) + k, 1), :] for k in range(TALL // CORES)]
        scale = jnp.concatenate(rows, axis=1)
        lanes = pl.ds(pl.multiple_of(core * HALF, HALF), HALF)

        def body(i, _):
            at = pl.ds(pl.multiple_of(i * BLOCK, BLOCK), BLOCK)
            grad[core, at, :] = (e_s[at, lanes] - e_t[at, lanes] * scale).astype(bf16)
            return 0

        lax.fori_loop(0, PROTOS // BLOCK, body, 0)

    gradients(oc)
    push(grad.at[oc], grad_mate, mate_send.at[1], mate_recv.at[1], mate)
    gradients(c)

    def row_product(left, px, right):
        at = pl.ds(pl.multiple_of(px * SLAB, SLAB), SLAB)
        return lax.dot_general(left[:, at], right[...], (((0,), (0,)), ((), ())), preferred_element_type=f32)

    for px in range(NX):
        own[px] = row_product(grad.at[c], px, proto_hat)
    wait(proto_mate, mate_recv.at[0])
    wait(grad_mate, mate_recv.at[1])
    for k in range(NX):
        px = turned(x, k, NX)
        total = own[px] + row_product(grad_mate, px, proto_mate)
        xbuf[px] = total[:, :CUT]
        ubuf[px] = total[:, CUT:].reshape(NU, TILE, D - CUT)
        if k < NX - 1:
            push(xbuf.at[px], xslots.at[x], big_send.at[0], big_recv.at[0], device(px, u, v))

    def send_u(k, _):
        pu = turned(u, k, NU)
        push(ubuf.at[:, pu], uslots.at[u], big_send.at[1], big_recv.at[1], device(x, pu, v))
        return 0

    lax.fori_loop(0, NU - 1, send_u, 0)
    xslots[x] = xbuf[x]
    uslots[u] = ubuf[:, u]

    def proto_block(i):
        at = slice(i * 256, (i + 1) * 256)
        halves = [
            sum(
                jnp.dot(grad[core, at, :], gat_s[h, core].reshape(HALF, CUT), preferred_element_type=f32)
                for core in range(CORES)
            )
            for h in range(2)
        ]
        step = jnp.concatenate(halves, axis=1)
        inv = proto_inv[at, 0:1]
        unit = proto_ref[at, :].astype(f32) * inv
        pgrad_ref[at, :] = (step - unit * jnp.sum(unit * step, axis=1, keepdims=True)) * inv

    for i in range(PROTOS // 256):
        proto_block(i)

    for sem in (big_recv, big_send):
        wait(xslots.at[pl.ds(0, NX - 1)], sem.at[0])
    xsum[...] = jnp.sum(xslots[...], axis=0)

    def send_xu(k, _):
        pu = turned(u, k, NU)
        src = xsum.at[pl.ds(pl.multiple_of(pu * TILE, TILE), TILE)]
        push(src, xuslots.at[u], end_send.at[0], end_recv.at[0], device(x, pu, v))
        return 0

    lax.fori_loop(0, NU - 1, send_xu, 0)
    xuslots[u] = xsum[pl.ds(pl.multiple_of(u * TILE, TILE), TILE), :]

    for sem in (big_recv, big_send):
        wait(uslots.at[pl.ds(0, NU - 1)], sem.at[1])
    uxsrc[...] = jnp.sum(uslots[...], axis=0)

    def send_ux(k, _):
        px = turned(x, k, NX)
        push(uxsrc.at[px], uxslots.at[x], end_send.at[1], end_recv.at[1], device(px, u, v))
        return 0

    lax.fori_loop(0, NX - 1, send_ux, 0)
    uxslots[x] = uxsrc[x]

    for sem in (end_recv, end_send):
        wait(xuslots.at[pl.ds(0, NU - 1)], sem.at[0])
    left = jnp.sum(xuslots[...], axis=0)
    for sem in (end_recv, end_send):
        wait(uxslots.at[pl.ds(0, NX - 1)], sem.at[1])
    right = jnp.sum(uxslots[...], axis=0)
    for pv in range(NU):
        at = slice(pv * OWN, (pv + 1) * OWN)
        vsrc[pv, :, :CUT] = left[at, :]
        vsrc[pv, :, CUT:] = right[at, :]

    def send_v(k, _):
        pv = turned(v, k, NU)
        push(vsrc.at[pv], vslots.at[v], end_send.at[2], end_recv.at[2], device(x, u, pv))
        return 0

    lax.fori_loop(0, NU - 1, send_v, 0)
    vslots[v] = vsrc[v]
    for sem in (end_recv, end_send):
        wait(vslots.at[pl.ds(0, NU - 1)], sem.at[2])
    step = jnp.sum(vslots[...], axis=0)
    wait(proto_mate, mate_send.at[0])
    wait(grad_mate, mate_send.at[1])

    sgrad_ref[...] = (step - s_unit * jnp.sum(s_unit * step, axis=1, keepdims=True)) * s_inv


def on_device(student, teacher, protos):
    vmem = pl.BlockSpec(memory_space=pltpu.VMEM)
    dma = pltpu.SemaphoreType.DMA
    return pl.pallas_call(
        kernel,
        out_shape=(
            jax.ShapeDtypeStruct((OWN, D), f32),
            jax.ShapeDtypeStruct((PROTOS, D), f32),
        ),
        in_specs=[pl.BlockSpec(memory_space=pltpu.HBM)] * 3,
        out_specs=(vmem, vmem),
        scratch_shapes=[
            pltpu.VMEM((OWN, D), bf16),
            pltpu.VMEM((OWN, D), bf16),
            pltpu.VMEM((PROTOS, D), bf16),
            pltpu.VMEM((NU, 2 * OWN, D), f32),
            pltpu.VMEM((2, TILE, D), f32),
            pltpu.VMEM((2, CORES, NX, NU, TILE, CUT), bf16),
            pltpu.VMEM((2, CORES, NX, NU, TILE, CUT), bf16),
            pltpu.VMEM((PROTOS, D), bf16),
            pltpu.VMEM((PROTOS, LANES), f32),
            pltpu.VMEM((PROTOS, ROWS), f32),
            pltpu.VMEM((PROTOS, ROWS), f32),
            pltpu.VMEM((PROTOS, LANES), f32),
            pltpu.VMEM((CORES, PROTOS, HALF), bf16),
            pltpu.VMEM((SUMS, TALL, LANES), f32),
            pltpu.VMEM((SUMS, NU * CORES, TALL, LANES), f32),
            pltpu.VMEM((SUMS, TALL, LANES), f32),
            pltpu.VMEM((SUMS, NX * NU, TALL, LANES), f32),
            pltpu.VMEM((TALL, LANES), f32),
            pltpu.VMEM((NX, SLAB, D), f32),
            pltpu.VMEM((PROTOS, D), bf16),
            pltpu.VMEM((PROTOS, HALF), bf16),
            pltpu.VMEM((NX, SLAB, CUT), f32),
            pltpu.VMEM((NX, NU, TILE, D - CUT), f32),
            pltpu.VMEM((NX, SLAB, CUT), f32),
            pltpu.VMEM((NU, NX, TILE, D - CUT), f32),
            pltpu.VMEM((SLAB, CUT), f32),
            pltpu.VMEM((NU, TILE, CUT), f32),
            pltpu.VMEM((NX, TILE, D - CUT), f32),
            pltpu.VMEM((NX, TILE, D - CUT), f32),
            pltpu.VMEM((NU, OWN, D), f32),
            pltpu.VMEM((NU, OWN, D), f32),
            pltpu.VMEM((TALL, 1, LANES), f32),
            pltpu.VMEM((NU, 1, LANES), f32),
            pltpu.VMEM((1, LANES), f32),
            pltpu.VMEM((NX * NU, 1, LANES), f32),
            pltpu.VMEM((1, LANES), f32),
            pltpu.VMEM((NU * CORES, 1, LANES), f32),
            dma((3,)),
            dma,
            dma,
            dma((2, 4)),
            dma((2, 3 + NX)),
            dma((2,)),
            dma((2,)),
            dma((SUMS,)),
            dma((SUMS,)),
            dma((SUMS,)),
            dma((SUMS,)),
            dma((2,)),
            dma((2,)),
            dma((2,)),
            dma((2,)),
            dma((3,)),
            dma((3,)),
            dma((3,)),
            dma((3,)),
        ],
        compiler_params=pltpu.CompilerParams(
            collective_id=0, has_side_effects=True, vmem_limit_bytes=48 << 20
        ),
        name="prototype_head",
    )(*(pltpu.with_memory_space_constraint(a, pltpu.HBM) for a in (student, teacher, protos)))


def solution(mesh):
    torus = Mesh(mesh.devices.reshape(NX, NU, NU, CORES), AXES)
    return jax.shard_map(
        on_device,
        mesh=torus,
        in_specs=(P(AXES, None),) * 3,
        out_specs=(P(AXES, None), P(AXES, None)),
        check_vma=False,
    )
```

```python
import jax
import jax.numpy as jnp
from jax import lax
from jax.experimental import pallas as pl
from jax.experimental.pallas import tpu as pltpu
from jax.sharding import Mesh
from jax.sharding import PartitionSpec as P

MESH = pl.DeviceIdType.MESH
AXES = ("wide_0", "wide_1", "narrow_0", "narrow_1")
SUMS = 3
NX, NU, CORES = 4, 8, 2
D = 512
OWN = 2
ROWS = NX * NU * NU * CORES * OWN
HALF = ROWS // CORES
SLAB = HALF // NX
TILE = NU * OWN
PROTOS = 512
BLOCK = 128
SWEEP = 256
LANES = 128
TALL = ROWS // LANES
CUT = D // 2

epsilon = 1e-06
teacher_temp = 0.07
student_temp = 0.1

f32 = jnp.float32
bf16 = jnp.bfloat16


def each(n, act):
    for k in range(n):
        act(k)


def inverse_norm(wide):
    return lax.rsqrt(jnp.sum(wide * wide, axis=1, keepdims=True) + epsilon)


def kernel(
    student_hbm,
    teacher_hbm,
    proto_hbm,
    sgrad_ref,
    pgrad_ref,
    student_ref,
    teacher_ref,
    proto_ref,
    first,
    stage,
    gat_t,
    gat_s,
    proto_hat,
    proto_inv,
    e_t,
    e_s,
    cols,
    grad,
    near_src,
    near,
    far_src,
    far,
    part,
    own,
    proto_mate,
    grad_mate,
    xbuf,
    ubuf,
    xslots,
    uslots,
    xsum,
    xuslots,
    uxsrc,
    uxslots,
    vsrc,
    vslots,
    st_src,
    st_near,
    st_part,
    st_far,
    st_tot,
    st_all,
    load,
    first_send,
    first_recv,
    gat_send,
    gat_recv,
    swap_send,
    swap_recv,
    near_send,
    near_recv,
    far_send,
    far_recv,
    mate_send,
    mate_recv,
    big_send,
    big_recv,
    end_send,
    end_recv,
    st_send,
    st_recv,
):
    x, y, z, c = (lax.axis_index(a) for a in AXES)
    u = z + c * (y - z)
    v = y + c * (z - y)
    oc = 1 - c

    def device(px, pu, pv):
        return (px, pv + c * (pu - pv), pu + c * (pv - pu), c)

    mate = (x, y, z, oc)

    def turned(at, k, n):
        return lax.rem(at + (n // 2 + (1 - 2 * (k % 2)) * ((k + 1) // 2)), n)

    def near_peer(k):
        return (x, y, turned(z, k // CORES, NU), lax.rem(c + (1 + k % CORES), CORES))

    def far_peer(k):
        return (turned(x, k % NX, NX), turned(y, k // NX, NU), z, c)

    def wait(ref, sem):
        pltpu.make_async_copy(ref, ref, sem).wait()

    def push(src, dst, send, recv, target):
        pltpu.make_async_remote_copy(
            src_ref=src, dst_ref=dst, send_sem=send, recv_sem=recv, device_id=target, device_id_type=MESH
        ).start()

    inputs = [
        pltpu.make_async_copy(src, dst, load.at[i])
        for i, (src, dst) in enumerate(
            ((student_hbm, student_ref), (teacher_hbm, teacher_ref), (proto_hbm, proto_ref))
        )
    ]
    for copy in inputs:
        copy.start()

    barrier = pltpu.get_barrier_semaphore()

    def greet(target):
        pl.semaphore_signal(barrier, inc=1, device_id=target, device_id_type=MESH)

    each(NX * NU - 1, lambda k: greet(far_peer(k)))
    each(NU * CORES - 1, lambda k: greet(near_peer(k)))

    for copy in inputs[:2]:
        copy.wait()
    wide_s = student_ref[...].astype(f32)
    wide_t = teacher_ref[...].astype(f32)
    s_inv = inverse_norm(wide_s)
    s_unit = wide_s * s_inv
    t_unit = wide_t * inverse_norm(wide_t)
    first[v, 0:OWN, :] = s_unit
    first[v, OWN : 2 * OWN, :] = t_unit

    def norm_block(i, _):
        at = pl.ds(pl.multiple_of(i * BLOCK, BLOCK), BLOCK)
        wide = proto_ref[at, :].astype(f32)
        inv = inverse_norm(wide)
        proto_inv[at, :] = jnp.broadcast_to(inv, (BLOCK, LANES))
        proto_hat[at, :] = (wide * inv).astype(bf16)
        return 0

    pl.semaphore_wait(barrier, NU * CORES - 1 + NX * NU - 1)

    def send_first(k):
        push(first.at[v], first.at[v], first_send, first_recv, device(x, u, turned(v, k, NU)))

    each(NU - 1, send_first)
    inputs[2].wait()
    lax.fori_loop(0, PROTOS // BLOCK, norm_block, 0)
    wait(first.at[pl.ds(0, NU - 1)], first_recv)
    for i in range(NU):
        stage[0, OWN * i : OWN * (i + 1), :] = first[i, 0:OWN, :]
        stage[1, OWN * i : OWN * (i + 1), :] = first[i, OWN : 2 * OWN, :]
    for h in range(2):
        at = slice(h * CUT, (h + 1) * CUT)
        gat_s[h, c, x, u] = stage[0, :, at].astype(bf16)
        gat_t[h, c, x, u] = stage[1, :, at].astype(bf16)

    def open_step(buf, n):
        def send_hi(k):
            block = buf.at[1, c, x, u]
            push(block, block, gat_send.at[n, 1], gat_recv.at[n, 1], device(turned(x, k, NX), u, v))

        def send_lo(k):
            block = buf.at[0, c, x, u]
            push(block, block, gat_send.at[n, 0], gat_recv.at[n, 0], device(x, turned(u, k, NU), v))

        each(NX - 1, send_hi)
        each(NU - 1, send_lo)

    def spread_hi(buf, n):
        def send(k):
            block = buf.at[1, c, :, u]
            push(block, block, gat_send.at[n, 2], gat_recv.at[n, 2], device(x, turned(u, k, NU), v))

        each(NU - 1, send)

    def spread_lo(buf, n):
        def send(k):
            block = buf.at[0, c, x]
            push(block, block, gat_send.at[n, 3], gat_recv.at[n, 3 + x], device(turned(x, k, NX), u, v))

        each(NX - 1, send)

    def opened_hi(buf, n):
        wait(buf.at[0, 0, 0, pl.ds(0, NX - 1)], gat_recv.at[n, 1])

    def opened_lo(buf, n):
        wait(buf.at[0, 0, 0, pl.ds(0, NU - 1)], gat_recv.at[n, 0])

    def relay(buf, n):
        for k in range(NX):
            px = turned(x, NX - 1 if k == 0 else k - 1, NX)
            if k > 0:
                wait(buf.at[0, 0, 0], gat_recv.at[n, 3 + px])
            push(buf.at[0, c, px], buf.at[0, c, px], swap_send.at[n], swap_recv.at[n], mate)
        wait(buf.at[0, 0, :, pl.ds(0, NU - 1)], gat_recv.at[n, 2])
        push(buf.at[1, c], buf.at[1, c], swap_send.at[n], swap_recv.at[n], mate)

    def settle(buf, n):
        wait(buf.at[:, 0], swap_recv.at[n])
        wait(buf.at[0, 0, 0, pl.ds(0, NU - 1)], gat_send.at[n, 0])
        wait(buf.at[0, 0, 0, pl.ds(0, NX - 1)], gat_send.at[n, 1])
        wait(buf.at[0, 0, :, pl.ds(0, NU - 1)], gat_send.at[n, 2])
        wait(buf.at[0, 0, pl.ds(0, NX - 1)], gat_send.at[n, 3])
        wait(buf.at[:, 0], swap_send.at[n])

    open_step(gat_t, 1)
    wait(first.at[pl.ds(0, NU - 1)], first_send)
    opened_hi(gat_t, 1)
    spread_hi(gat_t, 1)
    opened_lo(gat_t, 1)
    spread_lo(gat_t, 1)
    open_step(gat_s, 0)
    relay(gat_t, 1)

    def exponentials(buf, out, temp, core):
        for k in range(HALF // 256):
            at = pl.ds(pl.multiple_of(core * HALF + k * 256, 256), 256)
            px = k * 256 // SLAB
            product = sum(
                lax.dot_general(
                    proto_hat[:, h * CUT : (h + 1) * CUT],
                    buf[h, core, px : px + 256 // SLAB].reshape(256, CUT),
                    (((1,), (1,)), ((), ())),
                    preferred_element_type=f32,
                )
                for h in range(2)
            )
            out[:, at] = jnp.exp(product * (1.0 / temp))

    def folded(value):
        return jnp.sum(value.reshape(-1, 8, ROWS), axis=0)

    def flat(ref):
        return jnp.concatenate([ref[k : k + 1, :] for k in range(TALL)], axis=1)

    def put(dst, acc):
        for k in range(TALL):
            dst[k : k + 1, :] = jnp.sum(acc[:, k * LANES : (k + 1) * LANES], axis=0, keepdims=True)

    def sweep(scale):
        def body(i, acc):
            at = pl.ds(pl.multiple_of(i * SWEEP, SWEEP), SWEEP)
            e = e_t[at, :]
            weighed = e if scale is None else e * scale
            col = 1.0 / jnp.sum(weighed, axis=1, keepdims=True)
            cols[at, :] = jnp.broadcast_to(col, (SWEEP, LANES))
            return acc + folded(e * col)

        return lax.fori_loop(0, PROTOS // SWEEP, body, jnp.zeros((8, ROWS), f32))

    def near_start(n):
        me = z * CORES + c

        def send(k):
            push(near_src.at[n], near.at[n, me], near_send.at[n], near_recv.at[n], near_peer(k))

        each(NU * CORES - 1, send)
        near[n, me] = near_src[n]

    def near_end(n):
        for sem in (near_recv, near_send):
            wait(near.at[n, pl.ds(0, NU * CORES - 1)], sem.at[n])
        far_src[n] = jnp.sum(near[n], axis=0)

    def far_start(n):
        me = x * NU + y

        def send(k):
            push(far_src.at[n], far.at[n, me], far_send.at[n], far_recv.at[n], far_peer(k))

        each(NX * NU - 1, send)
        far[n, me] = far_src[n]

    def far_end(n):
        for sem in (far_recv, far_send):
            wait(far.at[n, pl.ds(0, NX * NU - 1)], sem.at[n])
        return 1.0 / jnp.sum(far[n], axis=0)

    def row_of(inverse):
        part[...] = inverse
        return flat(part)

    def student_sum(i, acc):
        at = pl.ds(pl.multiple_of(i * BLOCK, BLOCK), BLOCK)
        return acc + folded(e_s[at, :])

    exponentials(gat_t, e_t, teacher_temp, c)
    settle(gat_t, 1)
    exponentials(gat_t, e_t, teacher_temp, oc)
    put(near_src.at[0], sweep(None))
    near_start(0)
    push(proto_hat, proto_mate, mate_send.at[0], mate_recv.at[0], mate)
    opened_hi(gat_s, 0)
    opened_lo(gat_s, 0)
    spread_lo(gat_s, 0)
    pl.when(c == 1)(lambda: spread_hi(gat_s, 0))
    near_end(0)
    far_start(0)
    pl.when(c == 0)(lambda: spread_hi(gat_s, 0))
    row_scale = row_of(far_end(0))

    put(near_src.at[1], sweep(row_scale))
    near_start(1)
    relay(gat_s, 0)
    near_end(1)
    far_start(1)
    settle(gat_s, 0)
    for core in range(CORES):
        exponentials(gat_s, e_s, student_temp, core)
    student_part = lax.fori_loop(0, PROTOS // BLOCK, student_sum, jnp.zeros((8, ROWS), f32))
    for k in range(TALL):
        st_src[k] = jnp.sum(student_part[:, k * LANES : (k + 1) * LANES], axis=0, keepdims=True)

    def send_piece(k):
        pz = turned(z, k, NU)
        push(st_src.at[pz], st_near.at[z], st_send.at[0], st_recv.at[0], (x, y, pz, c))

    def send_sum(k):
        push(st_part, st_far.at[x * NU + y], st_send.at[1], st_recv.at[1], far_peer(k))

    def send_back(k):
        push(st_tot, st_all.at[z * CORES + c], st_send.at[2], st_recv.at[2], near_peer(k))

    each(NU - 1, send_piece)
    st_near[z] = st_src[z]
    for sem in (st_recv, st_send):
        wait(st_near.at[pl.ds(0, NU - 1)], sem.at[0])
    st_part[...] = jnp.sum(st_near[...], axis=0)
    each(NX * NU - 1, send_sum)
    st_far[x * NU + y] = st_part[...]
    row_scale = row_of(far_end(1))

    put(near_src.at[2], sweep(row_scale))
    near_start(2)
    near_end(2)
    far_start(2)
    for sem in (st_recv, st_send):
        wait(st_far.at[pl.ds(0, NX * NU - 1)], sem.at[1])
    st_tot[...] = jnp.sum(st_far[...], axis=0)
    each(NU * CORES - 1, send_back)
    st_all[z * CORES + c] = st_tot[...]
    for sem in (st_recv, st_send):
        wait(st_all.at[pl.ds(0, NU * CORES - 1)], sem.at[2])
    totals = [st_all[CORES * k] + st_all[CORES * k + 1] for k in range(TALL)]
    student_scale = (1.0 / jnp.concatenate(totals, axis=1)) * (1.0 / student_temp)

    def scale_block(i, _):
        at = pl.ds(pl.multiple_of(i * BLOCK, BLOCK), BLOCK)
        e_s[at, :] = e_s[at, :] * student_scale
        e_t[at, :] = e_t[at, :] * cols[at, 0:1]
        return 0

    lax.fori_loop(0, PROTOS // BLOCK, scale_block, 0)
    part[...] = far_end(2) * (1.0 / student_temp)

    def gradients(core):
        rows = [part[pl.ds(core * (TALL // CORES) + k, 1), :] for k in range(TALL // CORES)]
        scale = jnp.concatenate(rows, axis=1)
        lanes = pl.ds(pl.multiple_of(core * HALF, HALF), HALF)

        def body(i, _):
            at = pl.ds(pl.multiple_of(i * BLOCK, BLOCK), BLOCK)
            grad[core, at, :] = (e_s[at, lanes] - e_t[at, lanes] * scale).astype(bf16)
            return 0

        lax.fori_loop(0, PROTOS // BLOCK, body, 0)

    gradients(oc)
    push(grad.at[oc], grad_mate, mate_send.at[1], mate_recv.at[1], mate)
    gradients(c)

    def row_product(left, px, right):
        at = pl.ds(pl.multiple_of(px * SLAB, SLAB), SLAB)
        return lax.dot_general(left[:, at], right[...], (((0,), (0,)), ((), ())), preferred_element_type=f32)

    for px in range(NX):
        own[px] = row_product(grad.at[c], px, proto_hat)
    wait(proto_mate, mate_recv.at[0])
    wait(grad_mate, mate_recv.at[1])
    for k in range(NX):
        px = turned(x, k, NX)
        total = own[px] + row_product(grad_mate, px, proto_mate)
        xbuf[px] = total[:, :CUT]
        ubuf[px] = total[:, CUT:].reshape(NU, TILE, D - CUT)
        if k < NX - 1:
            push(xbuf.at[px], xslots.at[x], big_send.at[0], big_recv.at[0], device(px, u, v))

    def send_u(k):
        pu = turned(u, k, NU)
        push(ubuf.at[:, pu], uslots.at[u], big_send.at[1], big_recv.at[1], device(x, pu, v))

    each(NU - 1, send_u)
    xslots[x] = xbuf[x]
    uslots[u] = ubuf[:, u]

    def proto_block(i):
        at = slice(i * 256, (i + 1) * 256)
        halves = [
            sum(
                jnp.dot(grad[core, at, :], gat_s[h, core].reshape(HALF, CUT), preferred_element_type=f32)
                for core in range(CORES)
            )
            for h in range(2)
        ]
        step = jnp.concatenate(halves, axis=1)
        inv = proto_inv[at, 0:1]
        unit = proto_ref[at, :].astype(f32) * inv
        pgrad_ref[at, :] = (step - unit * jnp.sum(unit * step, axis=1, keepdims=True)) * inv

    for i in range(PROTOS // 256):
        proto_block(i)

    for sem in (big_recv, big_send):
        wait(xslots.at[pl.ds(0, NX - 1)], sem.at[0])
    xsum[...] = jnp.sum(xslots[...], axis=0)

    def send_xu(k):
        pu = turned(u, k, NU)
        src = xsum.at[pl.ds(pl.multiple_of(pu * TILE, TILE), TILE)]
        push(src, xuslots.at[u], end_send.at[0], end_recv.at[0], device(x, pu, v))

    each(NU - 1, send_xu)
    xuslots[u] = xsum[pl.ds(pl.multiple_of(u * TILE, TILE), TILE), :]

    for sem in (big_recv, big_send):
        wait(uslots.at[pl.ds(0, NU - 1)], sem.at[1])
    uxsrc[...] = jnp.sum(uslots[...], axis=0)

    def send_ux(k):
        px = turned(x, k, NX)
        push(uxsrc.at[px], uxslots.at[x], end_send.at[1], end_recv.at[1], device(px, u, v))

    each(NX - 1, send_ux)
    uxslots[x] = uxsrc[x]

    for sem in (end_recv, end_send):
        wait(xuslots.at[pl.ds(0, NU - 1)], sem.at[0])
    left = jnp.sum(xuslots[...], axis=0)
    for sem in (end_recv, end_send):
        wait(uxslots.at[pl.ds(0, NX - 1)], sem.at[1])
    right = jnp.sum(uxslots[...], axis=0)
    for pv in range(NU):
        at = slice(pv * OWN, (pv + 1) * OWN)
        vsrc[pv, :, :CUT] = left[at, :]
        vsrc[pv, :, CUT:] = right[at, :]

    def send_v(k):
        pv = turned(v, k, NU)
        push(vsrc.at[pv], vslots.at[v], end_send.at[2], end_recv.at[2], device(x, u, pv))

    each(NU - 1, send_v)
    vslots[v] = vsrc[v]
    for sem in (end_recv, end_send):
        wait(vslots.at[pl.ds(0, NU - 1)], sem.at[2])
    step = jnp.sum(vslots[...], axis=0)
    wait(proto_mate, mate_send.at[0])
    wait(grad_mate, mate_send.at[1])

    sgrad_ref[...] = (step - s_unit * jnp.sum(s_unit * step, axis=1, keepdims=True)) * s_inv


def on_device(student, teacher, protos):
    vmem = pl.BlockSpec(memory_space=pltpu.VMEM)
    dma = pltpu.SemaphoreType.DMA
    return pl.pallas_call(
        kernel,
        out_shape=(
            jax.ShapeDtypeStruct((OWN, D), f32),
            jax.ShapeDtypeStruct((PROTOS, D), f32),
        ),
        in_specs=[pl.BlockSpec(memory_space=pltpu.HBM)] * 3,
        out_specs=(vmem, vmem),
        scratch_shapes=[
            pltpu.VMEM((OWN, D), bf16),
            pltpu.VMEM((OWN, D), bf16),
            pltpu.VMEM((PROTOS, D), bf16),
            pltpu.VMEM((NU, 2 * OWN, D), f32),
            pltpu.VMEM((2, TILE, D), f32),
            pltpu.VMEM((2, CORES, NX, NU, TILE, CUT), bf16),
            pltpu.VMEM((2, CORES, NX, NU, TILE, CUT), bf16),
            pltpu.VMEM((PROTOS, D), bf16),
            pltpu.VMEM((PROTOS, LANES), f32),
            pltpu.VMEM((PROTOS, ROWS), f32),
            pltpu.VMEM((PROTOS, ROWS), f32),
            pltpu.VMEM((PROTOS, LANES), f32),
            pltpu.VMEM((CORES, PROTOS, HALF), bf16),
            pltpu.VMEM((SUMS, TALL, LANES), f32),
            pltpu.VMEM((SUMS, NU * CORES, TALL, LANES), f32),
            pltpu.VMEM((SUMS, TALL, LANES), f32),
            pltpu.VMEM((SUMS, NX * NU, TALL, LANES), f32),
            pltpu.VMEM((TALL, LANES), f32),
            pltpu.VMEM((NX, SLAB, D), f32),
            pltpu.VMEM((PROTOS, D), bf16),
            pltpu.VMEM((PROTOS, HALF), bf16),
            pltpu.VMEM((NX, SLAB, CUT), f32),
            pltpu.VMEM((NX, NU, TILE, D - CUT), f32),
            pltpu.VMEM((NX, SLAB, CUT), f32),
            pltpu.VMEM((NU, NX, TILE, D - CUT), f32),
            pltpu.VMEM((SLAB, CUT), f32),
            pltpu.VMEM((NU, TILE, CUT), f32),
            pltpu.VMEM((NX, TILE, D - CUT), f32),
            pltpu.VMEM((NX, TILE, D - CUT), f32),
            pltpu.VMEM((NU, OWN, D), f32),
            pltpu.VMEM((NU, OWN, D), f32),
            pltpu.VMEM((TALL, 1, LANES), f32),
            pltpu.VMEM((NU, 1, LANES), f32),
            pltpu.VMEM((1, LANES), f32),
            pltpu.VMEM((NX * NU, 1, LANES), f32),
            pltpu.VMEM((1, LANES), f32),
            pltpu.VMEM((NU * CORES, 1, LANES), f32),
            dma((3,)),
            dma,
            dma,
            dma((2, 4)),
            dma((2, 3 + NX)),
            dma((2,)),
            dma((2,)),
            dma((SUMS,)),
            dma((SUMS,)),
            dma((SUMS,)),
            dma((SUMS,)),
            dma((2,)),
            dma((2,)),
            dma((2,)),
            dma((2,)),
            dma((3,)),
            dma((3,)),
            dma((3,)),
            dma((3,)),
        ],
        compiler_params=pltpu.CompilerParams(
            collective_id=0, has_side_effects=True, vmem_limit_bytes=48 << 20
        ),
        name="prototype_head",
    )(*(pltpu.with_memory_space_constraint(a, pltpu.HBM) for a in (student, teacher, protos)))


def solution(mesh):
    torus = Mesh(mesh.devices.reshape(NX, NU, NU, CORES), AXES)
    return jax.shard_map(
        on_device,
        mesh=torus,
        in_specs=(P(AXES, None),) * 3,
        out_specs=(P(AXES, None), P(AXES, None)),
        check_vma=False,
    )
```

```python
import jax
import jax.numpy as jnp
from jax import lax
from jax.experimental import pallas as pl
from jax.experimental.pallas import tpu as pltpu
from jax.sharding import Mesh
from jax.sharding import PartitionSpec as P

MESH = pl.DeviceIdType.MESH
AXES = ("wide_0", "wide_1", "narrow_0", "narrow_1")
SUMS = 3
NX, NU, CORES = 4, 8, 2
D = 512
OWN = 2
ROWS = NX * NU * NU * CORES * OWN
HALF = ROWS // CORES
SLAB = HALF // NX
TILE = NU * OWN
PROTOS = 512
BLOCK = 128
SWEEP = 256
LANES = 128
TALL = ROWS // LANES
CUT = D // 2

epsilon = 1e-06
teacher_temp = 0.07
student_temp = 0.1

f32 = jnp.float32
bf16 = jnp.bfloat16


def each(n, act):
    for k in range(n):
        act(k)


def inverse_norm(wide):
    return lax.rsqrt(jnp.sum(wide * wide, axis=1, keepdims=True) + epsilon)


def kernel(
    student_hbm,
    teacher_hbm,
    proto_hbm,
    sgrad_ref,
    pgrad_ref,
    student_ref,
    teacher_ref,
    proto_ref,
    first,
    stage,
    gat_t,
    gat_s,
    proto_hat,
    proto_inv,
    e_t,
    e_s,
    cols,
    grad,
    near_src,
    near,
    far_src,
    far,
    part,
    proto_mate,
    grad_mate,
    xbuf,
    ubuf,
    xslots,
    uslots,
    xsum,
    xuslots,
    uxsrc,
    uxslots,
    vsrc,
    vslots,
    st_src,
    st_near,
    st_part,
    st_far,
    st_tot,
    st_all,
    load,
    first_send,
    first_recv,
    gat_send,
    gat_recv,
    swap_send,
    swap_recv,
    near_send,
    near_recv,
    far_send,
    far_recv,
    mate_send,
    mate_recv,
    grad_recv,
    big_send,
    big_recv,
    end_send,
    end_recv,
    st_send,
    st_recv,
):
    x, y, z, c = (lax.axis_index(a) for a in AXES)
    u = z + c * (y - z)
    v = y + c * (z - y)
    oc = 1 - c

    def device(px, pu, pv):
        return (px, pv + c * (pu - pv), pu + c * (pv - pu), c)

    mate = (x, y, z, oc)

    def turned(at, k, n):
        return lax.rem(at + (n // 2 + (1 - 2 * (k % 2)) * ((k + 1) // 2)), n)

    def near_peer(k):
        return (x, y, turned(z, k // CORES, NU), lax.rem(c + (1 + k % CORES), CORES))

    def far_peer(k):
        return (turned(x, k % NX, NX), turned(y, k // NX, NU), z, c)

    def wait(ref, sem):
        pltpu.make_async_copy(ref, ref, sem).wait()

    def push(src, dst, send, recv, target):
        pltpu.make_async_remote_copy(
            src_ref=src, dst_ref=dst, send_sem=send, recv_sem=recv, device_id=target, device_id_type=MESH
        ).start()

    inputs = [
        pltpu.make_async_copy(src, dst, load.at[i])
        for i, (src, dst) in enumerate(
            ((student_hbm, student_ref), (teacher_hbm, teacher_ref), (proto_hbm, proto_ref))
        )
    ]
    for copy in inputs:
        copy.start()

    barrier = pltpu.get_barrier_semaphore()

    def greet(target):
        pl.semaphore_signal(barrier, inc=1, device_id=target, device_id_type=MESH)

    each(NX * NU - 1, lambda k: greet(far_peer(k)))
    each(NU * CORES - 1, lambda k: greet(near_peer(k)))

    for copy in inputs[:2]:
        copy.wait()
    wide_s = student_ref[...].astype(f32)
    wide_t = teacher_ref[...].astype(f32)
    s_inv = inverse_norm(wide_s)
    s_unit = wide_s * s_inv
    t_unit = wide_t * inverse_norm(wide_t)
    first[v, 0:OWN, :] = s_unit
    first[v, OWN : 2 * OWN, :] = t_unit

    def norm_block(i, _):
        at = pl.ds(pl.multiple_of(i * BLOCK, BLOCK), BLOCK)
        wide = proto_ref[at, :].astype(f32)
        inv = inverse_norm(wide)
        proto_inv[at, :] = jnp.broadcast_to(inv, (BLOCK, LANES))
        proto_hat[at, :] = (wide * inv).astype(bf16)
        return 0

    pl.semaphore_wait(barrier, NU * CORES - 1 + NX * NU - 1)

    def send_first(k):
        push(first.at[v], first.at[v], first_send, first_recv, device(x, u, turned(v, k, NU)))

    each(NU - 1, send_first)
    inputs[2].wait()
    lax.fori_loop(0, PROTOS // BLOCK, norm_block, 0)
    wait(first.at[pl.ds(0, NU - 1)], first_recv)
    for i in range(NU):
        stage[0, OWN * i : OWN * (i + 1), :] = first[i, 0:OWN, :]
        stage[1, OWN * i : OWN * (i + 1), :] = first[i, OWN : 2 * OWN, :]
    for h in range(2):
        at = slice(h * CUT, (h + 1) * CUT)
        gat_s[h, c, x, u] = stage[0, :, at].astype(bf16)
        gat_t[h, c, x, u] = stage[1, :, at].astype(bf16)

    def open_step(buf, n):
        def send_hi(k):
            block = buf.at[1, c, x, u]
            push(block, block, gat_send.at[n, 1], gat_recv.at[n, 1], device(turned(x, k, NX), u, v))

        def send_lo(k):
            block = buf.at[0, c, x, u]
            push(block, block, gat_send.at[n, 0], gat_recv.at[n, 0], device(x, turned(u, k, NU), v))

        each(NX - 1, send_hi)
        each(NU - 1, send_lo)

    def spread_hi(buf, n):
        def send(k):
            block = buf.at[1, c, :, u]
            push(block, block, gat_send.at[n, 2], gat_recv.at[n, 2], device(x, turned(u, k, NU), v))

        each(NU - 1, send)

    def spread_lo(buf, n):
        def send(k):
            block = buf.at[0, c, x]
            push(block, block, gat_send.at[n, 3], gat_recv.at[n, 3 + x], device(turned(x, k, NX), u, v))

        each(NX - 1, send)

    def opened_hi(buf, n):
        wait(buf.at[0, 0, 0, pl.ds(0, NX - 1)], gat_recv.at[n, 1])

    def opened_lo(buf, n):
        wait(buf.at[0, 0, 0, pl.ds(0, NU - 1)], gat_recv.at[n, 0])

    def relay(buf, n):
        for k in range(NX):
            px = turned(x, NX - 1 if k == 0 else k - 1, NX)
            if k > 0:
                wait(buf.at[0, 0, 0], gat_recv.at[n, 3 + px])
            push(buf.at[0, c, px], buf.at[0, c, px], swap_send.at[n], swap_recv.at[n], mate)
        wait(buf.at[0, 0, :, pl.ds(0, NU - 1)], gat_recv.at[n, 2])
        push(buf.at[1, c], buf.at[1, c], swap_send.at[n], swap_recv.at[n], mate)

    def settle(buf, n):
        wait(buf.at[:, 0], swap_recv.at[n])
        wait(buf.at[0, 0, 0, pl.ds(0, NU - 1)], gat_send.at[n, 0])
        wait(buf.at[0, 0, 0, pl.ds(0, NX - 1)], gat_send.at[n, 1])
        wait(buf.at[0, 0, :, pl.ds(0, NU - 1)], gat_send.at[n, 2])
        wait(buf.at[0, 0, pl.ds(0, NX - 1)], gat_send.at[n, 3])
        wait(buf.at[:, 0], swap_send.at[n])

    open_step(gat_t, 1)
    wait(first.at[pl.ds(0, NU - 1)], first_send)
    opened_hi(gat_t, 1)
    spread_hi(gat_t, 1)
    opened_lo(gat_t, 1)
    spread_lo(gat_t, 1)
    open_step(gat_s, 0)
    relay(gat_t, 1)

    def exponentials(buf, out, temp, core):
        for k in range(HALF // 256):
            at = pl.ds(pl.multiple_of(core * HALF + k * 256, 256), 256)
            px = k * 256 // SLAB
            product = sum(
                lax.dot_general(
                    proto_hat[:, h * CUT : (h + 1) * CUT],
                    buf[h, core, px : px + 256 // SLAB].reshape(256, CUT),
                    (((1,), (1,)), ((), ())),
                    preferred_element_type=f32,
                )
                for h in range(2)
            )
            out[:, at] = jnp.exp(product * (1.0 / temp))

    def folded(value):
        return jnp.sum(value.reshape(-1, 8, ROWS), axis=0)

    def flat(ref):
        return jnp.concatenate([ref[k : k + 1, :] for k in range(TALL)], axis=1)

    def put(dst, acc):
        for k in range(TALL):
            dst[k : k + 1, :] = jnp.sum(acc[:, k * LANES : (k + 1) * LANES], axis=0, keepdims=True)

    def sweep(scale):
        def body(i, acc):
            at = pl.ds(pl.multiple_of(i * SWEEP, SWEEP), SWEEP)
            e = e_t[at, :]
            weighed = e if scale is None else e * scale
            col = 1.0 / jnp.sum(weighed, axis=1, keepdims=True)
            cols[at, :] = jnp.broadcast_to(col, (SWEEP, LANES))
            return acc + folded(e * col)

        return lax.fori_loop(0, PROTOS // SWEEP, body, jnp.zeros((8, ROWS), f32))

    def near_start(n):
        me = z * CORES + c

        def send(k):
            push(near_src.at[n], near.at[n, me], near_send.at[n], near_recv.at[n], near_peer(k))

        each(NU * CORES - 1, send)
        near[n, me] = near_src[n]

    def near_end(n):
        for sem in (near_recv, near_send):
            wait(near.at[n, pl.ds(0, NU * CORES - 1)], sem.at[n])
        far_src[n] = jnp.sum(near[n], axis=0)

    def far_start(n):
        me = x * NU + y

        def send(k):
            push(far_src.at[n], far.at[n, me], far_send.at[n], far_recv.at[n], far_peer(k))

        each(NX * NU - 1, send)
        far[n, me] = far_src[n]

    def far_end(n):
        for sem in (far_recv, far_send):
            wait(far.at[n, pl.ds(0, NX * NU - 1)], sem.at[n])
        return 1.0 / jnp.sum(far[n], axis=0)

    def row_of(inverse):
        part[...] = inverse
        return flat(part)

    def student_sum(i, acc):
        at = pl.ds(pl.multiple_of(i * BLOCK, BLOCK), BLOCK)
        return acc + folded(e_s[at, :])

    exponentials(gat_t, e_t, teacher_temp, c)
    settle(gat_t, 1)
    exponentials(gat_t, e_t, teacher_temp, oc)
    put(near_src.at[0], sweep(None))
    near_start(0)
    push(proto_hat, proto_mate, mate_send.at[0], mate_recv, mate)
    opened_hi(gat_s, 0)
    opened_lo(gat_s, 0)
    spread_lo(gat_s, 0)
    pl.when(c == 1)(lambda: spread_hi(gat_s, 0))
    near_end(0)
    far_start(0)
    pl.when(c == 0)(lambda: spread_hi(gat_s, 0))
    row_scale = row_of(far_end(0))

    put(near_src.at[1], sweep(row_scale))
    near_start(1)
    relay(gat_s, 0)
    near_end(1)
    far_start(1)
    settle(gat_s, 0)
    for core in range(CORES):
        exponentials(gat_s, e_s, student_temp, core)
    student_part = lax.fori_loop(0, PROTOS // BLOCK, student_sum, jnp.zeros((8, ROWS), f32))
    for k in range(TALL):
        st_src[k] = jnp.sum(student_part[:, k * LANES : (k + 1) * LANES], axis=0, keepdims=True)

    def send_piece(k):
        pz = turned(z, k, NU)
        push(st_src.at[pz], st_near.at[z], st_send.at[0], st_recv.at[0], (x, y, pz, c))

    def send_sum(k):
        push(st_part, st_far.at[x * NU + y], st_send.at[1], st_recv.at[1], far_peer(k))

    def send_back(k):
        push(st_tot, st_all.at[z * CORES + c], st_send.at[2], st_recv.at[2], near_peer(k))

    each(NU - 1, send_piece)
    st_near[z] = st_src[z]
    for sem in (st_recv, st_send):
        wait(st_near.at[pl.ds(0, NU - 1)], sem.at[0])
    st_part[...] = jnp.sum(st_near[...], axis=0)
    each(NX * NU - 1, send_sum)
    st_far[x * NU + y] = st_part[...]
    row_scale = row_of(far_end(1))

    put(near_src.at[2], sweep(row_scale))
    near_start(2)
    near_end(2)
    far_start(2)
    for sem in (st_recv, st_send):
        wait(st_far.at[pl.ds(0, NX * NU - 1)], sem.at[1])
    st_tot[...] = jnp.sum(st_far[...], axis=0)
    each(NU * CORES - 1, send_back)
    st_all[z * CORES + c] = st_tot[...]
    for sem in (st_recv, st_send):
        wait(st_all.at[pl.ds(0, NU * CORES - 1)], sem.at[2])
    totals = [st_all[CORES * k] + st_all[CORES * k + 1] for k in range(TALL)]
    student_scale = (1.0 / jnp.concatenate(totals, axis=1)) * (1.0 / student_temp)

    def scale_block(i, _):
        at = pl.ds(pl.multiple_of(i * BLOCK, BLOCK), BLOCK)
        e_s[at, :] = e_s[at, :] * student_scale
        e_t[at, :] = e_t[at, :] * cols[at, 0:1]
        return 0

    lax.fori_loop(0, PROTOS // BLOCK, scale_block, 0)
    part[...] = far_end(2) * (1.0 / student_temp)

    def gradients(core, px):
        lanes = pl.ds(pl.multiple_of(core * HALF + px * SLAB, SLAB), SLAB)
        scale = part[pl.ds(core * NX + px, 1), :]
        grad[core, px] = (e_s[:, lanes] - e_t[:, lanes] * scale).astype(bf16)

    def row_product(left, right):
        return lax.dot_general(left[...], right[...], (((0,), (0,)), ((), ())), preferred_element_type=f32)

    for k in range(NX):
        px = turned(x, k, NX)
        gradients(oc, px)
        push(grad.at[oc, px], grad_mate.at[px], mate_send.at[1], grad_recv.at[px], mate)
    wait(proto_mate, mate_recv)
    for k in range(NX):
        px = turned(x, k, NX)
        gradients(c, px)
        own = row_product(grad.at[c, px], proto_hat)
        wait(grad_mate.at[px], grad_recv.at[px])
        total = own + row_product(grad_mate.at[px], proto_mate)
        xbuf[px] = total[:, :CUT]
        ubuf[px] = total[:, CUT:].reshape(NU, TILE, D - CUT)
        if k < NX - 1:
            push(xbuf.at[px], xslots.at[x], big_send.at[0], big_recv.at[0], device(px, u, v))

    def send_u(k):
        pu = turned(u, k, NU)
        push(ubuf.at[:, pu], uslots.at[u], big_send.at[1], big_recv.at[1], device(x, pu, v))

    each(NU - 1, send_u)
    xslots[x] = xbuf[x]
    uslots[u] = ubuf[:, u]

    def proto_block(i):
        at = slice(i * 256, (i + 1) * 256)
        halves = [0.0, 0.0]
        for core in range(CORES):
            for px in range(0, NX, 2):
                left = jnp.concatenate([grad[core, px, at, :], grad[core, px + 1, at, :]], axis=1)
                for h in range(2):
                    right = gat_s[h, core, px : px + 2].reshape(2 * SLAB, CUT)
                    halves[h] += jnp.dot(left, right, preferred_element_type=f32)
        step = jnp.concatenate(halves, axis=1)
        inv = proto_inv[at, 0:1]
        unit = proto_ref[at, :].astype(f32) * inv
        pgrad_ref[at, :] = (step - unit * jnp.sum(unit * step, axis=1, keepdims=True)) * inv

    for i in range(PROTOS // 256):
        proto_block(i)

    for sem in (big_recv, big_send):
        wait(xslots.at[pl.ds(0, NX - 1)], sem.at[0])
    xsum[...] = jnp.sum(xslots[...], axis=0)

    def send_xu(k):
        pu = turned(u, k, NU)
        src = xsum.at[pl.ds(pl.multiple_of(pu * TILE, TILE), TILE)]
        push(src, xuslots.at[u], end_send.at[0], end_recv.at[0], device(x, pu, v))

    each(NU - 1, send_xu)
    xuslots[u] = xsum[pl.ds(pl.multiple_of(u * TILE, TILE), TILE), :]

    for sem in (big_recv, big_send):
        wait(uslots.at[pl.ds(0, NU - 1)], sem.at[1])
    uxsrc[...] = jnp.sum(uslots[...], axis=0)

    def send_ux(k):
        px = turned(x, k, NX)
        push(uxsrc.at[px], uxslots.at[x], end_send.at[1], end_recv.at[1], device(px, u, v))

    each(NX - 1, send_ux)
    uxslots[x] = uxsrc[x]

    for sem in (end_recv, end_send):
        wait(xuslots.at[pl.ds(0, NU - 1)], sem.at[0])
    left = jnp.sum(xuslots[...], axis=0)
    for sem in (end_recv, end_send):
        wait(uxslots.at[pl.ds(0, NX - 1)], sem.at[1])
    right = jnp.sum(uxslots[...], axis=0)
    for pv in range(NU):
        at = slice(pv * OWN, (pv + 1) * OWN)
        vsrc[pv, :, :CUT] = left[at, :]
        vsrc[pv, :, CUT:] = right[at, :]

    def send_v(k):
        pv = turned(v, k, NU)
        push(vsrc.at[pv], vslots.at[v], end_send.at[2], end_recv.at[2], device(x, u, pv))

    each(NU - 1, send_v)
    vslots[v] = vsrc[v]
    for sem in (end_recv, end_send):
        wait(vslots.at[pl.ds(0, NU - 1)], sem.at[2])
    step = jnp.sum(vslots[...], axis=0)
    wait(proto_mate, mate_send.at[0])
    wait(grad_mate, mate_send.at[1])

    sgrad_ref[...] = (step - s_unit * jnp.sum(s_unit * step, axis=1, keepdims=True)) * s_inv


def on_device(student, teacher, protos):
    vmem = pl.BlockSpec(memory_space=pltpu.VMEM)
    dma = pltpu.SemaphoreType.DMA
    return pl.pallas_call(
        kernel,
        out_shape=(
            jax.ShapeDtypeStruct((OWN, D), f32),
            jax.ShapeDtypeStruct((PROTOS, D), f32),
        ),
        in_specs=[pl.BlockSpec(memory_space=pltpu.HBM)] * 3,
        out_specs=(vmem, vmem),
        scratch_shapes=[
            pltpu.VMEM((OWN, D), bf16),
            pltpu.VMEM((OWN, D), bf16),
            pltpu.VMEM((PROTOS, D), bf16),
            pltpu.VMEM((NU, 2 * OWN, D), f32),
            pltpu.VMEM((2, TILE, D), f32),
            pltpu.VMEM((2, CORES, NX, NU, TILE, CUT), bf16),
            pltpu.VMEM((2, CORES, NX, NU, TILE, CUT), bf16),
            pltpu.VMEM((PROTOS, D), bf16),
            pltpu.VMEM((PROTOS, LANES), f32),
            pltpu.VMEM((PROTOS, ROWS), f32),
            pltpu.VMEM((PROTOS, ROWS), f32),
            pltpu.VMEM((PROTOS, LANES), f32),
            pltpu.VMEM((CORES, NX, PROTOS, SLAB), bf16),
            pltpu.VMEM((SUMS, TALL, LANES), f32),
            pltpu.VMEM((SUMS, NU * CORES, TALL, LANES), f32),
            pltpu.VMEM((SUMS, TALL, LANES), f32),
            pltpu.VMEM((SUMS, NX * NU, TALL, LANES), f32),
            pltpu.VMEM((TALL, LANES), f32),
            pltpu.VMEM((PROTOS, D), bf16),
            pltpu.VMEM((NX, PROTOS, SLAB), bf16),
            pltpu.VMEM((NX, SLAB, CUT), f32),
            pltpu.VMEM((NX, NU, TILE, D - CUT), f32),
            pltpu.VMEM((NX, SLAB, CUT), f32),
            pltpu.VMEM((NU, NX, TILE, D - CUT), f32),
            pltpu.VMEM((SLAB, CUT), f32),
            pltpu.VMEM((NU, TILE, CUT), f32),
            pltpu.VMEM((NX, TILE, D - CUT), f32),
            pltpu.VMEM((NX, TILE, D - CUT), f32),
            pltpu.VMEM((NU, OWN, D), f32),
            pltpu.VMEM((NU, OWN, D), f32),
            pltpu.VMEM((TALL, 1, LANES), f32),
            pltpu.VMEM((NU, 1, LANES), f32),
            pltpu.VMEM((1, LANES), f32),
            pltpu.VMEM((NX * NU, 1, LANES), f32),
            pltpu.VMEM((1, LANES), f32),
            pltpu.VMEM((NU * CORES, 1, LANES), f32),
            dma((3,)),
            dma,
            dma,
            dma((2, 4)),
            dma((2, 3 + NX)),
            dma((2,)),
            dma((2,)),
            dma((SUMS,)),
            dma((SUMS,)),
            dma((SUMS,)),
            dma((SUMS,)),
            dma((2,)),
            dma,
            dma((NX,)),
            dma((2,)),
            dma((2,)),
            dma((3,)),
            dma((3,)),
            dma((3,)),
            dma((3,)),
        ],
        compiler_params=pltpu.CompilerParams(
            collective_id=0, has_side_effects=True, vmem_limit_bytes=48 << 20
        ),
        name="prototype_head",
    )(*(pltpu.with_memory_space_constraint(a, pltpu.HBM) for a in (student, teacher, protos)))


def solution(mesh):
    torus = Mesh(mesh.devices.reshape(NX, NU, NU, CORES), AXES)
    return jax.shard_map(
        on_device,
        mesh=torus,
        in_specs=(P(AXES, None),) * 3,
        out_specs=(P(AXES, None), P(AXES, None)),
        check_vma=False,
    )
```

```python
import jax
import jax.numpy as jnp
from jax import lax
from jax.experimental import pallas as pl
from jax.experimental.pallas import tpu as pltpu
from jax.sharding import Mesh
from jax.sharding import PartitionSpec as P

MESH = pl.DeviceIdType.MESH
AXES = ("wide_0", "wide_1", "narrow_0", "narrow_1")
SUMS = 3
NX, NU, CORES = 4, 8, 2
D = 512
OWN = 2
ROWS = NX * NU * NU * CORES * OWN
HALF = ROWS // CORES
SLAB = HALF // NX
TILE = NU * OWN
PROTOS = 512
BLOCK = 128
SWEEP = 256
LANES = 128
TALL = ROWS // LANES
CUT = D // 2

epsilon = 1e-06
teacher_temp = 0.07
student_temp = 0.1

f32 = jnp.float32
bf16 = jnp.bfloat16


def each(n, act):
    for k in range(n):
        act(k)


def inverse_norm(wide):
    return lax.rsqrt(jnp.sum(wide * wide, axis=1, keepdims=True) + epsilon)


def kernel(
    student_hbm,
    teacher_hbm,
    proto_hbm,
    sgrad_ref,
    pgrad_ref,
    student_ref,
    teacher_ref,
    proto_ref,
    first,
    stage,
    gat_t,
    gat_s,
    proto_hat,
    proto_inv,
    e_t,
    e_s,
    cols,
    grad,
    near_src,
    near,
    far_src,
    far,
    part,
    proto_mate,
    grad_mate,
    xbuf,
    ubuf,
    xslots,
    uslots,
    xsum,
    xuslots,
    uxsrc,
    uxslots,
    vsrc,
    vslots,
    st_src,
    st_near,
    st_part,
    st_far,
    st_tot,
    st_all,
    load,
    first_send,
    first_recv,
    gat_send,
    gat_recv,
    swap_send,
    swap_recv,
    near_send,
    near_recv,
    far_send,
    far_recv,
    mate_send,
    mate_recv,
    grad_recv,
    big_send,
    big_recv,
    end_send,
    end_recv,
    st_send,
    st_recv,
):
    x, y, z, c = (lax.axis_index(a) for a in AXES)
    u = z + c * (y - z)
    v = y + c * (z - y)
    oc = 1 - c

    def device(px, pu, pv):
        return (px, pv + c * (pu - pv), pu + c * (pv - pu), c)

    mate = (x, y, z, oc)

    def turned(at, k, n):
        return lax.rem(at + (n // 2 + (1 - 2 * (k % 2)) * ((k + 1) // 2)), n)

    def near_peer(k):
        return (x, y, turned(z, k // CORES, NU), lax.rem(c + (1 + k % CORES), CORES))

    def far_peer(k):
        return (turned(x, k % NX, NX), turned(y, k // NX, NU), z, c)

    def wait(ref, sem):
        pltpu.make_async_copy(ref, ref, sem).wait()

    def push(src, dst, send, recv, target):
        pltpu.make_async_remote_copy(
            src_ref=src, dst_ref=dst, send_sem=send, recv_sem=recv, device_id=target, device_id_type=MESH
        ).start()

    inputs = [
        pltpu.make_async_copy(src, dst, load.at[i])
        for i, (src, dst) in enumerate(
            ((student_hbm, student_ref), (teacher_hbm, teacher_ref), (proto_hbm, proto_ref))
        )
    ]
    for copy in inputs:
        copy.start()

    barrier = pltpu.get_barrier_semaphore()

    def greet(target):
        pl.semaphore_signal(barrier, inc=1, device_id=target, device_id_type=MESH)

    each(NX * NU - 1, lambda k: greet(far_peer(k)))
    each(NU * CORES - 1, lambda k: greet(near_peer(k)))

    for copy in inputs[:2]:
        copy.wait()
    wide_s = student_ref[...].astype(f32)
    wide_t = teacher_ref[...].astype(f32)
    s_inv = inverse_norm(wide_s)
    s_unit = wide_s * s_inv
    t_unit = wide_t * inverse_norm(wide_t)
    first[v, 0:OWN, :] = s_unit
    first[v, OWN : 2 * OWN, :] = t_unit

    def norm_block(i, _):
        at = pl.ds(pl.multiple_of(i * BLOCK, BLOCK), BLOCK)
        wide = proto_ref[at, :].astype(f32)
        inv = inverse_norm(wide)
        proto_inv[at, :] = jnp.broadcast_to(inv, (BLOCK, LANES))
        proto_hat[at, :] = (wide * inv).astype(bf16)
        return 0

    pl.semaphore_wait(barrier, NU * CORES - 1 + NX * NU - 1)

    def send_first(k):
        push(first.at[v], first.at[v], first_send, first_recv, device(x, u, turned(v, k, NU)))

    each(NU - 1, send_first)
    inputs[2].wait()
    lax.fori_loop(0, PROTOS // BLOCK, norm_block, 0)
    wait(first.at[pl.ds(0, NU - 1)], first_recv)
    for i in range(NU):
        stage[0, OWN * i : OWN * (i + 1), :] = first[i, 0:OWN, :]
        stage[1, OWN * i : OWN * (i + 1), :] = first[i, OWN : 2 * OWN, :]
    for h in range(2):
        at = slice(h * CUT, (h + 1) * CUT)
        gat_s[h, c, x, u] = stage[0, :, at].astype(bf16)
        gat_t[h, c, x, u] = stage[1, :, at].astype(bf16)

    def open_step(buf, n):
        def send_hi(k):
            block = buf.at[1, c, x, u]
            push(block, block, gat_send.at[n, 1], gat_recv.at[n, 1], device(turned(x, k, NX), u, v))

        def send_lo(k):
            block = buf.at[0, c, x, u]
            push(block, block, gat_send.at[n, 0], gat_recv.at[n, 0], device(x, turned(u, k, NU), v))

        each(NX - 1, send_hi)
        each(NU - 1, send_lo)

    def spread_hi(buf, n):
        def send(k):
            block = buf.at[1, c, :, u]
            push(block, block, gat_send.at[n, 2], gat_recv.at[n, 2], device(x, turned(u, k, NU), v))

        each(NU - 1, send)

    def spread_lo(buf, n):
        def send(k):
            block = buf.at[0, c, x]
            push(block, block, gat_send.at[n, 3], gat_recv.at[n, 3 + x], device(turned(x, k, NX), u, v))

        each(NX - 1, send)

    def opened_hi(buf, n):
        wait(buf.at[0, 0, 0, pl.ds(0, NX - 1)], gat_recv.at[n, 1])

    def opened_lo(buf, n):
        wait(buf.at[0, 0, 0, pl.ds(0, NU - 1)], gat_recv.at[n, 0])

    def relay(buf, n):
        for k in range(NX):
            px = turned(x, NX - 1 if k == 0 else k - 1, NX)
            if k > 0:
                wait(buf.at[0, 0, 0], gat_recv.at[n, 3 + px])
            push(buf.at[0, c, px], buf.at[0, c, px], swap_send.at[n], swap_recv.at[n], mate)
        wait(buf.at[0, 0, :, pl.ds(0, NU - 1)], gat_recv.at[n, 2])
        push(buf.at[1, c], buf.at[1, c], swap_send.at[n], swap_recv.at[n], mate)

    def settle(buf, n):
        wait(buf.at[:, 0], swap_recv.at[n])
        wait(buf.at[0, 0, 0, pl.ds(0, NU - 1)], gat_send.at[n, 0])
        wait(buf.at[0, 0, 0, pl.ds(0, NX - 1)], gat_send.at[n, 1])
        wait(buf.at[0, 0, :, pl.ds(0, NU - 1)], gat_send.at[n, 2])
        wait(buf.at[0, 0, pl.ds(0, NX - 1)], gat_send.at[n, 3])
        wait(buf.at[:, 0], swap_send.at[n])

    open_step(gat_t, 1)
    wait(first.at[pl.ds(0, NU - 1)], first_send)
    opened_hi(gat_t, 1)
    spread_hi(gat_t, 1)
    opened_lo(gat_t, 1)
    spread_lo(gat_t, 1)
    relay(gat_t, 1)
    open_step(gat_s, 0)

    def exponentials(buf, out, temp, core):
        for k in range(HALF // 256):
            at = pl.ds(pl.multiple_of(core * HALF + k * 256, 256), 256)
            px = k * 256 // SLAB
            product = sum(
                lax.dot_general(
                    proto_hat[:, h * CUT : (h + 1) * CUT],
                    buf[h, core, px : px + 256 // SLAB].reshape(256, CUT),
                    (((1,), (1,)), ((), ())),
                    preferred_element_type=f32,
                )
                for h in range(2)
            )
            out[:, at] = jnp.exp(product * (1.0 / temp))

    def folded(value):
        return jnp.sum(value.reshape(-1, 8, ROWS), axis=0)

    def flat(ref):
        return jnp.concatenate([ref[k : k + 1, :] for k in range(TALL)], axis=1)

    def put(dst, acc):
        for k in range(TALL):
            dst[k : k + 1, :] = jnp.sum(acc[:, k * LANES : (k + 1) * LANES], axis=0, keepdims=True)

    def sweep(scale):
        def body(i, acc):
            at = pl.ds(pl.multiple_of(i * SWEEP, SWEEP), SWEEP)
            e = e_t[at, :]
            weighed = e if scale is None else e * scale
            col = 1.0 / jnp.sum(weighed, axis=1, keepdims=True)
            cols[at, :] = jnp.broadcast_to(col, (SWEEP, LANES))
            return acc + folded(e * col)

        return lax.fori_loop(0, PROTOS // SWEEP, body, jnp.zeros((8, ROWS), f32))

    def near_start(n):
        me = z * CORES + c

        def send(k):
            push(near_src.at[n], near.at[n, me], near_send.at[n], near_recv.at[n], near_peer(k))

        each(NU * CORES - 1, send)
        near[n, me] = near_src[n]

    def near_end(n):
        for sem in (near_recv, near_send):
            wait(near.at[n, pl.ds(0, NU * CORES - 1)], sem.at[n])
        far_src[n] = jnp.sum(near[n], axis=0)

    def far_start(n):
        me = x * NU + y

        def send(k):
            push(far_src.at[n], far.at[n, me], far_send.at[n], far_recv.at[n], far_peer(k))

        each(NX * NU - 1, send)
        far[n, me] = far_src[n]

    def far_end(n):
        for sem in (far_recv, far_send):
            wait(far.at[n, pl.ds(0, NX * NU - 1)], sem.at[n])
        return 1.0 / jnp.sum(far[n], axis=0)

    def row_of(inverse):
        part[...] = inverse
        return flat(part)

    def student_sum(i, acc):
        at = pl.ds(pl.multiple_of(i * BLOCK, BLOCK), BLOCK)
        return acc + folded(e_s[at, :])

    exponentials(gat_t, e_t, teacher_temp, c)
    settle(gat_t, 1)
    exponentials(gat_t, e_t, teacher_temp, oc)
    put(near_src.at[0], sweep(None))
    near_start(0)
    push(proto_hat, proto_mate, mate_send.at[0], mate_recv, mate)
    opened_hi(gat_s, 0)
    opened_lo(gat_s, 0)
    spread_lo(gat_s, 0)
    pl.when(c == 1)(lambda: spread_hi(gat_s, 0))
    near_end(0)
    far_start(0)
    pl.when(c == 0)(lambda: spread_hi(gat_s, 0))
    row_scale = row_of(far_end(0))

    put(near_src.at[1], sweep(row_scale))
    near_start(1)
    relay(gat_s, 0)
    near_end(1)
    far_start(1)
    settle(gat_s, 0)
    for core in range(CORES):
        exponentials(gat_s, e_s, student_temp, core)
    student_part = lax.fori_loop(0, PROTOS // BLOCK, student_sum, jnp.zeros((8, ROWS), f32))
    for k in range(TALL):
        st_src[k] = jnp.sum(student_part[:, k * LANES : (k + 1) * LANES], axis=0, keepdims=True)

    def send_piece(k):
        pz = turned(z, k, NU)
        push(st_src.at[pz], st_near.at[z], st_send.at[0], st_recv.at[0], (x, y, pz, c))

    def send_sum(k):
        push(st_part, st_far.at[x * NU + y], st_send.at[1], st_recv.at[1], far_peer(k))

    def send_back(k):
        push(st_tot, st_all.at[z * CORES + c], st_send.at[2], st_recv.at[2], near_peer(k))

    each(NU - 1, send_piece)
    st_near[z] = st_src[z]
    for sem in (st_recv, st_send):
        wait(st_near.at[pl.ds(0, NU - 1)], sem.at[0])
    st_part[...] = jnp.sum(st_near[...], axis=0)
    each(NX * NU - 1, send_sum)
    st_far[x * NU + y] = st_part[...]
    row_scale = row_of(far_end(1))

    put(near_src.at[2], sweep(row_scale))
    near_start(2)
    near_end(2)
    far_start(2)
    for sem in (st_recv, st_send):
        wait(st_far.at[pl.ds(0, NX * NU - 1)], sem.at[1])
    st_tot[...] = jnp.sum(st_far[...], axis=0)
    each(NU * CORES - 1, send_back)
    st_all[z * CORES + c] = st_tot[...]
    for sem in (st_recv, st_send):
        wait(st_all.at[pl.ds(0, NU * CORES - 1)], sem.at[2])
    totals = [st_all[CORES * k] + st_all[CORES * k + 1] for k in range(TALL)]
    student_scale = (1.0 / jnp.concatenate(totals, axis=1)) * (1.0 / student_temp)

    def scale_block(i, _):
        at = pl.ds(pl.multiple_of(i * BLOCK, BLOCK), BLOCK)
        e_s[at, :] = e_s[at, :] * student_scale
        e_t[at, :] = e_t[at, :] * cols[at, 0:1]
        return 0

    lax.fori_loop(0, PROTOS // BLOCK, scale_block, 0)
    part[...] = far_end(2) * (1.0 / student_temp)

    def gradients(core, px):
        lanes = pl.ds(pl.multiple_of(core * HALF + px * SLAB, SLAB), SLAB)
        scale = part[pl.ds(core * NX + px, 1), :]
        grad[core, px] = (e_s[:, lanes] - e_t[:, lanes] * scale).astype(bf16)

    def row_product(left, right):
        return lax.dot_general(left[...], right[...], (((0,), (0,)), ((), ())), preferred_element_type=f32)

    for k in range(NX):
        px = turned(x, k, NX)
        gradients(oc, px)
        push(grad.at[oc, px], grad_mate.at[px], mate_send.at[1], grad_recv.at[px], mate)
    wait(proto_mate, mate_recv)
    for k in range(NX):
        px = turned(x, k, NX)
        gradients(c, px)
        own = row_product(grad.at[c, px], proto_hat)
        wait(grad_mate.at[px], grad_recv.at[px])
        total = own + row_product(grad_mate.at[px], proto_mate)
        xbuf[px] = total[:, :CUT]
        ubuf[px] = total[:, CUT:].reshape(NU, TILE, D - CUT)
        if k < NX - 1:
            push(xbuf.at[px], xslots.at[x], big_send.at[0], big_recv.at[0], device(px, u, v))

    def send_u(k):
        pu = turned(u, k, NU)
        push(ubuf.at[:, pu], uslots.at[u], big_send.at[1], big_recv.at[1], device(x, pu, v))

    each(NU - 1, send_u)
    xslots[x] = xbuf[x]
    uslots[u] = ubuf[:, u]

    def proto_block(i):
        at = slice(i * 256, (i + 1) * 256)
        halves = [0.0, 0.0]
        for core in range(CORES):
            for px in range(0, NX, 2):
                left = jnp.concatenate([grad[core, px, at, :], grad[core, px + 1, at, :]], axis=1)
                for h in range(2):
                    right = gat_s[h, core, px : px + 2].reshape(2 * SLAB, CUT)
                    halves[h] += jnp.dot(left, right, preferred_element_type=f32)
        step = jnp.concatenate(halves, axis=1)
        inv = proto_inv[at, 0:1]
        unit = proto_ref[at, :].astype(f32) * inv
        pgrad_ref[at, :] = (step - unit * jnp.sum(unit * step, axis=1, keepdims=True)) * inv

    for i in range(PROTOS // 256):
        proto_block(i)

    for sem in (big_recv, big_send):
        wait(xslots.at[pl.ds(0, NX - 1)], sem.at[0])
    xsum[...] = jnp.sum(xslots[...], axis=0)

    def send_xu(k):
        pu = turned(u, k, NU)
        src = xsum.at[pl.ds(pl.multiple_of(pu * TILE, TILE), TILE)]
        push(src, xuslots.at[u], end_send.at[0], end_recv.at[0], device(x, pu, v))

    each(NU - 1, send_xu)
    xuslots[u] = xsum[pl.ds(pl.multiple_of(u * TILE, TILE), TILE), :]

    for sem in (big_recv, big_send):
        wait(uslots.at[pl.ds(0, NU - 1)], sem.at[1])
    uxsrc[...] = jnp.sum(uslots[...], axis=0)

    def send_ux(k):
        px = turned(x, k, NX)
        push(uxsrc.at[px], uxslots.at[x], end_send.at[1], end_recv.at[1], device(px, u, v))

    each(NX - 1, send_ux)
    uxslots[x] = uxsrc[x]

    for sem in (end_recv, end_send):
        wait(xuslots.at[pl.ds(0, NU - 1)], sem.at[0])
    left = jnp.sum(xuslots[...], axis=0)
    for sem in (end_recv, end_send):
        wait(uxslots.at[pl.ds(0, NX - 1)], sem.at[1])
    right = jnp.sum(uxslots[...], axis=0)
    for pv in range(NU):
        at = slice(pv * OWN, (pv + 1) * OWN)
        vsrc[pv, :, :CUT] = left[at, :]
        vsrc[pv, :, CUT:] = right[at, :]

    def send_v(k):
        pv = turned(v, k, NU)
        push(vsrc.at[pv], vslots.at[v], end_send.at[2], end_recv.at[2], device(x, u, pv))

    each(NU - 1, send_v)
    vslots[v] = vsrc[v]
    for sem in (end_recv, end_send):
        wait(vslots.at[pl.ds(0, NU - 1)], sem.at[2])
    step = jnp.sum(vslots[...], axis=0)
    wait(proto_mate, mate_send.at[0])
    wait(grad_mate, mate_send.at[1])

    sgrad_ref[...] = (step - s_unit * jnp.sum(s_unit * step, axis=1, keepdims=True)) * s_inv


def on_device(student, teacher, protos):
    vmem = pl.BlockSpec(memory_space=pltpu.VMEM)
    dma = pltpu.SemaphoreType.DMA
    return pl.pallas_call(
        kernel,
        out_shape=(
            jax.ShapeDtypeStruct((OWN, D), f32),
            jax.ShapeDtypeStruct((PROTOS, D), f32),
        ),
        in_specs=[pl.BlockSpec(memory_space=pltpu.HBM)] * 3,
        out_specs=(vmem, vmem),
        scratch_shapes=[
            pltpu.VMEM((OWN, D), bf16),
            pltpu.VMEM((OWN, D), bf16),
            pltpu.VMEM((PROTOS, D), bf16),
            pltpu.VMEM((NU, 2 * OWN, D), f32),
            pltpu.VMEM((2, TILE, D), f32),
            pltpu.VMEM((2, CORES, NX, NU, TILE, CUT), bf16),
            pltpu.VMEM((2, CORES, NX, NU, TILE, CUT), bf16),
            pltpu.VMEM((PROTOS, D), bf16),
            pltpu.VMEM((PROTOS, LANES), f32),
            pltpu.VMEM((PROTOS, ROWS), f32),
            pltpu.VMEM((PROTOS, ROWS), f32),
            pltpu.VMEM((PROTOS, LANES), f32),
            pltpu.VMEM((CORES, NX, PROTOS, SLAB), bf16),
            pltpu.VMEM((SUMS, TALL, LANES), f32),
            pltpu.VMEM((SUMS, NU * CORES, TALL, LANES), f32),
            pltpu.VMEM((SUMS, TALL, LANES), f32),
            pltpu.VMEM((SUMS, NX * NU, TALL, LANES), f32),
            pltpu.VMEM((TALL, LANES), f32),
            pltpu.VMEM((PROTOS, D), bf16),
            pltpu.VMEM((NX, PROTOS, SLAB), bf16),
            pltpu.VMEM((NX, SLAB, CUT), f32),
            pltpu.VMEM((NX, NU, TILE, D - CUT), f32),
            pltpu.VMEM((NX, SLAB, CUT), f32),
            pltpu.VMEM((NU, NX, TILE, D - CUT), f32),
            pltpu.VMEM((SLAB, CUT), f32),
            pltpu.VMEM((NU, TILE, CUT), f32),
            pltpu.VMEM((NX, TILE, D - CUT), f32),
            pltpu.VMEM((NX, TILE, D - CUT), f32),
            pltpu.VMEM((NU, OWN, D), f32),
            pltpu.VMEM((NU, OWN, D), f32),
            pltpu.VMEM((TALL, 1, LANES), f32),
            pltpu.VMEM((NU, 1, LANES), f32),
            pltpu.VMEM((1, LANES), f32),
            pltpu.VMEM((NX * NU, 1, LANES), f32),
            pltpu.VMEM((1, LANES), f32),
            pltpu.VMEM((NU * CORES, 1, LANES), f32),
            dma((3,)),
            dma,
            dma,
            dma((2, 4)),
            dma((2, 3 + NX)),
            dma((2,)),
            dma((2,)),
            dma((SUMS,)),
            dma((SUMS,)),
            dma((SUMS,)),
            dma((SUMS,)),
            dma((2,)),
            dma,
            dma((NX,)),
            dma((2,)),
            dma((2,)),
            dma((3,)),
            dma((3,)),
            dma((3,)),
            dma((3,)),
        ],
        compiler_params=pltpu.CompilerParams(
            collective_id=0, has_side_effects=True, vmem_limit_bytes=48 << 20
        ),
        name="prototype_head",
    )(*(pltpu.with_memory_space_constraint(a, pltpu.HBM) for a in (student, teacher, protos)))


def solution(mesh):
    torus = Mesh(mesh.devices.reshape(NX, NU, NU, CORES), AXES)
    return jax.shard_map(
        on_device,
        mesh=torus,
        in_specs=(P(AXES, None),) * 3,
        out_specs=(P(AXES, None), P(AXES, None)),
        check_vma=False,
    )
```

```python
import jax
import jax.numpy as jnp
from jax import lax
from jax.experimental import pallas as pl
from jax.experimental.pallas import tpu as pltpu
from jax.sharding import Mesh
from jax.sharding import PartitionSpec as P

MESH = pl.DeviceIdType.MESH
AXES = ("wide_0", "wide_1", "narrow_0", "narrow_1")
SUMS = 3
NX, NU, CORES = 4, 8, 2
D = 512
OWN = 2
ROWS = NX * NU * NU * CORES * OWN
HALF = ROWS // CORES
SLAB = HALF // NX
TILE = NU * OWN
PROTOS = 512
BLOCK = 128
SWEEP = 256
LANES = 128
TALL = ROWS // LANES
CUT = D // 2

epsilon = 1e-06
teacher_temp = 0.07
student_temp = 0.1

f32 = jnp.float32
bf16 = jnp.bfloat16


def each(n, act):
    for k in range(n):
        act(k)


def inverse_norm(wide):
    return lax.rsqrt(jnp.sum(wide * wide, axis=1, keepdims=True) + epsilon)


def kernel(
    student_hbm,
    teacher_hbm,
    proto_hbm,
    sgrad_ref,
    pgrad_ref,
    student_ref,
    teacher_ref,
    proto_ref,
    first,
    stage,
    gat_t,
    gat_s,
    proto_hat,
    proto_inv,
    e_t,
    e_s,
    cols,
    grad,
    near_src,
    near,
    far_src,
    far,
    part,
    proto_mate,
    grad_mate,
    xbuf,
    ubuf,
    xslots,
    uslots,
    xsum,
    xuslots,
    uxsrc,
    uxslots,
    vsrc,
    vslots,
    st_src,
    st_near,
    st_part,
    st_far,
    st_tot,
    st_all,
    load,
    first_send,
    first_recv,
    gat_send,
    gat_recv,
    swap_send,
    swap_recv,
    near_send,
    near_recv,
    far_send,
    far_recv,
    mate_send,
    mate_recv,
    grad_recv,
    big_send,
    big_recv,
    end_send,
    end_recv,
    st_send,
    st_recv,
):
    x, y, z, c = (lax.axis_index(a) for a in AXES)
    u = z + c * (y - z)
    v = y + c * (z - y)
    oc = 1 - c

    def device(px, pu, pv):
        return (px, pv + c * (pu - pv), pu + c * (pv - pu), c)

    mate = (x, y, z, oc)

    def turned(at, k, n):
        return lax.rem(at + (n // 2 + (1 - 2 * (k % 2)) * ((k + 1) // 2)), n)

    def near_peer(k):
        return (x, y, turned(z, k // CORES, NU), lax.rem(c + (1 + k % CORES), CORES))

    def far_peer(k):
        return (turned(x, k % NX, NX), turned(y, k // NX, NU), z, c)

    def wait(ref, sem):
        pltpu.make_async_copy(ref, ref, sem).wait()

    def push(src, dst, send, recv, target):
        pltpu.make_async_remote_copy(
            src_ref=src, dst_ref=dst, send_sem=send, recv_sem=recv, device_id=target, device_id_type=MESH
        ).start()

    inputs = [
        pltpu.make_async_copy(src, dst, load.at[i])
        for i, (src, dst) in enumerate(
            ((student_hbm, student_ref), (teacher_hbm, teacher_ref), (proto_hbm, proto_ref))
        )
    ]
    for copy in inputs:
        copy.start()

    barrier = pltpu.get_barrier_semaphore()

    def greet(target):
        pl.semaphore_signal(barrier, inc=1, device_id=target, device_id_type=MESH)

    each(NX * NU - 1, lambda k: greet(far_peer(k)))
    each(NU * CORES - 1, lambda k: greet(near_peer(k)))

    for copy in inputs[:2]:
        copy.wait()
    wide_s = student_ref[...].astype(f32)
    wide_t = teacher_ref[...].astype(f32)
    s_inv = inverse_norm(wide_s)
    s_unit = wide_s * s_inv
    t_unit = wide_t * inverse_norm(wide_t)
    first[v, 0:OWN, :] = s_unit
    first[v, OWN : 2 * OWN, :] = t_unit

    def norm_block(i, _):
        at = pl.ds(pl.multiple_of(i * BLOCK, BLOCK), BLOCK)
        wide = proto_ref[at, :].astype(f32)
        inv = inverse_norm(wide)
        proto_inv[at, :] = jnp.broadcast_to(inv, (BLOCK, LANES))
        proto_hat[at, :] = (wide * inv).astype(bf16)
        return 0

    pl.semaphore_wait(barrier, NU * CORES - 1 + NX * NU - 1)

    def send_first(k):
        push(first.at[v], first.at[v], first_send, first_recv, device(x, u, turned(v, k, NU)))

    each(NU - 1, send_first)
    inputs[2].wait()
    lax.fori_loop(0, PROTOS // BLOCK, norm_block, 0)
    wait(first.at[pl.ds(0, NU - 1)], first_recv)
    for i in range(NU):
        stage[0, OWN * i : OWN * (i + 1), :] = first[i, 0:OWN, :]
        stage[1, OWN * i : OWN * (i + 1), :] = first[i, OWN : 2 * OWN, :]
    for h in range(2):
        at = slice(h * CUT, (h + 1) * CUT)
        gat_s[h, c, x, u] = stage[0, :, at].astype(bf16)
        gat_t[h, c, x, u] = stage[1, :, at].astype(bf16)

    def open_step(buf, n):
        def send_hi(k):
            block = buf.at[1, c, x, u]
            push(block, block, gat_send.at[n, 1], gat_recv.at[n, 1], device(turned(x, k, NX), u, v))

        def send_lo(k):
            block = buf.at[0, c, x, u]
            push(block, block, gat_send.at[n, 0], gat_recv.at[n, 0], device(x, turned(u, k, NU), v))

        each(NX - 1, send_hi)
        each(NU - 1, send_lo)

    def spread_hi(buf, n):
        def send(k):
            block = buf.at[1, c, :, u]
            push(block, block, gat_send.at[n, 2], gat_recv.at[n, 2], device(x, turned(u, k, NU), v))

        each(NU - 1, send)

    def spread_lo(buf, n):
        def send(k):
            block = buf.at[0, c, x]
            push(block, block, gat_send.at[n, 3], gat_recv.at[n, 3 + x], device(turned(x, k, NX), u, v))

        each(NX - 1, send)

    def opened_hi(buf, n):
        wait(buf.at[0, 0, 0, pl.ds(0, NX - 1)], gat_recv.at[n, 1])

    def opened_lo(buf, n):
        wait(buf.at[0, 0, 0, pl.ds(0, NU - 1)], gat_recv.at[n, 0])

    def relay(buf, n):
        for k in range(NX):
            px = turned(x, NX - 1 if k == 0 else k - 1, NX)
            if k > 0:
                wait(buf.at[0, 0, 0], gat_recv.at[n, 3 + px])
            push(buf.at[0, c, px], buf.at[0, c, px], swap_send.at[n], swap_recv.at[n], mate)
        wait(buf.at[0, 0, :, pl.ds(0, NU - 1)], gat_recv.at[n, 2])
        push(buf.at[1, c], buf.at[1, c], swap_send.at[n], swap_recv.at[n], mate)

    def settle(buf, n):
        wait(buf.at[:, 0], swap_recv.at[n])
        wait(buf.at[0, 0, 0, pl.ds(0, NU - 1)], gat_send.at[n, 0])
        wait(buf.at[0, 0, 0, pl.ds(0, NX - 1)], gat_send.at[n, 1])
        wait(buf.at[0, 0, :, pl.ds(0, NU - 1)], gat_send.at[n, 2])
        wait(buf.at[0, 0, pl.ds(0, NX - 1)], gat_send.at[n, 3])
        wait(buf.at[:, 0], swap_send.at[n])

    open_step(gat_t, 1)
    wait(first.at[pl.ds(0, NU - 1)], first_send)
    opened_hi(gat_t, 1)
    spread_hi(gat_t, 1)
    opened_lo(gat_t, 1)
    spread_lo(gat_t, 1)
    open_step(gat_s, 0)
    relay(gat_t, 1)

    def exponentials(buf, out, temp, core):
        for k in range(HALF // 256):
            at = pl.ds(pl.multiple_of(core * HALF + k * 256, 256), 256)
            px = k * 256 // SLAB
            product = sum(
                lax.dot_general(
                    proto_hat[:, h * CUT : (h + 1) * CUT],
                    buf[h, core, px : px + 256 // SLAB].reshape(256, CUT),
                    (((1,), (1,)), ((), ())),
                    preferred_element_type=f32,
                )
                for h in range(2)
            )
            out[:, at] = jnp.exp(product * (1.0 / temp))

    def folded(value):
        return jnp.sum(value.reshape(-1, 8, ROWS), axis=0)

    def flat(ref):
        return jnp.concatenate([ref[k : k + 1, :] for k in range(TALL)], axis=1)

    def put(dst, acc):
        for k in range(TALL):
            dst[k : k + 1, :] = jnp.sum(acc[:, k * LANES : (k + 1) * LANES], axis=0, keepdims=True)

    def sweep(scale):
        def body(i, acc):
            at = pl.ds(pl.multiple_of(i * SWEEP, SWEEP), SWEEP)
            e = e_t[at, :]
            weighed = e if scale is None else e * scale
            col = 1.0 / jnp.sum(weighed, axis=1, keepdims=True)
            cols[at, :] = jnp.broadcast_to(col, (SWEEP, LANES))
            return acc + folded(e * col)

        return lax.fori_loop(0, PROTOS // SWEEP, body, jnp.zeros((8, ROWS), f32), unroll=True)

    def near_start(n):
        me = z * CORES + c

        def send(k):
            push(near_src.at[n], near.at[n, me], near_send.at[n], near_recv.at[n], near_peer(k))

        each(NU * CORES - 1, send)
        near[n, me] = near_src[n]

    def near_end(n):
        for sem in (near_recv, near_send):
            wait(near.at[n, pl.ds(0, NU * CORES - 1)], sem.at[n])
        far_src[n] = jnp.sum(near[n], axis=0)

    def far_start(n):
        me = x * NU + y

        def send(k):
            push(far_src.at[n], far.at[n, me], far_send.at[n], far_recv.at[n], far_peer(k))

        each(NX * NU - 1, send)
        far[n, me] = far_src[n]

    def far_end(n):
        for sem in (far_recv, far_send):
            wait(far.at[n, pl.ds(0, NX * NU - 1)], sem.at[n])
        return 1.0 / jnp.sum(far[n], axis=0)

    def row_of(inverse):
        part[...] = inverse
        return flat(part)

    def student_sum(i, acc):
        at = pl.ds(pl.multiple_of(i * BLOCK, BLOCK), BLOCK)
        return acc + folded(e_s[at, :])

    exponentials(gat_t, e_t, teacher_temp, c)
    settle(gat_t, 1)
    exponentials(gat_t, e_t, teacher_temp, oc)
    put(near_src.at[0], sweep(None))
    near_start(0)
    push(proto_hat, proto_mate, mate_send.at[0], mate_recv, mate)
    opened_hi(gat_s, 0)
    opened_lo(gat_s, 0)
    spread_lo(gat_s, 0)
    pl.when(c == 1)(lambda: spread_hi(gat_s, 0))
    near_end(0)
    far_start(0)
    pl.when(c == 0)(lambda: spread_hi(gat_s, 0))
    row_scale = row_of(far_end(0))

    put(near_src.at[1], sweep(row_scale))
    near_start(1)
    relay(gat_s, 0)
    near_end(1)
    far_start(1)
    settle(gat_s, 0)
    for core in range(CORES):
        exponentials(gat_s, e_s, student_temp, core)
    student_part = lax.fori_loop(0, PROTOS // BLOCK, student_sum, jnp.zeros((8, ROWS), f32))
    for k in range(TALL):
        st_src[k] = jnp.sum(student_part[:, k * LANES : (k + 1) * LANES], axis=0, keepdims=True)

    def send_piece(k):
        pz = turned(z, k, NU)
        push(st_src.at[pz], st_near.at[z], st_send.at[0], st_recv.at[0], (x, y, pz, c))

    def send_sum(k):
        push(st_part, st_far.at[x * NU + y], st_send.at[1], st_recv.at[1], far_peer(k))

    def send_back(k):
        push(st_tot, st_all.at[z * CORES + c], st_send.at[2], st_recv.at[2], near_peer(k))

    each(NU - 1, send_piece)
    st_near[z] = st_src[z]
    for sem in (st_recv, st_send):
        wait(st_near.at[pl.ds(0, NU - 1)], sem.at[0])
    st_part[...] = jnp.sum(st_near[...], axis=0)
    each(NX * NU - 1, send_sum)
    st_far[x * NU + y] = st_part[...]
    row_scale = row_of(far_end(1))

    put(near_src.at[2], sweep(row_scale))
    near_start(2)
    near_end(2)
    far_start(2)
    for sem in (st_recv, st_send):
        wait(st_far.at[pl.ds(0, NX * NU - 1)], sem.at[1])
    st_tot[...] = jnp.sum(st_far[...], axis=0)
    each(NU * CORES - 1, send_back)
    st_all[z * CORES + c] = st_tot[...]
    for sem in (st_recv, st_send):
        wait(st_all.at[pl.ds(0, NU * CORES - 1)], sem.at[2])
    totals = [st_all[CORES * k] + st_all[CORES * k + 1] for k in range(TALL)]
    student_scale = (1.0 / jnp.concatenate(totals, axis=1)) * (1.0 / student_temp)

    def scale_block(i, _):
        at = pl.ds(pl.multiple_of(i * BLOCK, BLOCK), BLOCK)
        e_s[at, :] = e_s[at, :] * student_scale
        e_t[at, :] = e_t[at, :] * cols[at, 0:1]
        return 0

    lax.fori_loop(0, PROTOS // BLOCK, scale_block, 0)
    part[...] = far_end(2) * (1.0 / student_temp)

    def gradients(core, px):
        lanes = pl.ds(pl.multiple_of(core * HALF + px * SLAB, SLAB), SLAB)
        scale = part[pl.ds(core * NX + px, 1), :]
        grad[core, px] = (e_s[:, lanes] - e_t[:, lanes] * scale).astype(bf16)

    def row_product(left, right):
        return lax.dot_general(left[...], right[...], (((0,), (0,)), ((), ())), preferred_element_type=f32)

    for k in range(NX):
        px = turned(x, k, NX)
        gradients(oc, px)
        push(grad.at[oc, px], grad_mate.at[px], mate_send.at[1], grad_recv.at[px], mate)
    wait(proto_mate, mate_recv)
    for k in range(NX):
        px = turned(x, k, NX)
        gradients(c, px)
        own = row_product(grad.at[c, px], proto_hat)
        wait(grad_mate.at[px], grad_recv.at[px])
        total = own + row_product(grad_mate.at[px], proto_mate)
        xbuf[px] = total[:, :CUT]
        ubuf[px] = total[:, CUT:].reshape(NU, TILE, D - CUT)
        if k < NX - 1:
            push(xbuf.at[px], xslots.at[x], big_send.at[0], big_recv.at[0], device(px, u, v))

    def send_u(k):
        pu = turned(u, k, NU)
        push(ubuf.at[:, pu], uslots.at[u], big_send.at[1], big_recv.at[1], device(x, pu, v))

    each(NU - 1, send_u)
    xslots[x] = xbuf[x]
    uslots[u] = ubuf[:, u]

    def proto_block(i):
        at = slice(i * 256, (i + 1) * 256)
        halves = [0.0, 0.0]
        for core in range(CORES):
            for px in range(0, NX, 2):
                left = jnp.concatenate([grad[core, px, at, :], grad[core, px + 1, at, :]], axis=1)
                for h in range(2):
                    right = gat_s[h, core, px : px + 2].reshape(2 * SLAB, CUT)
                    halves[h] += jnp.dot(left, right, preferred_element_type=f32)
        step = jnp.concatenate(halves, axis=1)
        inv = proto_inv[at, 0:1]
        unit = proto_ref[at, :].astype(f32) * inv
        pgrad_ref[at, :] = (step - unit * jnp.sum(unit * step, axis=1, keepdims=True)) * inv

    for i in range(PROTOS // 256):
        proto_block(i)

    for sem in (big_recv, big_send):
        wait(xslots.at[pl.ds(0, NX - 1)], sem.at[0])
    xsum[...] = jnp.sum(xslots[...], axis=0)

    def send_xu(k):
        pu = turned(u, k, NU)
        src = xsum.at[pl.ds(pl.multiple_of(pu * TILE, TILE), TILE)]
        push(src, xuslots.at[u], end_send.at[0], end_recv.at[0], device(x, pu, v))

    each(NU - 1, send_xu)
    xuslots[u] = xsum[pl.ds(pl.multiple_of(u * TILE, TILE), TILE), :]

    for sem in (big_recv, big_send):
        wait(uslots.at[pl.ds(0, NU - 1)], sem.at[1])
    uxsrc[...] = jnp.sum(uslots[...], axis=0)

    def send_ux(k):
        px = turned(x, k, NX)
        push(uxsrc.at[px], uxslots.at[x], end_send.at[1], end_recv.at[1], device(px, u, v))

    each(NX - 1, send_ux)
    uxslots[x] = uxsrc[x]

    for sem in (end_recv, end_send):
        wait(xuslots.at[pl.ds(0, NU - 1)], sem.at[0])
    left = jnp.sum(xuslots[...], axis=0)
    for sem in (end_recv, end_send):
        wait(uxslots.at[pl.ds(0, NX - 1)], sem.at[1])
    right = jnp.sum(uxslots[...], axis=0)
    for pv in range(NU):
        at = slice(pv * OWN, (pv + 1) * OWN)
        vsrc[pv, :, :CUT] = left[at, :]
        vsrc[pv, :, CUT:] = right[at, :]

    def send_v(k):
        pv = turned(v, k, NU)
        push(vsrc.at[pv], vslots.at[v], end_send.at[2], end_recv.at[2], device(x, u, pv))

    each(NU - 1, send_v)
    vslots[v] = vsrc[v]
    for sem in (end_recv, end_send):
        wait(vslots.at[pl.ds(0, NU - 1)], sem.at[2])
    step = jnp.sum(vslots[...], axis=0)
    wait(proto_mate, mate_send.at[0])
    wait(grad_mate, mate_send.at[1])

    sgrad_ref[...] = (step - s_unit * jnp.sum(s_unit * step, axis=1, keepdims=True)) * s_inv


def on_device(student, teacher, protos):
    vmem = pl.BlockSpec(memory_space=pltpu.VMEM)
    dma = pltpu.SemaphoreType.DMA
    return pl.pallas_call(
        kernel,
        out_shape=(
            jax.ShapeDtypeStruct((OWN, D), f32),
            jax.ShapeDtypeStruct((PROTOS, D), f32),
        ),
        in_specs=[pl.BlockSpec(memory_space=pltpu.HBM)] * 3,
        out_specs=(vmem, vmem),
        scratch_shapes=[
            pltpu.VMEM((OWN, D), bf16),
            pltpu.VMEM((OWN, D), bf16),
            pltpu.VMEM((PROTOS, D), bf16),
            pltpu.VMEM((NU, 2 * OWN, D), f32),
            pltpu.VMEM((2, TILE, D), f32),
            pltpu.VMEM((2, CORES, NX, NU, TILE, CUT), bf16),
            pltpu.VMEM((2, CORES, NX, NU, TILE, CUT), bf16),
            pltpu.VMEM((PROTOS, D), bf16),
            pltpu.VMEM((PROTOS, LANES), f32),
            pltpu.VMEM((PROTOS, ROWS), f32),
            pltpu.VMEM((PROTOS, ROWS), f32),
            pltpu.VMEM((PROTOS, LANES), f32),
            pltpu.VMEM((CORES, NX, PROTOS, SLAB), bf16),
            pltpu.VMEM((SUMS, TALL, LANES), f32),
            pltpu.VMEM((SUMS, NU * CORES, TALL, LANES), f32),
            pltpu.VMEM((SUMS, TALL, LANES), f32),
            pltpu.VMEM((SUMS, NX * NU, TALL, LANES), f32),
            pltpu.VMEM((TALL, LANES), f32),
            pltpu.VMEM((PROTOS, D), bf16),
            pltpu.VMEM((NX, PROTOS, SLAB), bf16),
            pltpu.VMEM((NX, SLAB, CUT), f32),
            pltpu.VMEM((NX, NU, TILE, D - CUT), f32),
            pltpu.VMEM((NX, SLAB, CUT), f32),
            pltpu.VMEM((NU, NX, TILE, D - CUT), f32),
            pltpu.VMEM((SLAB, CUT), f32),
            pltpu.VMEM((NU, TILE, CUT), f32),
            pltpu.VMEM((NX, TILE, D - CUT), f32),
            pltpu.VMEM((NX, TILE, D - CUT), f32),
            pltpu.VMEM((NU, OWN, D), f32),
            pltpu.VMEM((NU, OWN, D), f32),
            pltpu.VMEM((TALL, 1, LANES), f32),
            pltpu.VMEM((NU, 1, LANES), f32),
            pltpu.VMEM((1, LANES), f32),
            pltpu.VMEM((NX * NU, 1, LANES), f32),
            pltpu.VMEM((1, LANES), f32),
            pltpu.VMEM((NU * CORES, 1, LANES), f32),
            dma((3,)),
            dma,
            dma,
            dma((2, 4)),
            dma((2, 3 + NX)),
            dma((2,)),
            dma((2,)),
            dma((SUMS,)),
            dma((SUMS,)),
            dma((SUMS,)),
            dma((SUMS,)),
            dma((2,)),
            dma,
            dma((NX,)),
            dma((2,)),
            dma((2,)),
            dma((3,)),
            dma((3,)),
            dma((3,)),
            dma((3,)),
        ],
        compiler_params=pltpu.CompilerParams(
            collective_id=0, has_side_effects=True, vmem_limit_bytes=48 << 20
        ),
        name="prototype_head",
    )(*(pltpu.with_memory_space_constraint(a, pltpu.HBM) for a in (student, teacher, protos)))


def solution(mesh):
    torus = Mesh(mesh.devices.reshape(NX, NU, NU, CORES), AXES)
    return jax.shard_map(
        on_device,
        mesh=torus,
        in_specs=(P(AXES, None),) * 3,
        out_specs=(P(AXES, None), P(AXES, None)),
        check_vma=False,
    )
```
